256 devices in a mesh: seq: 64 (over x, z, core), head: 4 (over y).
Axes of the slice: x: 4, y: 4, z: 8, core: 2. Of those that a mesh axis runs over, the one named last changes fastest.
Arguments:
- queries: bfloat16 [8192, 2048], P('seq', 'head'), may hold values from -6 to 6
- keys: bfloat16 [8192, 2048], P('seq', 'head'), may hold values from -6 to 6
- values: bfloat16 [8192, 2048], P('seq', 'head'), may hold values from -6 to 6
- gate_log: float32 [8192, 16], P('seq', 'head'), may hold values from -1 to 0
- beta: float32 [8192, 16], P('seq', 'head'), may hold values from 0.0002 to 1
- stream: bfloat16 [8192, 2048], P('seq'), may hold values from -6 to 6
- w_out: bfloat16 [2048, 2048], P('head'), may hold values from -0.125 to 0.125
- w_qkv: bfloat16 [2048, 6144], P(None, 'head'), may hold values from -0.125 to 0.125
Outputs:
- hidden: bfloat16 [8192, 2048], P('seq', 'head')
- attended: bfloat16 [8192, 2048], P('seq', 'head')
The draws below stay inside these ranges and needn't reach their ends.
All inputs are finite; a program needn't handle non-finite values.
Results may differ from the reference program's by a relative error of at most 0.015.
Values may be sent and summed in bfloat16 or wider, within the bound.
No kernel may reach another device: no remote copies, remote signals or barrier semaphores. Data moves between devices by JAX's collectives and lax.ppermute only.
A program may use at most 128 MiB of HBM per device.

```python
import math
import jax
import jax.numpy as jnp
from jax import lax

HEADS = 16
DK = 128
D = 2048
TOK_DEV = 128
WINDOW = 1024
STRETCH = 64
TEXT_LENGTH = 8192


def head_slow(key):
    pick = jax.random.uniform(jax.random.fold_in(key, 11), (HEADS,))
    share = 0.5
    return pick < share


def draw_gate_log(key, part):
    slow = head_slow(key)
    concurrent_lanes = jax.random.split(jax.random.fold_in(key, 3), 6)
    fast_rate = jnp.exp(jax.random.uniform(concurrent_lanes[0], (HEADS,), minval=math.log(1.0 / 2048.0), maxval=math.log(1.0 / 30.0)))
    slow_rate = jnp.exp(jax.random.uniform(concurrent_lanes[1], (HEADS,), minval=math.log(0.05), maxval=math.log(0.3))) / TEXT_LENGTH
    fading_factor = jnp.where(slow, slow_rate, fast_rate)
    chips_factor_count = jnp.exp(jax.random.uniform(concurrent_lanes[2], (TEXT_LENGTH // TOK_DEV, HEADS), minval=math.log(0.5), maxval=math.log(2.0)))
    chips_factor_count = jnp.repeat(chips_factor_count, TOK_DEV, axis=0)
    word_scaling_factor = jax.random.uniform(concurrent_lanes[3], (TEXT_LENGTH, HEADS), minval=0.5, maxval=1.5)
    block_index_within = jax.random.randint(concurrent_lanes[4], (3,), 0, TEXT_LENGTH)
    kept_after_block = jax.random.uniform(concurrent_lanes[5], (3,), minval=0.6, maxval=0.8)
    masked_cells = jnp.arange(TEXT_LENGTH)[:, None] == block_index_within[None, :]
    word_group_length = jnp.sum(jnp.where(masked_cells, jnp.log(kept_after_block)[None, :], 0.0), axis=1)
    return (-fading_factor[None, :] * chips_factor_count * word_scaling_factor + word_group_length[:, None]).astype(jnp.float32)


def draw_beta(key, part):
    slow = head_slow(key)
    concurrent_lanes = jax.random.split(jax.random.fold_in(key, 5), 2)
    small = jnp.exp(jax.random.uniform(concurrent_lanes[0], (TEXT_LENGTH, HEADS), minval=math.log(0.0002), maxval=math.log(0.001)))
    strong = jax.random.uniform(concurrent_lanes[1], (TEXT_LENGTH, HEADS), minval=0.2, maxval=1.0)
    return jnp.where(slow[None, :], small, strong).astype(jnp.float32)


def steps_of(own_key, extent, cuts, smallest, top_value):
    def one(dim, shards_of):
        heights = jax.random.uniform(jax.random.fold_in(jax.random.fold_in(own_key, 6), dim), (shards_of,), jnp.float32, smallest / len(cuts), top_value / len(cuts))
        return jnp.repeat(jnp.exp(heights), extent[dim] // shards_of).reshape((-1,) + (1,) * (len(extent) - dim - 1))

    level = one(*cuts[0])
    for cut in cuts[1:]:
        level = level * one(*cut)
    return level


def bell_draw(stream_key, shape, deviation, most, pieces=(), kind=jnp.bfloat16):
    entries = deviation * jax.random.normal(stream_key, shape, jnp.float32)
    if pieces:
        entries = entries * steps_of(stream_key, shape, pieces, -0.22, 0.18)
    return jnp.clip(entries, -most, most).astype(kind)


def setup_inputs(seed: int = 0) -> dict:
    key_of = jax.random.split(jax.random.key(seed), 9)
    return {
        "queries": bell_draw(key_of[0], (TEXT_LENGTH, D), 1.0, 6.0, ((0, 64), (1, 4))),
        "keys": bell_draw(key_of[1], (TEXT_LENGTH, D), 1.0, 6.0, ((0, 64), (1, 4))),
        "values": bell_draw(key_of[2], (TEXT_LENGTH, D), 1.0, 6.0, ((0, 64), (1, 4))),
        "gate_log": draw_gate_log(jax.random.fold_in(key_of[8], 71), 0),
        "beta": draw_beta(jax.random.fold_in(key_of[8], 71), 0),
        "stream": bell_draw(key_of[5], (TEXT_LENGTH, D), 1.0, 6.0, ((0, 64),)),
        "w_out": bell_draw(key_of[6], (D, D), D ** -0.5, 0.125, ((0, 4),)),
        "w_qkv": bell_draw(key_of[7], (D, 3 * D), D ** -0.5, 0.125, ((1, 4),)),
    }


score_scale = 10.0

def product(left, right):
    return jnp.einsum('hij,hjk->hik', left, right, precision=lax.Precision.HIGHEST)

def to_unit(vectors):
    return vectors * lax.rsqrt(lax.optimization_barrier(jnp.sum(vectors * vectors, axis=-1, keepdims=True)) + 1e-06)

def lower_inverse(coupling):
    identity = jnp.eye(coupling.shape[-1], dtype=jnp.float32)
    result = identity - coupling
    power = coupling
    span = 2
    while span < coupling.shape[-1]:
        power = product(power, power)
        result = product(result, identity + power)
        span = span * 2
    return result

def stretch_parts(query_rows, key_rows, value_rows, gate_rows, beta_rows):
    length = gate_rows.shape[-1]
    cumulative = jnp.cumsum(gate_rows, axis=-1)
    later = lax.broadcasted_iota(jnp.int32, (length, length), 0)
    sooner = lax.broadcasted_iota(jnp.int32, (length, length), 1)
    causal = later >= sooner
    strict = later > sooner
    spread = cumulative[:, :, None] - cumulative[:, None, :]
    decay = jnp.where(causal, jnp.exp(jnp.where(causal, spread, 0.0)), 0.0)
    key_intersection = jnp.einsum('hcd,hed->hce', key_rows, key_rows, precision=lax.Precision.HIGHEST)
    coupling = jnp.where(strict, beta_rows[:, :, None] * decay * key_intersection, 0.0)
    inverse = lower_inverse(coupling)
    writes = product(inverse, beta_rows[:, :, None] * value_rows)
    erasers = product(inverse, (beta_rows * jnp.exp(cumulative))[:, :, None] * key_rows)
    key_end = jnp.swapaxes(jnp.exp(cumulative[:, -1:] - cumulative)[:, :, None] * key_rows, 1, 2)
    identity = jnp.eye(key_rows.shape[-1], dtype=jnp.float32)
    transition = jnp.exp(cumulative[:, -1])[:, None, None] * identity - product(key_end, erasers)
    offset = product(key_end, writes)
    intersection = jnp.einsum('hcd,hed->hce', query_rows, key_rows, precision=lax.Precision.HIGHEST)
    mixing = jnp.where(causal, intersection * decay, 0.0)
    query_decayed = jnp.exp(cumulative)[:, :, None] * query_rows
    return (query_decayed, mixing, writes, erasers, transition, offset)

def attend_block(query_block, key_block, value_block, query_start, key_start):
    scores = score_scale * jnp.einsum('qhd,khd->hqk', query_block.astype(jnp.float32), key_block.astype(jnp.float32))
    query_place = query_start + jnp.arange(query_block.shape[0], dtype=jnp.int32)[:, None]
    key_place = key_start + jnp.arange(key_block.shape[0], dtype=jnp.int32)[None, :]
    allowed = (key_place <= query_place) & (key_place > query_place - WINDOW) & (key_place >= 0)
    expo = jnp.where(allowed[None], jnp.exp(scores), 0.0)
    totals = lax.optimization_barrier(jnp.sum(expo, axis=-1))
    rounded = lax.optimization_barrier(expo.astype(jnp.bfloat16))
    mixed = jnp.einsum('hqk,khd->qhd', rounded.astype(jnp.float32), value_block.astype(jnp.float32))
    return (mixed / jnp.transpose(totals)[:, :, None]).astype(jnp.bfloat16)

def reference(queries, keys, values, gate_log, beta, stream, w_out, w_qkv):
    blocks = TEXT_LENGTH // STRETCH

    def arrange(matrix):
        return matrix.astype(jnp.float32).reshape(blocks, STRETCH, HEADS, DK).transpose(0, 2, 1, 3)
    query_blocks = to_unit(arrange(queries))
    key_blocks = to_unit(arrange(keys))
    value_blocks = arrange(values)
    gate_blocks = gate_log.reshape(blocks, STRETCH, HEADS).transpose(0, 2, 1)
    beta_blocks = beta.reshape(blocks, STRETCH, HEADS).transpose(0, 2, 1)

    def advance(state, inputs):
        query_decayed, mixing, writes, erasers, transition, offset = stretch_parts(*inputs)
        local = product(query_decayed, state) + product(mixing, writes - product(erasers, state))
        return (product(transition, state) + offset, local)
    start = jnp.zeros((HEADS, DK, DK), jnp.float32)
    last_state, outputs = lax.scan(advance, start, (query_blocks, key_blocks, value_blocks, gate_blocks, beta_blocks))
    delta_out = outputs.transpose(0, 2, 1, 3).reshape(TEXT_LENGTH, HEADS, DK)
    head_normed = (delta_out * lax.rsqrt(lax.optimization_barrier(jnp.mean(delta_out * delta_out, axis=-1, keepdims=True)) + 1e-05)).astype(jnp.bfloat16).reshape(TEXT_LENGTH, D)
    hidden = (stream.astype(jnp.float32) + jnp.dot(head_normed, w_out, preferred_element_type=jnp.float32)).astype(jnp.bfloat16)
    hidden_float = hidden.astype(jnp.float32)
    normed = (hidden_float * lax.rsqrt(lax.optimization_barrier(jnp.mean(hidden_float * hidden_float, axis=-1, keepdims=True)) + 1e-05)).astype(jnp.bfloat16)
    projected = jnp.dot(normed, w_qkv, preferred_element_type=jnp.float32).reshape(TEXT_LENGTH, HEADS, 3, DK)
    unit_queries = to_unit(projected[:, :, 0]).astype(jnp.bfloat16)
    unit_keys = to_unit(projected[:, :, 1]).astype(jnp.bfloat16)
    head_values = projected[:, :, 2].astype(jnp.bfloat16)
    block = math.gcd(TEXT_LENGTH, 512)
    padding = jnp.zeros((WINDOW, HEADS, DK), jnp.bfloat16)
    keys_padded = jnp.concatenate([padding, unit_keys], axis=0)
    values_padded = jnp.concatenate([padding, head_values], axis=0)

    def one_block(number):
        begin = number * block
        query_block = lax.dynamic_slice_in_dim(unit_queries, begin, block, 0)
        key_block = lax.dynamic_slice_in_dim(keys_padded, begin, WINDOW + block, 0)
        value_block = lax.dynamic_slice_in_dim(values_padded, begin, WINDOW + block, 0)
        return attend_block(query_block, key_block, value_block, begin, begin - WINDOW)
    attended = lax.map(one_block, jnp.arange(TEXT_LENGTH // block, dtype=jnp.int32)).reshape(TEXT_LENGTH, D)
    return (hidden, attended)
```

```python
import functools

import jax
import jax.numpy as jnp
from jax import lax
from jax.experimental import pallas as pl
from jax.experimental.pallas import tpu as pltpu
from jax.sharding import PartitionSpec as P

WINDOW = 1024
WIDTH = 128
SCORE_SCALE = 10.0
F32 = jnp.float32
BF16 = jnp.bfloat16
HIGHEST = lax.Precision.HIGHEST
VMEM = pltpu.VMEM
SMEM = pltpu.SMEM
LIMIT = 40 * 1024 * 1024


def dot(left, right, contract=(1, 0), precision=None):
    return lax.dot_general(
        left,
        right,
        (((contract[0],), (contract[1],)), ((), ())),
        precision=precision,
        preferred_element_type=F32,
    )


def exact(left, right, contract=(1, 0)):
    return dot(left, right, contract, HIGHEST)


def iotas(rows, columns):
    return (
        lax.broadcasted_iota(jnp.int32, (rows, columns), 0),
        lax.broadcasted_iota(jnp.int32, (rows, columns), 1),
    )


def split_diagonal(matrix):
    row, column = iotas(WIDTH, WIDTH)
    high = matrix.astype(BF16)
    return high, jnp.where(row == column, matrix - high.astype(F32), 0.0)


def compose(left_t, left_o, right_t, right_o):
    left_high, left_rest = split_diagonal(left_t)
    right_high, right_rest = split_diagonal(right_t)
    left_column = jnp.sum(left_rest, axis=1, keepdims=True)
    right_row = jnp.sum(right_rest, axis=0, keepdims=True)
    offset = dot(left_high, right_o.astype(BF16)) + left_column * right_o + left_o
    product = dot(left_high, right_high) + left_column * right_t + left_high.astype(F32) * right_row
    return product, offset


def apply(left_t, left_o, state):
    left_high, left_rest = split_diagonal(left_t)
    left_column = jnp.sum(left_rest, axis=1, keepdims=True)
    return dot(left_high, state.astype(BF16)) + left_column * state + left_o


def store_payload(ref, pairs):
    row, _ = iotas(16, WIDTH)
    for n, (transition, offset) in enumerate(pairs):
        high, rest = split_diagonal(transition)
        ref[n * WIDTH : (n + 1) * WIDTH, 0:WIDTH] = high
        ref[n * WIDTH : (n + 1) * WIDTH, WIDTH : 2 * WIDTH] = offset.astype(BF16)
        line = jnp.sum(rest, axis=0, keepdims=True)
        ref[2 * WIDTH : 2 * WIDTH + 16, n * WIDTH : (n + 1) * WIDTH] = jnp.where(
            row == 0, line, 0.0
        ).astype(BF16)


def load_payload(ref, n):
    row, column = iotas(WIDTH, WIDTH)
    line = ref[2 * WIDTH : 2 * WIDTH + 16, n * WIDTH : (n + 1) * WIDTH].astype(F32)
    line = jnp.sum(line, axis=0, keepdims=True)
    transition = ref[n * WIDTH : (n + 1) * WIDTH, 0:WIDTH].astype(F32)
    transition = transition + jnp.where(row == column, line, 0.0)
    offset = ref[n * WIDTH : (n + 1) * WIDTH, WIDTH : 2 * WIDTH].astype(F32)
    return transition, offset


def to_unit(vectors):
    return vectors * lax.rsqrt(jnp.sum(vectors * vectors, axis=-1, keepdims=True) + 1e-06)


def lower_inverses(couplings):
    rows = couplings[0].shape[0]
    row, column = iotas(rows, rows)
    identity = (row == column).astype(F32)
    inside = (row >> 4) == (column >> 4)
    powers = [jnp.where(inside, c, 0.0) for c in couplings]
    results = [identity - p for p in powers]
    span = 2
    while span < 16:
        powers = [exact(p, p) for p in powers]
        results = [exact(r, identity + p) for r, p in zip(results, powers)]
        span *= 2
    shift = 4
    while (1 << shift) < rows:
        level = ((row >> (shift + 1)) == (column >> (shift + 1))) & ((row >> shift) > (column >> shift))
        crossing = [exact(r, jnp.where(level, c, 0.0)) for r, c in zip(results, couplings)]
        results = [r - exact(x, r) for r, x in zip(results, crossing)]
        shift += 1
    return results


def chunk_kernel(place, q_ref, k_ref, v_ref, g_ref, b_ref, local_ref, through_ref, own_ref, pay_ref, pairs):
    rows, groups = g_ref.shape
    core = place[1]
    row, column = iotas(rows, rows)
    causal = row >= column
    strict = row > column
    gates = g_ref[...]
    betas = b_ref[...]
    summed = exact(causal.astype(F32), gates)
    summed_row = exact(gates, (row <= column).astype(F32), (0, 0))
    keys, mixings, couplings, decayed = [], [], [], []
    for h in range(groups):
        span = slice(h * WIDTH, (h + 1) * WIDTH)
        key = to_unit(k_ref[:, span].astype(F32))
        query = to_unit(q_ref[:, span].astype(F32))
        along = summed[:, h : h + 1]
        spread = along - summed_row[h : h + 1, :]
        decay = jnp.where(causal, jnp.exp(jnp.where(causal, spread, 0.0)), 0.0)
        both = exact(jnp.concatenate([key, query], axis=0), key, (1, 1))
        couplings.append(jnp.where(strict, betas[:, h : h + 1] * decay * both[:rows], 0.0))
        mixings.append(both[rows:] * decay)
        keys.append(key)
        decayed.append(jnp.exp(along) * query)
    inverses = lower_inverses(couplings)
    for h in range(groups):
        span = slice(h * WIDTH, (h + 1) * WIDTH)
        along = summed[:, h : h + 1]
        last = summed[rows - 1 : rows, h : h + 1]
        beta = betas[:, h : h + 1]
        value = v_ref[:, span].astype(F32)
        made = exact(
            inverses[h],
            jnp.concatenate([beta * value, (beta * jnp.exp(along)) * keys[h]], axis=1),
        )
        ended = jnp.exp(last - along) * keys[h]
        effect = exact(ended, made, (0, 0))
        inner = exact(mixings[h], made)
        local_ref[h] = inner[:, :WIDTH]
        through_ref[h] = (decayed[h] - inner[:, WIDTH:]).astype(BF16)
        identity = iotas(WIDTH, WIDTH)
        kept = jnp.where(identity[0] == identity[1], jnp.exp(last), 0.0)
        pairs[h, :, 0:WIDTH] = kept - effect[:, WIDTH:]
        pairs[h, :, WIDTH:] = effect[:, :WIDTH]
    half = groups // 2
    own_ref[...] = pairs[pl.ds(core * half, half)]
    away = pairs[pl.ds((1 - core) * half, half)]
    store_payload(pay_ref, [(away[n, :, :WIDTH], away[n, :, WIDTH:]) for n in range(half)])


def pair_kernel(place, own_ref, recv_ref, now_ref, pay_ref, first_ref):
    core = place[1]
    pairs = []
    for n in range(own_ref.shape[0]):
        own = own_ref[n]
        other = jnp.concatenate(load_payload(recv_ref, n), axis=1)
        later = jnp.where(core == 1, own, other)
        sooner = jnp.where(core == 1, other, own)
        first_ref[n] = sooner
        pair = compose(later[:, :WIDTH], later[:, WIDTH:], sooner[:, :WIDTH], sooner[:, WIDTH:])
        now_ref[n, :, :WIDTH] = pair[0]
        now_ref[n, :, WIDTH:] = pair[1]
        pairs.append(pair)
    store_payload(pay_ref, pairs)


def step_kernel(now_ref, recv_ref, next_ref, pay_ref):
    pairs = []
    for n in range(now_ref.shape[0]):
        now = now_ref[n]
        pair = compose(now[:, :WIDTH], now[:, WIDTH:], *load_payload(recv_ref, n))
        next_ref[n, :, :WIDTH] = pair[0]
        next_ref[n, :, WIDTH:] = pair[1]
        pairs.append(pair)
    store_payload(pay_ref, pairs)


def far_kernel(now_ref, recv_ref, pay_ref, offset_ref):
    pairs = []
    for n in range(now_ref.shape[0]):
        now = now_ref[n]
        pair = compose(now[:, :WIDTH], now[:, WIDTH:], *load_payload(recv_ref, n))
        offset_ref[n * WIDTH : (n + 1) * WIDTH, :] = pair[1].astype(BF16)
        pairs.append(pair)
    store_payload(pay_ref, pairs)


def state_kernel(place, near_ref, far_ref, first_ref, mine_ref, away_ref):
    core = place[1]
    for n in range(first_ref.shape[0]):
        span = slice(n * WIDTH, (n + 1) * WIDTH)
        near = load_payload(near_ref, n)
        zeroth = apply(near[0], near[1], far_ref[span, :].astype(F32))
        first = first_ref[n]
        oneth = apply(first[:, :WIDTH], first[:, WIDTH:], zeroth)
        mine_ref[span, :] = jnp.where(core == 0, zeroth, oneth).astype(BF16)
        away_ref[span, :] = jnp.where(core == 0, oneth, zeroth).astype(BF16)


def out_kernel(place, local_ref, through_ref, mine_ref, recv_ref, w_ref, term_ref, *sent_refs):
    core = place[1]
    me = place[2]
    groups = local_ref.shape[0]
    half = groups // 2
    normed = []
    for h in range(groups):
        span = slice((h % half) * WIDTH, (h % half + 1) * WIDTH)
        state = jnp.where(core == h // half, mine_ref[span, :], recv_ref[span, :])
        result = local_ref[h] + dot(through_ref[h], state)
        normed.append(
            (
                result * lax.rsqrt(jnp.mean(result * result, axis=-1, keepdims=True) + 1e-05)
            ).astype(BF16)
        )
    normed = jnp.concatenate(normed, axis=1)
    width = term_ref.shape[1]
    count = len(sent_refs) + 1
    for r in range(count):
        begin = pl.multiple_of(lax.rem(me + r, count) * width, width)
        term = dot(normed, w_ref[:, pl.ds(begin, width)])
        if r == 0:
            term_ref[...] = term
        else:
            sent_refs[r - 1][...] = term.astype(BF16)


def hidden_kernel(place, stream_ref, term_ref, *refs):
    me = place[2]
    width = term_ref.shape[1]
    begin = pl.multiple_of(me * width, width)
    total = term_ref[...]
    for ref in refs[:-1]:
        total = total + ref[...].astype(F32)
    refs[-1][...] = (stream_ref[:, pl.ds(begin, width)].astype(F32) + total).astype(BF16)


def project_kernel(place, w_ref, *refs):
    me = place[2]
    blocks, (q_ref, kv_ref) = refs[:-2], refs[-2:]
    count = len(blocks)
    rows, width = blocks[0].shape
    values = [ref[...].astype(F32) for ref in blocks]
    squares = sum(jnp.sum(v * v, axis=-1, keepdims=True) for v in values)
    scale = lax.rsqrt(squares / (count * width) + 1e-05)
    total = None
    for r in range(count):
        begin = pl.multiple_of(lax.rem(me + count - r, count) * width, width)
        part = dot((values[r] * scale).astype(BF16), w_ref[pl.ds(begin, width), :])
        total = part if total is None else total + part
    groups = q_ref.shape[1] // WIDTH
    for h in range(groups):
        base = h * 3 * WIDTH
        span = slice(h * WIDTH, (h + 1) * WIDTH)
        q_ref[:, span] = to_unit(total[:, base : base + WIDTH]).astype(BF16)
        kv_ref[:, span] = to_unit(total[:, base + WIDTH : base + 2 * WIDTH]).astype(BF16)
        kv_ref[:, groups * WIDTH + h * WIDTH : groups * WIDTH + (h + 1) * WIDTH] = total[
            :, base + 2 * WIDTH : base + 3 * WIDTH
        ].astype(BF16)


def window_kernel(place, q_ref, *refs):
    seq, core = place[0], place[1]
    blocks, out_ref = refs[:-1], refs[-1]
    rows = q_ref.shape[0]
    groups = q_ref.shape[1] // WIDTH
    row, column = iotas(rows, rows)
    query_place = seq * rows + row
    mixed = [None] * groups
    totals = [None] * groups
    for n, ref in enumerate(blocks):
        owner = seq - 2 * (n // 2) if n % 2 == 0 else seq - 2 * (n // 2) + 1 - 2 * core
        key_place = owner * rows + column
        allowed = (key_place <= query_place) & (key_place > query_place - WINDOW) & (key_place >= 0)
        for h in range(groups):
            span = slice(h * WIDTH, (h + 1) * WIDTH)
            scores = SCORE_SCALE * dot(q_ref[:, span], ref[:, span], (1, 1))
            weights = jnp.where(allowed, jnp.exp(scores), 0.0)
            total = jnp.sum(weights, axis=-1, keepdims=True)
            part = dot(
                weights.astype(BF16),
                ref[:, (groups + h) * WIDTH : (groups + h + 1) * WIDTH],
            )
            mixed[h] = part if mixed[h] is None else mixed[h] + part
            totals[h] = total if totals[h] is None else totals[h] + total
    for h in range(groups):
        out_ref[:, h * WIDTH : (h + 1) * WIDTH] = (mixed[h] / totals[h]).astype(BF16)


def call(kernel, outs, smem=0, scratch=()):
    def run(*args):
        return pl.pallas_call(
            kernel,
            out_shape=[jax.ShapeDtypeStruct(shape, kind) for shape, kind in outs],
            in_specs=[pl.BlockSpec(memory_space=SMEM)] * smem
            + [pl.BlockSpec(memory_space=VMEM)] * (len(args) - smem),
            out_specs=[pl.BlockSpec(memory_space=VMEM)] * len(outs),
            scratch_shapes=list(scratch),
            compiler_params=pltpu.CompilerParams(vmem_limit_bytes=LIMIT),
        )(*args)

    return run


def moved(array, axis, distance):
    size = lax.axis_size(axis)
    return lax.ppermute(array, axis, [(i, i + distance) for i in range(size - distance)])


def turned(array, axis, distance):
    size = lax.axis_size(axis)
    return lax.ppermute(array, axis, [(i, (i + distance) % size) for i in range(size)])


def swapped(array):
    return lax.ppermute(array, "seq", [(i, i ^ 1) for i in range(lax.axis_size("seq"))])


def body(queries, keys, values, gate_log, beta, stream, w_out, w_qkv):
    rows, wide = queries.shape
    groups = gate_log.shape[1]
    half = groups // 2
    seq = lax.axis_index("seq")
    head = lax.axis_index("head")
    heads = lax.axis_size("head")
    length = lax.axis_size("seq")
    place = jnp.stack([seq, seq % 2, head]).astype(jnp.int32)
    pair_shape = ((half, WIDTH, 2 * WIDTH), F32)
    pay_shape = ((half * WIDTH + 16, 2 * WIDTH), BF16)
    state_shape = ((half * WIDTH, WIDTH), BF16)

    local, through, own, pay = call(
        chunk_kernel,
        [((groups, rows, WIDTH), F32), ((groups, rows, WIDTH), BF16), pair_shape, pay_shape],
        1,
        [pltpu.VMEM((groups, WIDTH, 2 * WIDTH), F32)],
    )(place, queries, keys, values, gate_log, beta)
    now, pay, first = call(pair_kernel, [pair_shape, pay_shape, pair_shape], 1)(
        place, own, swapped(pay)
    )
    distance = 2
    while distance * 4 < length:
        now, pay = call(step_kernel, [pair_shape, pay_shape])(now, moved(pay, "seq", distance))
        distance *= 2
    pay, offset = call(far_kernel, [pay_shape, state_shape])(now, moved(pay, "seq", distance))
    near = moved(pay, "seq", 2)
    far = moved(offset, "seq", distance * 2 + 2)
    mine, away = call(state_kernel, [state_shape, state_shape], 1)(place, near, far, first)
    terms = call(
        out_kernel,
        [((rows, wide), F32)] + [((rows, wide), BF16)] * (heads - 1),
        1,
    )(place, local, through, mine, swapped(away), w_out)
    received = [turned(terms[r], "head", r) for r in range(1, heads)]
    (hidden,) = call(hidden_kernel, [((rows, wide), BF16)], 1)(place, stream, terms[0], *received)
    others = [turned(hidden, "head", r) for r in range(1, heads)]
    unit_queries, pack = call(
        project_kernel, [((rows, wide), BF16), ((rows, 2 * wide), BF16)], 1
    )(place, w_qkv, hidden, *others)
    blocks = [pack, swapped(pack)]
    moving = pack
    for _ in range(WINDOW // (2 * rows)):
        moving = moved(moving, "seq", 2)
        blocks += [moving, swapped(moving)]
    (attended,) = call(window_kernel, [((rows, wide), BF16)], 1)(place, unit_queries, *blocks)
    return (hidden, attended)


def solution(mesh):
    in_specs = (
        P("seq", "head"),
        P("seq", "head"),
        P("seq", "head"),
        P("seq", "head"),
        P("seq", "head"),
        P("seq", None),
        P("head", None),
        P(None, "head"),
    )
    out_specs = (P("seq", "head"), P("seq", "head"))
    return jax.shard_map(body, mesh=mesh, in_specs=in_specs, out_specs=out_specs, check_vma=False)
```

```python
import functools

import jax
import jax.numpy as jnp
from jax import lax
from jax.experimental import pallas as pl
from jax.experimental.pallas import tpu as pltpu
from jax.sharding import PartitionSpec as P

WINDOW = 1024
WIDTH = 128
SCORE_SCALE = 10.0
F32 = jnp.float32
BF16 = jnp.bfloat16
HIGHEST = lax.Precision.HIGHEST
VMEM = pltpu.VMEM
SMEM = pltpu.SMEM
LIMIT = 16 * 1024 * 1024
CHUNK_LIMIT = 54579 * 1024


def dot(left, right, contract=(1, 0), precision=None):
    return lax.dot_general(
        left,
        right,
        (((contract[0],), (contract[1],)), ((), ())),
        precision=precision,
        preferred_element_type=F32,
    )


def exact(left, right, contract=(1, 0)):
    return dot(left, right, contract, HIGHEST)


def iotas(rows, columns):
    return (
        lax.broadcasted_iota(jnp.int32, (rows, columns), 0),
        lax.broadcasted_iota(jnp.int32, (rows, columns), 1),
    )


def fine(left, right, contract=(1, 0)):
    left_high = left.astype(BF16)
    right_high = right.astype(BF16)
    left_low = (left - left_high.astype(F32)).astype(BF16)
    right_low = (right - right_high.astype(F32)).astype(BF16)
    return (
        dot(left_high, right_high, contract)
        + dot(left_high, right_low, contract)
        + dot(left_low, right_high, contract)
    )


def split_diagonal(matrix):
    row, column = iotas(WIDTH, WIDTH)
    high = matrix.astype(BF16)
    return high, jnp.where(row == column, matrix - high.astype(F32), 0.0)


def compose(left, right):
    left_t, left_o = left
    right_t, right_o = right
    left_high, left_rest = split_diagonal(left_t)
    right_high, right_rest = split_diagonal(right_t)
    left_column = jnp.sum(left_rest, axis=1, keepdims=True)
    right_row = jnp.sum(right_rest, axis=0, keepdims=True)
    offset = dot(left_high, right_o.astype(BF16)) + left_column * right_o + left_o
    product = dot(left_high, right_high) + left_column * right_t + left_high.astype(F32) * right_row
    return product, offset


def apply(left, state):
    left_t, left_o = left
    left_high, left_rest = split_diagonal(left_t)
    left_column = jnp.sum(left_rest, axis=1, keepdims=True)
    return dot(left_high, state.astype(BF16)) + left_column * state + left_o


def store_payload(ref, pair):
    row, _ = iotas(16, 2 * WIDTH)
    transition, offset = pair
    high, rest = split_diagonal(transition)
    ref[0:WIDTH, 0:WIDTH] = high
    ref[0:WIDTH, WIDTH : 2 * WIDTH] = offset.astype(BF16)
    line = jnp.sum(rest, axis=0, keepdims=True)
    line = jnp.concatenate([line, jnp.zeros_like(line)], axis=1)
    ref[WIDTH : WIDTH + 16, :] = jnp.where(row == 0, line, 0.0).astype(BF16)


def load_payload(ref):
    row, column = iotas(WIDTH, WIDTH)
    line = ref[WIDTH : WIDTH + 16, 0:WIDTH].astype(F32)
    line = jnp.sum(line, axis=0, keepdims=True)
    transition = ref[0:WIDTH, 0:WIDTH].astype(F32)
    transition = transition + jnp.where(row == column, line, 0.0)
    return transition, ref[0:WIDTH, WIDTH : 2 * WIDTH].astype(F32)


def joined(pair):
    return jnp.concatenate(pair, axis=1)


def parted(array):
    return array[:, :WIDTH], array[:, WIDTH:]


def to_unit(vectors):
    return vectors * lax.rsqrt(jnp.sum(vectors * vectors, axis=-1, keepdims=True) + 1e-06)


def lower_inverses(couplings):
    rows = couplings[0].shape[0]
    row, column = iotas(rows, rows)
    identity = (row == column).astype(F32)
    inside = (row >> 3) == (column >> 3)
    powers = [jnp.where(inside, c, 0.0) for c in couplings]
    results = [identity - p for p in powers]
    span = 2
    while span < 8:
        powers = [fine(p, p) for p in powers]
        results = [fine(r, identity + p) for r, p in zip(results, powers)]
        span *= 2
    shift = 3
    while (1 << shift) < rows:
        level = ((row >> (shift + 1)) == (column >> (shift + 1))) & ((row >> shift) > (column >> shift))
        crossing = [fine(r, jnp.where(level, c, 0.0)) for r, c in zip(results, couplings)]
        results = [r - fine(x, r) for r, x in zip(results, crossing)]
        shift += 1
    return results


def chunk_kernel(
    place,
    g_ref,
    b_ref,
    q_hbm,
    k_hbm,
    v_hbm,
    local_ref,
    through_ref,
    own_ref,
    pay1_ref,
    pay2_ref,
    pay3_ref,
    q_ref,
    k_ref,
    v_ref,
    pairs,
    sems,
):
    part = place[1]
    groups, rows = g_ref.shape
    loads = [
        pltpu.make_async_copy(src, dst, sems.at[n])
        for n, (src, dst) in enumerate(
            [
                (k_hbm, k_ref),
                (q_hbm, q_ref),
                (v_hbm, v_ref),
            ]
        )
    ]
    for load in loads:
        load.start()
    row, column = iotas(rows, rows)
    causal = row >= column
    strict = row > column
    gates = g_ref[...]
    summed = exact(causal.astype(F32), gates, (1, 1))
    summed_row = exact(gates, (row <= column).astype(F32))
    betas = exact((row == column).astype(F32), b_ref[...], (1, 1))
    loads[0].wait()
    loads[1].wait()
    keys, mixings, couplings, decayed = [], [], [], []
    for h in range(groups):
        span = slice(h * WIDTH, (h + 1) * WIDTH)
        key = to_unit(k_ref[:, span].astype(F32)).astype(BF16)
        query = to_unit(q_ref[:, span].astype(F32)).astype(BF16)
        along = summed[:, h : h + 1]
        spread = along - summed_row[h : h + 1, :]
        decay = jnp.where(causal, jnp.exp(jnp.where(causal, spread, 0.0)), 0.0)
        both = dot(jnp.concatenate([key, query], axis=0), key, (1, 1))
        couplings.append(jnp.where(strict, betas[:, h : h + 1] * decay * both[:rows], 0.0))
        mixings.append((both[rows:] * decay).astype(BF16))
        keys.append(key.astype(F32))
        decayed.append(jnp.exp(along) * query.astype(F32))
    inverses = lower_inverses(couplings)
    loads[2].wait()
    for h in range(groups):
        span = slice(h * WIDTH, (h + 1) * WIDTH)
        along = summed[:, h : h + 1]
        last = summed[rows - 1 : rows, h : h + 1]
        beta = betas[:, h : h + 1]
        value = v_ref[:, span].astype(F32)
        made = fine(
            inverses[h],
            jnp.concatenate([beta * value, (beta * jnp.exp(along)) * keys[h]], axis=1),
        ).astype(BF16)
        ended = (jnp.exp(last - along) * keys[h]).astype(BF16)
        effect = dot(ended, made, (0, 0))
        inner = dot(mixings[h], made)
        local_ref[h] = inner[:, :WIDTH].astype(BF16)
        through_ref[h] = (decayed[h] - inner[:, WIDTH:]).astype(BF16)
        identity = iotas(WIDTH, WIDTH)
        kept = jnp.where(identity[0] == identity[1], jnp.exp(last), 0.0)
        pairs[h, :, 0:WIDTH] = kept - effect[:, WIDTH:]
        pairs[h, :, WIDTH:] = effect[:, :WIDTH]
    own_ref[...] = pairs[part]
    for r, ref in ((1, pay1_ref), (2, pay2_ref), (3, pay3_ref)):
        store_payload(ref, parted(pairs[part ^ r]))


def group_kernel(place, own_ref, recv1_ref, recv2_ref, recv3_ref, before_ref, all_ref, pay_ref, pairs):
    part = place[1]
    pairs[part] = own_ref[...]
    for r, ref in ((1, recv1_ref), (2, recv2_ref), (3, recv3_ref)):
        pairs[part ^ r] = joined(load_payload(ref))
    blocks = [parted(pairs[n]) for n in range(4)]
    total = blocks[0]
    for n in range(1, 4):
        before_ref[n - 1] = joined(total)
        total = compose(blocks[n], total)
    all_ref[...] = joined(total)
    store_payload(pay_ref, total)


def fetch_kernel(place, all_ref, wout_ref, wqkv_ref, stream_ref, wout_out, wqkv_out, stream_out, all_out, sems):
    width = stream_out.shape[1]
    begin = pl.multiple_of(place[2] * width, width)
    loads = [
        pltpu.make_async_copy(src, dst, sems.at[n])
        for n, (src, dst) in enumerate(
            [
                (wout_ref, wout_out),
                (wqkv_ref, wqkv_out),
                (stream_ref.at[:, pl.ds(begin, width)], stream_out),
            ]
        )
    ]
    for load in loads:
        load.start()
    all_out[...] = all_ref[...]
    for load in loads:
        load.wait()


def row_kernel(place, all_ref, recv1_ref, recv2_ref, recv3_ref, before_ref, pay_ref, pairs, starts):
    group = place[3]
    pairs[group] = all_ref[...]
    for d, ref in ((1, recv1_ref), (2, recv2_ref), (3, recv3_ref)):
        pairs[(group + 4 - d) & 3] = joined(load_payload(ref))
    row, column = iotas(WIDTH, 2 * WIDTH)
    starts[0] = (row == column).astype(F32)
    total = parted(pairs[0])
    for n in range(1, 4):
        starts[n] = joined(total)
        total = compose(parted(pairs[n]), total)
    before_ref[...] = starts[group]
    store_payload(pay_ref, total)


def state_kernel(
    place, row1_ref, row2_ref, row3_ref, before_row_ref, before_ref, mine_ref, out1_ref, out2_ref, out3_ref, states
):
    part = place[1]
    state = load_payload(row3_ref)[1]
    state = apply(load_payload(row2_ref), state)
    state = apply(load_payload(row1_ref), state)
    state = apply(parted(before_row_ref[...]), state)
    states[0] = state.astype(BF16)
    for n in range(3):
        states[n + 1] = apply(parted(before_ref[n]), state).astype(BF16)
    mine_ref[...] = states[part]
    for r, ref in ((1, out1_ref), (2, out2_ref), (3, out3_ref)):
        ref[...] = states[part ^ r]


def out_kernel(
    place, local_ref, through_ref, mine_ref, recv1_ref, recv2_ref, recv3_ref, w_ref, term_ref, *refs
):
    part = place[1]
    me = place[2]
    sent_refs, states = refs[:-1], refs[-1]
    groups = local_ref.shape[0]
    states[part] = mine_ref[...]
    for r, ref in ((1, recv1_ref), (2, recv2_ref), (3, recv3_ref)):
        states[part ^ r] = ref[...]
    normed = []
    for h in range(groups):
        result = local_ref[h].astype(F32) + dot(through_ref[h], states[h])
        normed.append(
            (
                result * lax.rsqrt(jnp.mean(result * result, axis=-1, keepdims=True) + 1e-05)
            ).astype(BF16)
        )
    normed = jnp.concatenate(normed, axis=1)
    width = term_ref.shape[1]
    count = len(sent_refs) + 1
    for r in range(count):
        begin = pl.multiple_of(lax.rem(me + r, count) * width, width)
        term = dot(normed, w_ref[:, pl.ds(begin, width)])
        if r == 0:
            term_ref[...] = term
        else:
            sent_refs[r - 1][...] = term.astype(BF16)


def hidden_kernel(stream_ref, term_ref, *refs):
    total = term_ref[...]
    for ref in refs[:-1]:
        total = total + ref[...].astype(F32)
    refs[-1][...] = (stream_ref[...].astype(F32) + total).astype(BF16)


def project_kernel(place, w_ref, *refs):
    me = place[2]
    blocks, (q_ref, kv_ref) = refs[:-2], refs[-2:]
    count = len(blocks)
    rows, width = blocks[0].shape
    values = [ref[...].astype(F32) for ref in blocks]
    squares = sum(jnp.sum(v * v, axis=-1, keepdims=True) for v in values)
    scale = lax.rsqrt(squares / (count * width) + 1e-05)
    total = None
    for r in range(count):
        begin = pl.multiple_of(lax.rem(me + count - r, count) * width, width)
        part = dot((values[r] * scale).astype(BF16), w_ref[pl.ds(begin, width), :])
        total = part if total is None else total + part
    groups = q_ref.shape[1] // WIDTH
    for h in range(groups):
        base = h * 3 * WIDTH
        span = slice(h * WIDTH, (h + 1) * WIDTH)
        q_ref[:, span] = to_unit(total[:, base : base + WIDTH]).astype(BF16)
        kv_ref[:, span] = to_unit(total[:, base + WIDTH : base + 2 * WIDTH]).astype(BF16)
        kv_ref[:, groups * WIDTH + h * WIDTH : groups * WIDTH + (h + 1) * WIDTH] = total[
            :, base + 2 * WIDTH : base + 3 * WIDTH
        ].astype(BF16)


def window_parts(place, q_ref, blocks, first, mixed, totals):
    seq = place[0]
    core = seq & 1
    rows = q_ref.shape[0]
    groups = q_ref.shape[1] // WIDTH
    row, column = iotas(rows, rows)
    query_place = seq * rows + row
    for n, ref in enumerate(blocks):
        owner = seq - 2 * (first + n // 2)
        if n % 2 == 1:
            owner = owner + 1 - 2 * core
        key_place = owner * rows + column
        allowed = (key_place <= query_place) & (key_place > query_place - WINDOW) & (key_place >= 0)
        for h in range(groups):
            span = slice(h * WIDTH, (h + 1) * WIDTH)
            scores = SCORE_SCALE * dot(q_ref[:, span], ref[:, span], (1, 1))
            weights = jnp.where(allowed, jnp.exp(scores), 0.0)
            total = jnp.sum(weights, axis=-1, keepdims=True)
            part = dot(
                weights.astype(BF16),
                ref[:, (groups + h) * WIDTH : (groups + h + 1) * WIDTH],
            )
            mixed[h] = part if mixed[h] is None else mixed[h] + part
            totals[h] = total if totals[h] is None else totals[h] + total


def near_kernel(place, hidden_ref, q_ref, *refs):
    blocks, (mixed_ref, total_ref, keep_ref) = refs[:-3], refs[-3:]
    keep_ref[...] = hidden_ref[...]
    groups = q_ref.shape[1] // WIDTH
    mixed, totals = [None] * groups, [None] * groups
    window_parts(place, q_ref, blocks, 0, mixed, totals)
    for h in range(groups):
        span = slice(h * WIDTH, (h + 1) * WIDTH)
        mixed_ref[:, span] = mixed[h]
        total_ref[:, span] = jnp.broadcast_to(totals[h], mixed[h].shape)


def third_kernel(place, q_ref, mixed_ref, total_ref, own_ref, other_ref, mixed_out, total_out):
    groups = q_ref.shape[1] // WIDTH
    rows = q_ref.shape[0]
    spans = [slice(h * WIDTH, (h + 1) * WIDTH) for h in range(groups)]
    mixed = [mixed_ref[:, span] for span in spans]
    totals = [total_ref[:, span] for span in spans]
    window_parts(place, q_ref, [own_ref, other_ref], WINDOW // (2 * rows) - 1, mixed, totals)
    for h, span in enumerate(spans):
        mixed_out[:, span] = mixed[h]
        total_out[:, span] = totals[h]


def last_kernel(place, q_ref, mixed_ref, total_ref, own_ref, other_ref, out_ref):
    groups = q_ref.shape[1] // WIDTH
    rows = q_ref.shape[0]
    spans = [slice(h * WIDTH, (h + 1) * WIDTH) for h in range(groups)]
    mixed = [mixed_ref[:, span] for span in spans]
    totals = [total_ref[:, span] for span in spans]
    window_parts(place, q_ref, [own_ref, other_ref], WINDOW // (2 * rows), mixed, totals)
    for h, span in enumerate(spans):
        out_ref[:, span] = (mixed[h] / totals[h]).astype(BF16)


def call(kernel, outs, smem=0, scratch=(), spaces=None, limit=LIMIT):
    def run(*args):
        places = [SMEM] * smem + (spaces or [VMEM] * (len(args) - smem))
        return pl.pallas_call(
            kernel,
            out_shape=[jax.ShapeDtypeStruct(shape, kind) for shape, kind in outs],
            in_specs=[pl.BlockSpec(memory_space=place) for place in places],
            out_specs=[pl.BlockSpec(memory_space=VMEM)] * len(outs),
            scratch_shapes=list(scratch),
            compiler_params=pltpu.CompilerParams(vmem_limit_bytes=limit),
        )(*args)

    return run


def moved(array, axis, distance):
    size = lax.axis_size(axis)
    return lax.ppermute(array, axis, [(i, i + distance) for i in range(size - distance)])


def turned(array, axis, distance):
    size = lax.axis_size(axis)
    return lax.ppermute(array, axis, [(i, (i + distance) % size) for i in range(size)])


def crossed(array, mask):
    return lax.ppermute(array, "seq", [(i, i ^ mask) for i in range(lax.axis_size("seq"))])


def rotated(array, distance):
    return lax.ppermute(
        array,
        "seq",
        [(i, (i & -16) + ((i + 4 * distance) & 15)) for i in range(lax.axis_size("seq"))],
    )


def body(queries, keys, values, gate_log, beta, stream, w_out, w_qkv):
    rows, wide = queries.shape
    groups = gate_log.shape[1]
    seq = lax.axis_index("seq")
    head = lax.axis_index("head")
    heads = lax.axis_size("head")
    place = jnp.stack([seq, seq & 3, head, (seq >> 2) & 3]).astype(jnp.int32)
    pair_shape = ((WIDTH, 2 * WIDTH), F32)
    pay_shape = ((WIDTH + 16, 2 * WIDTH), BF16)
    state_shape = ((WIDTH, WIDTH), BF16)
    row_shape = ((rows, wide), BF16)
    four_pairs = pltpu.VMEM((4, WIDTH, 2 * WIDTH), F32)
    four_states = pltpu.VMEM((4, WIDTH, WIDTH), BF16)

    local, through, own, pay1, pay2, pay3 = call(
        chunk_kernel,
        [((groups, rows, WIDTH), BF16)] * 2 + [pair_shape]
        + [pay_shape] * 3,
        1,
        [pltpu.VMEM((rows, wide), BF16)] * 3 + [four_pairs, pltpu.SemaphoreType.DMA((3,))],
        [VMEM, VMEM] + [pltpu.HBM] * 3,
        CHUNK_LIMIT,
    )(place, gate_log.T, beta.T, queries, keys, values)
    before, everything, pay = call(
        group_kernel, [((3, WIDTH, 2 * WIDTH), F32), pair_shape, pay_shape], 1, [four_pairs]
    )(place, own, crossed(pay1, 1), crossed(pay2, 2), crossed(pay3, 3))
    rowed = [rotated(pay, d) for d in (1, 2, 3)]
    everything, w_out, w_qkv, stream = lax.optimization_barrier((everything, w_out, w_qkv, stream))
    w_out, w_qkv, stream, everything = call(
        fetch_kernel,
        [(w_out.shape, BF16), (w_qkv.shape, BF16), row_shape, pair_shape],
        1,
        [pltpu.SemaphoreType.DMA((3,))],
        [VMEM] + [pl.ANY] * 3,
    )(place, everything, w_out, w_qkv, stream)
    before_row, pay = call(row_kernel, [pair_shape, pay_shape], 1, [four_pairs] * 2)(
        place, everything, *rowed
    )
    mine, out1, out2, out3 = call(state_kernel, [state_shape] * 4, 1, [four_states])(
        place, *[moved(pay, "seq", 16 * d) for d in (1, 2, 3)], before_row, before
    )
    terms = call(
        out_kernel,
        [((rows, wide), F32)] + [row_shape] * (heads - 1),
        1,
        [four_states],
    )(
        place,
        local,
        through,
        mine,
        crossed(out1, 1),
        crossed(out2, 2),
        crossed(out3, 3),
        w_out,
    )
    received = [turned(terms[r], "head", r) for r in range(1, heads)]
    (hidden,) = call(hidden_kernel, [row_shape])(stream, terms[0], *received)
    others = [turned(hidden, "head", r) for r in range(1, heads)]
    unit_queries, pack = call(project_kernel, [row_shape, ((rows, 2 * wide), BF16)], 1)(
        place, w_qkv, hidden, *others
    )
    hops = [pack]
    for _ in range(WINDOW // (2 * rows) - 1):
        hops.append(moved(hops[-1], "seq", 2))
    blocks = [block for hop in hops[:-1] for block in (hop, crossed(hop, 1))]
    sums = [((rows, wide), F32)] * 2
    mixed, totals, kept = call(near_kernel, sums + [row_shape], 1)(
        place, hidden, unit_queries, *blocks
    )
    third, mixed, totals = lax.optimization_barrier((hops[-1], mixed, totals))
    fourth = moved(third, "seq", 2)
    mixed, totals = call(third_kernel, sums, 1)(
        place, unit_queries, mixed, totals, third, crossed(third, 1)
    )
    (attended,) = call(last_kernel, [row_shape], 1)(
        place, unit_queries, mixed, totals, fourth, crossed(fourth, 1)
    )
    return (kept, attended)


def solution(mesh):
    in_specs = (
        P("seq", "head"),
        P("seq", "head"),
        P("seq", "head"),
        P("seq", "head"),
        P("seq", "head"),
        P("seq", None),
        P("head", None),
        P(None, "head"),
    )
    out_specs = (P("seq", "head"), P("seq", "head"))
    return jax.shard_map(body, mesh=mesh, in_specs=in_specs, out_specs=out_specs, check_vma=False)
```

```python
import functools

import jax
import jax.numpy as jnp
from jax import lax
from jax.experimental import pallas as pl
from jax.experimental.pallas import tpu as pltpu
from jax.sharding import PartitionSpec as P

WINDOW = 1024
WIDTH = 128
SCORE_SCALE = 10.0
F32 = jnp.float32
BF16 = jnp.bfloat16
HIGHEST = lax.Precision.HIGHEST
VMEM = pltpu.VMEM
SMEM = pltpu.SMEM
LIMIT = 16 * 1024 * 1024
FETCH_LIMIT = 44 * 1024 * 1024
CHUNK_LIMIT = 54579 * 1024


def dot(left, right, contract=(1, 0), precision=None):
    return lax.dot_general(
        left,
        right,
        (((contract[0],), (contract[1],)), ((), ())),
        precision=precision,
        preferred_element_type=F32,
    )


def exact(left, right, contract=(1, 0)):
    return dot(left, right, contract, HIGHEST)


def iotas(rows, columns):
    return (
        lax.broadcasted_iota(jnp.int32, (rows, columns), 0),
        lax.broadcasted_iota(jnp.int32, (rows, columns), 1),
    )


def fine(left, right, contract=(1, 0)):
    left_high = left.astype(BF16)
    right_high = right.astype(BF16)
    left_low = (left - left_high.astype(F32)).astype(BF16)
    right_low = (right - right_high.astype(F32)).astype(BF16)
    return (
        dot(left_high, right_high, contract)
        + dot(left_high, right_low, contract)
        + dot(left_low, right_high, contract)
    )


def split_diagonal(matrix):
    row, column = iotas(WIDTH, WIDTH)
    high = matrix.astype(BF16)
    return high, jnp.where(row == column, matrix - high.astype(F32), 0.0)


def compose(left, right):
    left_t, left_o = left
    right_t, right_o = right
    left_high, left_rest = split_diagonal(left_t)
    right_high, right_rest = split_diagonal(right_t)
    left_column = jnp.sum(left_rest, axis=1, keepdims=True)
    right_row = jnp.sum(right_rest, axis=0, keepdims=True)
    offset = dot(left_high, right_o.astype(BF16)) + left_column * right_o + left_o
    product = dot(left_high, right_high) + left_column * right_t + left_high.astype(F32) * right_row
    return product, offset


def apply(left, state):
    left_t, left_o = left
    left_high, left_rest = split_diagonal(left_t)
    left_column = jnp.sum(left_rest, axis=1, keepdims=True)
    return dot(left_high, state.astype(BF16)) + left_column * state + left_o


def store_payload(ref, pair):
    row, _ = iotas(16, 2 * WIDTH)
    transition, offset = pair
    high, rest = split_diagonal(transition)
    ref[0:WIDTH, 0:WIDTH] = high
    ref[0:WIDTH, WIDTH : 2 * WIDTH] = offset.astype(BF16)
    line = jnp.sum(rest, axis=0, keepdims=True)
    line = jnp.concatenate([line, jnp.zeros_like(line)], axis=1)
    ref[WIDTH : WIDTH + 16, :] = jnp.where(row == 0, line, 0.0).astype(BF16)


def load_payload(ref):
    row, column = iotas(WIDTH, WIDTH)
    line = ref[WIDTH : WIDTH + 16, 0:WIDTH].astype(F32)
    line = jnp.sum(line, axis=0, keepdims=True)
    transition = ref[0:WIDTH, 0:WIDTH].astype(F32)
    transition = transition + jnp.where(row == column, line, 0.0)
    return transition, ref[0:WIDTH, WIDTH : 2 * WIDTH].astype(F32)


def joined(pair):
    return jnp.concatenate(pair, axis=1)


def parted(array):
    return array[:, :WIDTH], array[:, WIDTH:]


def to_unit(vectors):
    return vectors * lax.rsqrt(jnp.sum(vectors * vectors, axis=-1, keepdims=True) + 1e-06)


def lower_inverses(couplings):
    rows = couplings[0].shape[0]
    row, column = iotas(rows, rows)
    identity = (row == column).astype(F32)
    inside = (row >> 3) == (column >> 3)
    powers = [jnp.where(inside, c, 0.0) for c in couplings]
    results = [identity - p for p in powers]
    span = 2
    while span < 8:
        powers = [fine(p, p) for p in powers]
        results = [fine(r, identity + p) for r, p in zip(results, powers)]
        span *= 2
    shift = 3
    while (1 << shift) < rows:
        level = ((row >> (shift + 1)) == (column >> (shift + 1))) & ((row >> shift) > (column >> shift))
        crossing = [fine(r, jnp.where(level, c, 0.0)) for r, c in zip(results, couplings)]
        results = [r - fine(x, r) for r, x in zip(results, crossing)]
        shift += 1
    return results


def chunk_kernel(
    place,
    g_ref,
    b_ref,
    q_hbm,
    k_hbm,
    v_hbm,
    local_ref,
    through_ref,
    own_ref,
    pay1_ref,
    pay2_ref,
    pay3_ref,
    q_ref,
    k_ref,
    v_ref,
    pairs,
    sems,
):
    part = place[1]
    groups, rows = g_ref.shape
    loads = [
        pltpu.make_async_copy(src, dst, sems.at[n])
        for n, (src, dst) in enumerate(
            [
                (k_hbm, k_ref),
                (q_hbm, q_ref),
                (v_hbm, v_ref),
            ]
        )
    ]
    for load in loads:
        load.start()
    row, column = iotas(rows, rows)
    causal = row >= column
    strict = row > column
    gates = g_ref[...]
    summed = exact(causal.astype(F32), gates, (1, 1))
    summed_row = exact(gates, (row <= column).astype(F32))
    betas = exact((row == column).astype(F32), b_ref[...], (1, 1))
    loads[0].wait()
    loads[1].wait()
    keys, mixings, couplings, decayed = [], [], [], []
    for h in range(groups):
        span = slice(h * WIDTH, (h + 1) * WIDTH)
        key = to_unit(k_ref[:, span].astype(F32)).astype(BF16)
        query = to_unit(q_ref[:, span].astype(F32)).astype(BF16)
        along = summed[:, h : h + 1]
        spread = along - summed_row[h : h + 1, :]
        decay = jnp.where(causal, jnp.exp(jnp.where(causal, spread, 0.0)), 0.0)
        both = dot(jnp.concatenate([key, query], axis=0), key, (1, 1))
        couplings.append(jnp.where(strict, betas[:, h : h + 1] * decay * both[:rows], 0.0))
        mixings.append((both[rows:] * decay).astype(BF16))
        keys.append(key.astype(F32))
        decayed.append(jnp.exp(along) * query.astype(F32))
    inverses = lower_inverses(couplings)
    loads[2].wait()
    for h in range(groups):
        span = slice(h * WIDTH, (h + 1) * WIDTH)
        along = summed[:, h : h + 1]
        last = summed[rows - 1 : rows, h : h + 1]
        beta = betas[:, h : h + 1]
        value = v_ref[:, span].astype(F32)
        made = fine(
            inverses[h],
            jnp.concatenate([beta * value, (beta * jnp.exp(along)) * keys[h]], axis=1),
        ).astype(BF16)
        ended = (jnp.exp(last - along) * keys[h]).astype(BF16)
        effect = dot(ended, made, (0, 0))
        inner = dot(mixings[h], made)
        local_ref[h] = inner[:, :WIDTH].astype(BF16)
        through_ref[h] = (decayed[h] - inner[:, WIDTH:]).astype(BF16)
        identity = iotas(WIDTH, WIDTH)
        kept = jnp.where(identity[0] == identity[1], jnp.exp(last), 0.0)
        pairs[h, :, 0:WIDTH] = kept - effect[:, WIDTH:]
        pairs[h, :, WIDTH:] = effect[:, :WIDTH]
    own_ref[...] = pairs[part]
    for r, ref in ((1, pay1_ref), (2, pay2_ref), (3, pay3_ref)):
        store_payload(ref, parted(pairs[part ^ r]))


def group_kernel(place, own_ref, recv1_ref, recv2_ref, recv3_ref, before_ref, all_ref, pay_ref, pairs):
    part = place[1]
    pairs[part] = own_ref[...]
    for r, ref in ((1, recv1_ref), (2, recv2_ref), (3, recv3_ref)):
        pairs[part ^ r] = joined(load_payload(ref))
    blocks = [parted(pairs[n]) for n in range(4)]
    total = blocks[0]
    for n in range(1, 4):
        before_ref[n - 1] = joined(total)
        total = compose(blocks[n], total)
    all_ref[...] = joined(total)
    store_payload(pay_ref, total)


def fetch_wide_kernel(token_ref, source_ref, fetched_ref, token_out, sem):
    load = pltpu.make_async_copy(source_ref, fetched_ref, sem)
    load.start()
    token_out[...] = token_ref[...]
    load.wait()


def fetch_kernel(place, token_ref, weight_ref, stream_ref, weight_out, stream_out, token_out, sems):
    width = stream_out.shape[1]
    begin = pl.multiple_of(place[2] * width, width)
    loads = [
        pltpu.make_async_copy(weight_ref, weight_out, sems.at[0]),
        pltpu.make_async_copy(stream_ref.at[:, pl.ds(begin, width)], stream_out, sems.at[1]),
    ]
    for load in loads:
        load.start()
    token_out[...] = token_ref[...]
    for load in loads:
        load.wait()


def row_kernel(place, all_ref, recv1_ref, recv2_ref, recv3_ref, before_ref, pay_ref, pairs, starts):
    group = place[3]
    pairs[group] = all_ref[...]
    for d, ref in ((1, recv1_ref), (2, recv2_ref), (3, recv3_ref)):
        pairs[(group + 4 - d) & 3] = joined(load_payload(ref))
    row, column = iotas(WIDTH, 2 * WIDTH)
    starts[0] = (row == column).astype(F32)
    total = parted(pairs[0])
    for n in range(1, 4):
        starts[n] = joined(total)
        total = compose(parted(pairs[n]), total)
    before_ref[...] = starts[group]
    store_payload(pay_ref, total)


def state_kernel(
    place, row1_ref, row2_ref, row3_ref, before_row_ref, before_ref, mine_ref, out1_ref, out2_ref, out3_ref, states
):
    part = place[1]
    state = load_payload(row3_ref)[1]
    state = apply(load_payload(row2_ref), state)
    state = apply(load_payload(row1_ref), state)
    state = apply(parted(before_row_ref[...]), state)
    states[0] = state.astype(BF16)
    for n in range(3):
        states[n + 1] = apply(parted(before_ref[n]), state).astype(BF16)
    mine_ref[...] = states[part]
    for r, ref in ((1, out1_ref), (2, out2_ref), (3, out3_ref)):
        ref[...] = states[part ^ r]


def out_kernel(
    place, local_ref, through_ref, mine_ref, recv1_ref, recv2_ref, recv3_ref, w_ref, term_ref, *refs
):
    part = place[1]
    me = place[2]
    sent_refs, states = refs[:-1], refs[-1]
    groups = local_ref.shape[0]
    states[part] = mine_ref[...]
    for r, ref in ((1, recv1_ref), (2, recv2_ref), (3, recv3_ref)):
        states[part ^ r] = ref[...]
    normed = []
    for h in range(groups):
        result = local_ref[h].astype(F32) + dot(through_ref[h], states[h])
        normed.append(
            (
                result * lax.rsqrt(jnp.mean(result * result, axis=-1, keepdims=True) + 1e-05)
            ).astype(BF16)
        )
    normed = jnp.concatenate(normed, axis=1)
    width = term_ref.shape[1]
    count = len(sent_refs) + 1
    for r in range(count):
        begin = pl.multiple_of(lax.rem(me + r, count) * width, width)
        term = dot(normed, w_ref[:, pl.ds(begin, width)])
        if r == 0:
            term_ref[...] = term
        else:
            sent_refs[r - 1][...] = term.astype(BF16)


def hidden_kernel(stream_ref, term_ref, *refs):
    total = term_ref[...]
    for ref in refs[:-1]:
        total = total + ref[...].astype(F32)
    refs[-1][...] = (stream_ref[...].astype(F32) + total).astype(BF16)


def project_kernel(place, w_ref, *refs):
    me = place[2]
    blocks, (q_ref, kv_ref) = refs[:-2], refs[-2:]
    count = len(blocks)
    rows, width = blocks[0].shape
    values = [ref[...].astype(F32) for ref in blocks]
    squares = sum(jnp.sum(v * v, axis=-1, keepdims=True) for v in values)
    scale = lax.rsqrt(squares / (count * width) + 1e-05)
    total = None
    for r in range(count):
        begin = pl.multiple_of(lax.rem(me + count - r, count) * width, width)
        part = dot((values[r] * scale).astype(BF16), w_ref[pl.ds(begin, width), :])
        total = part if total is None else total + part
    groups = q_ref.shape[1] // WIDTH
    for h in range(groups):
        base = h * 3 * WIDTH
        span = slice(h * WIDTH, (h + 1) * WIDTH)
        q_ref[:, span] = to_unit(total[:, base : base + WIDTH]).astype(BF16)
        kv_ref[:, span] = to_unit(total[:, base + WIDTH : base + 2 * WIDTH]).astype(BF16)
        kv_ref[:, groups * WIDTH + h * WIDTH : groups * WIDTH + (h + 1) * WIDTH] = total[
            :, base + 2 * WIDTH : base + 3 * WIDTH
        ].astype(BF16)


def window_part(query_place, key_chip, core, q_ref, own_ref, other_ref, sums):
    rows = q_ref.shape[0]
    groups = q_ref.shape[1] // WIDTH
    row, column = iotas(rows, 2 * rows)
    query_place = query_place * rows + row
    own_place = (2 * key_chip + core) * rows + column
    other_place = (2 * key_chip + 1 - core) * rows + column - rows
    key_place = jnp.where(column < rows, own_place, other_place)
    allowed = (key_place <= query_place) & (key_place > query_place - WINDOW) & (key_place >= 0)
    ones = jnp.ones((2 * rows, WIDTH), BF16)
    for h in range(groups):
        span = slice(h * WIDTH, (h + 1) * WIDTH)
        value_span = slice((groups + h) * WIDTH, (groups + h + 1) * WIDTH)
        keys = jnp.concatenate([own_ref[:, span], other_ref[:, span]], axis=0)
        values = jnp.concatenate([own_ref[:, value_span], other_ref[:, value_span]], axis=0)
        scores = SCORE_SCALE * dot(q_ref[:, span], keys, (1, 1))
        weights = jnp.where(allowed, jnp.exp(scores), 0.0).astype(BF16)
        part = dot(weights, jnp.concatenate([values, ones], axis=1))
        sums[h] = part if sums[h] is None else sums[h] + part


def sum_spans(groups):
    return [slice(2 * h * WIDTH, 2 * (h + 1) * WIDTH) for h in range(groups)]


def away_kernel(place, hidden_ref, q_ref, own_ref, other_ref, sums_ref, keep_ref):
    keep_ref[...] = hidden_ref[...]
    seq = place[0]
    groups = q_ref.shape[1] // WIDTH
    sums = [None] * groups
    window_part(seq + 4, (seq >> 1) - 1, seq & 1, q_ref, own_ref, other_ref, sums)
    for h, span in enumerate(sum_spans(groups)):
        sums_ref[:, span] = sums[h]


def back_kernel(place, q_ref, sums_ref, own_ref, other_ref, back_ref):
    seq = place[0]
    rows = q_ref.shape[0]
    groups = q_ref.shape[1] // WIDTH
    sums = [sums_ref[:, span] for span in sum_spans(groups)]
    window_part(seq + 4, (seq >> 1) - 2, seq & 1, q_ref, own_ref, other_ref, sums)
    _, column = iotas(rows, WIDTH)
    totals = jnp.zeros((rows, WIDTH), BF16)
    for h in range(groups):
        back_ref[:, h * WIDTH : (h + 1) * WIDTH] = sums[h][:, :WIDTH].astype(BF16)
        total = sums[h][:, WIDTH:]
        high = total.astype(BF16)
        low = (total - high.astype(F32)).astype(BF16)
        totals = jnp.where(column == 2 * h, high, jnp.where(column == 2 * h + 1, low, totals))
    back_ref[:, groups * WIDTH :] = totals


def home_kernel(place, q_ref, *refs):
    blocks, sums_ref = refs[:-1], refs[-1]
    seq = place[0]
    groups = q_ref.shape[1] // WIDTH
    sums = [None] * groups
    for n in range(len(blocks) // 2):
        window_part(
            seq, (seq >> 1) - n, seq & 1, q_ref, blocks[2 * n], blocks[2 * n + 1], sums
        )
    for h, span in enumerate(sum_spans(groups)):
        sums_ref[:, span] = sums[h]


def last_kernel(sums_ref, back_ref, out_ref):
    groups = out_ref.shape[1] // WIDTH
    totals = back_ref[:, groups * WIDTH :].astype(F32)
    for h in range(groups):
        far = totals[:, 2 * h : 2 * h + 1] + totals[:, 2 * h + 1 : 2 * h + 2]
        span = slice(h * WIDTH, (h + 1) * WIDTH)
        mixed = sums_ref[:, 2 * h * WIDTH : (2 * h + 1) * WIDTH] + back_ref[:, span].astype(F32)
        total = sums_ref[:, (2 * h + 1) * WIDTH : (2 * h + 2) * WIDTH] + far
        out_ref[:, span] = (mixed / total).astype(BF16)


def call(kernel, outs, smem=0, scratch=(), spaces=None, limit=LIMIT):
    def run(*args):
        places = [SMEM] * smem + (spaces or [VMEM] * (len(args) - smem))
        return pl.pallas_call(
            kernel,
            out_shape=[jax.ShapeDtypeStruct(shape, kind) for shape, kind in outs],
            in_specs=[pl.BlockSpec(memory_space=place) for place in places],
            out_specs=[pl.BlockSpec(memory_space=VMEM)] * len(outs),
            scratch_shapes=list(scratch),
            compiler_params=pltpu.CompilerParams(vmem_limit_bytes=limit),
        )(*args)

    return run


def moved(array, axis, distance):
    size = lax.axis_size(axis)
    return lax.ppermute(
        array, axis, [(i, i + distance) for i in range(size) if 0 <= i + distance < size]
    )


def turned(array, axis, distance):
    size = lax.axis_size(axis)
    return lax.ppermute(array, axis, [(i, (i + distance) % size) for i in range(size)])


def crossed(array, mask):
    return lax.ppermute(array, "seq", [(i, i ^ mask) for i in range(lax.axis_size("seq"))])


def rotated(array, distance):
    return lax.ppermute(
        array,
        "seq",
        [(i, (i & -16) + ((i + 4 * distance) & 15)) for i in range(lax.axis_size("seq"))],
    )


def body(queries, keys, values, gate_log, beta, stream, w_out, w_qkv):
    rows, wide = queries.shape
    groups = gate_log.shape[1]
    seq = lax.axis_index("seq")
    head = lax.axis_index("head")
    heads = lax.axis_size("head")
    place = jnp.stack([seq, seq & 3, head, (seq >> 2) & 3]).astype(jnp.int32)
    pair_shape = ((WIDTH, 2 * WIDTH), F32)
    pay_shape = ((WIDTH + 16, 2 * WIDTH), BF16)
    state_shape = ((WIDTH, WIDTH), BF16)
    row_shape = ((rows, wide), BF16)
    four_pairs = pltpu.VMEM((4, WIDTH, 2 * WIDTH), F32)
    four_states = pltpu.VMEM((4, WIDTH, WIDTH), BF16)

    local, through, own, pay1, pay2, pay3 = call(
        chunk_kernel,
        [((groups, rows, WIDTH), BF16)] * 2 + [pair_shape]
        + [pay_shape] * 3,
        1,
        [pltpu.VMEM((rows, wide), BF16)] * 3 + [four_pairs, pltpu.SemaphoreType.DMA((3,))],
        [VMEM, VMEM] + [pltpu.HBM] * 3,
        CHUNK_LIMIT,
    )(place, gate_log.T, beta.T, queries, keys, values)
    before, everything, pay = call(
        group_kernel, [((3, WIDTH, 2 * WIDTH), F32), pair_shape, pay_shape], 1, [four_pairs]
    )(place, own, crossed(pay1, 1), crossed(pay2, 2), crossed(pay3, 3))
    rowed = [rotated(pay, d) for d in (1, 2, 3)]
    everything, w_qkv = lax.optimization_barrier((everything, w_qkv))
    w_qkv, everything = call(
        fetch_wide_kernel,
        [(w_qkv.shape, BF16), pair_shape],
        0,
        [pltpu.SemaphoreType.DMA],
        [VMEM, pltpu.HBM],
        FETCH_LIMIT,
    )(everything, w_qkv)
    before_row, pay = call(row_kernel, [pair_shape, pay_shape], 1, [four_pairs] * 2)(
        place, everything, *rowed
    )
    earlier = [moved(pay, "seq", 16 * d) for d in (1, 2, 3)]
    before_row, w_out, stream = lax.optimization_barrier((before_row, w_out, stream))
    w_out, stream, before_row = call(
        fetch_kernel,
        [(w_out.shape, BF16), row_shape, pair_shape],
        1,
        [pltpu.SemaphoreType.DMA((2,))],
        [VMEM, pltpu.HBM, pltpu.HBM],
        FETCH_LIMIT,
    )(place, before_row, w_out, stream)
    mine, out1, out2, out3 = call(state_kernel, [state_shape] * 4, 1, [four_states])(
        place, *earlier, before_row, before
    )
    terms = call(
        out_kernel,
        [((rows, wide), F32)] + [row_shape] * (heads - 1),
        1,
        [four_states],
    )(
        place,
        local,
        through,
        mine,
        crossed(out1, 1),
        crossed(out2, 2),
        crossed(out3, 3),
        w_out,
    )
    received = [turned(terms[r], "head", r) for r in range(1, heads)]
    (hidden,) = call(hidden_kernel, [row_shape])(stream, terms[0], *received)
    others = [turned(hidden, "head", r) for r in range(1, heads)]
    unit_queries, pack = call(project_kernel, [row_shape, ((rows, 2 * wide), BF16)], 1)(
        place, w_qkv, hidden, *others
    )
    first, visitors = lax.optimization_barrier(
        (moved(pack, "seq", 2), moved(unit_queries, "seq", -4))
    )
    home = [pack, crossed(pack, 1), first, crossed(first, 1)]
    sums_shape = ((rows, 2 * wide), F32)
    away, kept = call(away_kernel, [sums_shape, row_shape], 1)(
        place, hidden, visitors, home[2], home[3]
    )
    second, away = lax.optimization_barrier((moved(first, "seq", 2), away))
    home += [second, crossed(second, 1)]
    (back,) = call(back_kernel, [((rows, wide + WIDTH), BF16)], 1)(
        place, visitors, away, home[4], home[5]
    )
    returned = moved(back, "seq", 4)
    (sums,) = call(home_kernel, [sums_shape], 1)(place, unit_queries, *home)
    (attended,) = call(last_kernel, [row_shape])(sums, returned)
    return (kept, attended)


def solution(mesh):
    in_specs = (
        P("seq", "head"),
        P("seq", "head"),
        P("seq", "head"),
        P("seq", "head"),
        P("seq", "head"),
        P("seq", None),
        P("head", None),
        P(None, "head"),
    )
    out_specs = (P("seq", "head"), P("seq", "head"))
    return jax.shard_map(body, mesh=mesh, in_specs=in_specs, out_specs=out_specs, check_vma=False)
```

```python
import functools

import jax
import jax.numpy as jnp
from jax import lax
from jax.experimental import pallas as pl
from jax.experimental.pallas import tpu as pltpu
from jax.sharding import PartitionSpec as P

WINDOW = 1024
WIDTH = 128
SCORE_SCALE = 10.0
F32 = jnp.float32
BF16 = jnp.bfloat16
HIGHEST = lax.Precision.HIGHEST
VMEM = pltpu.VMEM
SMEM = pltpu.SMEM
LIMIT = 16 * 1024 * 1024
FETCH_LIMIT = 44 * 1024 * 1024
CHUNK_LIMIT = 54448 * 1024


def dot(left, right, contract=(1, 0), precision=None):
    return lax.dot_general(
        left,
        right,
        (((contract[0],), (contract[1],)), ((), ())),
        precision=precision,
        preferred_element_type=F32,
    )


def exact(left, right, contract=(1, 0)):
    return dot(left, right, contract, HIGHEST)


def iotas(rows, columns):
    return (
        lax.broadcasted_iota(jnp.int32, (rows, columns), 0),
        lax.broadcasted_iota(jnp.int32, (rows, columns), 1),
    )


def fine(left, right, contract=(1, 0)):
    left_high = left.astype(BF16)
    right_high = right.astype(BF16)
    left_low = (left - left_high.astype(F32)).astype(BF16)
    right_low = (right - right_high.astype(F32)).astype(BF16)
    return (
        dot(left_high, right_high, contract)
        + dot(left_high, right_low, contract)
        + dot(left_low, right_high, contract)
    )


def split_diagonal(matrix):
    row, column = iotas(WIDTH, WIDTH)
    high = matrix.astype(BF16)
    return high, jnp.where(row == column, matrix - high.astype(F32), 0.0)


def compose(left, right):
    left_t, left_o = left
    right_t, right_o = right
    left_high, left_rest = split_diagonal(left_t)
    right_high, right_rest = split_diagonal(right_t)
    left_column = jnp.sum(left_rest, axis=1, keepdims=True)
    right_row = jnp.sum(right_rest, axis=0, keepdims=True)
    offset = dot(left_high, right_o.astype(BF16)) + left_column * right_o + left_o
    product = dot(left_high, right_high) + left_column * right_t + left_high.astype(F32) * right_row
    return product, offset


def apply(left, state):
    left_t, left_o = left
    left_high, left_rest = split_diagonal(left_t)
    left_column = jnp.sum(left_rest, axis=1, keepdims=True)
    return dot(left_high, state.astype(BF16)) + left_column * state + left_o


def store_payload(ref, pair):
    row, _ = iotas(16, 2 * WIDTH)
    transition, offset = pair
    high, rest = split_diagonal(transition)
    ref[0:WIDTH, 0:WIDTH] = high
    ref[0:WIDTH, WIDTH : 2 * WIDTH] = offset.astype(BF16)
    line = jnp.sum(rest, axis=0, keepdims=True)
    line = jnp.concatenate([line, jnp.zeros_like(line)], axis=1)
    ref[WIDTH : WIDTH + 16, :] = jnp.where(row == 0, line, 0.0).astype(BF16)


def load_payload(ref):
    row, column = iotas(WIDTH, WIDTH)
    line = ref[WIDTH : WIDTH + 16, 0:WIDTH].astype(F32)
    line = jnp.sum(line, axis=0, keepdims=True)
    transition = ref[0:WIDTH, 0:WIDTH].astype(F32)
    transition = transition + jnp.where(row == column, line, 0.0)
    return transition, ref[0:WIDTH, WIDTH : 2 * WIDTH].astype(F32)


def joined(pair):
    return jnp.concatenate(pair, axis=1)


def parted(array):
    return array[:, :WIDTH], array[:, WIDTH:]


def to_unit(vectors):
    return vectors * lax.rsqrt(jnp.sum(vectors * vectors, axis=-1, keepdims=True) + 1e-06)


def lower_inverses(couplings):
    rows = couplings[0].shape[0]
    row, column = iotas(rows, rows)
    identity = (row == column).astype(F32)
    inside = (row >> 3) == (column >> 3)
    powers = [jnp.where(inside, c, 0.0) for c in couplings]
    results = [identity - p for p in powers]
    span = 2
    while span < 8:
        powers = [fine(p, p) for p in powers]
        results = [fine(r, identity + p) for r, p in zip(results, powers)]
        span *= 2
    shift = 3
    while (1 << shift) < rows:
        level = ((row >> (shift + 1)) == (column >> (shift + 1))) & ((row >> shift) > (column >> shift))
        crossing = [fine(r, jnp.where(level, c, 0.0)) for r, c in zip(results, couplings)]
        results = [r - fine(x, r) for r, x in zip(results, crossing)]
        shift += 1
    return results


def decays(g_ref):
    groups, rows = g_ref.shape
    row, column = iotas(rows, rows)
    gates = g_ref[...]
    causal = row >= column
    summed = exact(causal.astype(F32), gates, (1, 1))
    summed_row = exact(gates, (row <= column).astype(F32))
    spreads = [summed[:, h : h + 1] - summed_row[h : h + 1, :] for h in range(groups)]
    return summed, [
        jnp.where(causal, jnp.exp(jnp.where(causal, spread, 0.0)), 0.0) for spread in spreads
    ]


def map_kernel(
    place, g_ref, b_ref, k_hbm, v_hbm, keys_ref, writes_ref, erasers_ref, own_ref, pay1_ref, pay2_ref, pay3_ref, k_ref, v_ref, pairs, sems
):
    part = place[1]
    groups, rows = g_ref.shape
    loads = [
        pltpu.make_async_copy(k_hbm, k_ref, sems.at[0]),
        pltpu.make_async_copy(v_hbm, v_ref, sems.at[1]),
    ]
    for load in loads:
        load.start()
    row, column = iotas(rows, rows)
    summed, decay = decays(g_ref)
    betas = exact((row == column).astype(F32), b_ref[...], (1, 1))
    loads[0].wait()
    keys, couplings = [], []
    for h in range(groups):
        span = slice(h * WIDTH, (h + 1) * WIDTH)
        key = to_unit(k_ref[:, span].astype(F32)).astype(BF16)
        keys_ref[:, span] = key
        both = dot(key, key, (1, 1))
        couplings.append(jnp.where(row > column, betas[:, h : h + 1] * decay[h] * both, 0.0))
        keys.append(key.astype(F32))
    inverses = lower_inverses(couplings)
    loads[1].wait()
    for h in range(groups):
        span = slice(h * WIDTH, (h + 1) * WIDTH)
        along = summed[:, h : h + 1]
        last = summed[rows - 1 : rows, h : h + 1]
        beta = betas[:, h : h + 1]
        value = v_ref[:, span].astype(F32)
        made = fine(
            inverses[h],
            jnp.concatenate([beta * value, (beta * jnp.exp(along)) * keys[h]], axis=1),
        ).astype(BF16)
        writes_ref[h], erasers_ref[h] = parted(made)
        ended = (jnp.exp(last - along) * keys[h]).astype(BF16)
        effect = dot(ended, made, (0, 0))
        identity = iotas(WIDTH, WIDTH)
        kept = jnp.where(identity[0] == identity[1], jnp.exp(last), 0.0)
        pairs[h, :, 0:WIDTH] = kept - effect[:, WIDTH:]
        pairs[h, :, WIDTH:] = effect[:, :WIDTH]
    own_ref[...] = pairs[part]
    for r, ref in ((1, pay1_ref), (2, pay2_ref), (3, pay3_ref)):
        store_payload(ref, parted(pairs[part ^ r]))


def query_kernel(g_ref, q_ref, keys_ref, writes_ref, erasers_ref, local_ref, through_ref):
    groups = g_ref.shape[0]
    summed, decay = decays(g_ref)
    for h in range(groups):
        span = slice(h * WIDTH, (h + 1) * WIDTH)
        query = to_unit(q_ref[:, span].astype(F32)).astype(BF16)
        mixing = (dot(query, keys_ref[:, span], (1, 1)) * decay[h]).astype(BF16)
        inner = dot(mixing, joined((writes_ref[h], erasers_ref[h])))
        local_ref[h] = inner[:, :WIDTH].astype(BF16)
        decayed = jnp.exp(summed[:, h : h + 1]) * query.astype(F32)
        through_ref[h] = (decayed - inner[:, WIDTH:]).astype(BF16)


def prefixes(blocks):
    two = compose(blocks[1], blocks[0])
    return two, compose(blocks[2], two), compose(compose(blocks[3], blocks[2]), two)


def group_kernel(place, own_ref, recv2_ref, recv3_ref, recv1_ref, before_ref, all_ref, pay_ref, pairs):
    part = place[1]
    pairs[part] = own_ref[...]
    for r, ref in ((1, recv1_ref), (2, recv2_ref), (3, recv3_ref)):
        pairs[part ^ r] = joined(load_payload(ref))
    two, three, total = prefixes([parted(pairs[n]) for n in range(4)])
    store_payload(pay_ref, total)
    all_ref[...] = joined(total)
    before_ref[0] = pairs[0]
    before_ref[1] = joined(two)
    before_ref[2] = joined(three)


def fetch_wide_kernel(token_ref, source_ref, fetched_ref, token_out, sem):
    load = pltpu.make_async_copy(source_ref, fetched_ref, sem)
    load.start()
    token_out[...] = token_ref[...]
    load.wait()


def fetch_kernel(
    place, before_row_ref, before_ref, weight_ref, stream_ref, weight_out, stream_out, maps_ref, sems
):
    width = stream_out.shape[1]
    begin = pl.multiple_of(place[2] * width, width)
    loads = [
        pltpu.make_async_copy(weight_ref, weight_out, sems.at[0]),
        pltpu.make_async_copy(stream_ref.at[:, pl.ds(begin, width)], stream_out, sems.at[1]),
    ]
    for load in loads:
        load.start()
    maps_ref[0] = before_row_ref[...]
    for n in range(3):
        maps_ref[n + 1] = joined(compose(parted(before_ref[n]), parted(before_row_ref[...])))
    for load in loads:
        load.wait()


def row_kernel(place, all_ref, recv2_ref, recv1_ref, recv3_ref, before_ref, pay_ref, pairs, starts):
    group = place[3]
    pairs[group] = all_ref[...]
    for d, ref in ((1, recv1_ref), (2, recv2_ref), (3, recv3_ref)):
        pairs[(group + 4 - d) & 3] = joined(load_payload(ref))
    two, three, total = prefixes([parted(pairs[n]) for n in range(4)])
    store_payload(pay_ref, total)
    row, column = iotas(WIDTH, 2 * WIDTH)
    starts[0] = (row == column).astype(F32)
    starts[1] = pairs[0]
    starts[2] = joined(two)
    starts[3] = joined(three)
    before_ref[...] = starts[group]


def state_kernel(place, row2_ref, row1_ref, row3_ref, maps_ref, mine_ref, out1_ref, out2_ref, out3_ref, states):
    part = place[1]
    state = load_payload(row3_ref)[1]
    state = apply(load_payload(row2_ref), state)
    state = apply(load_payload(row1_ref), state)
    for n in range(4):
        states[n] = apply(parted(maps_ref[n]), state).astype(BF16)
    mine_ref[...] = states[part]
    for r, ref in ((1, out1_ref), (2, out2_ref), (3, out3_ref)):
        ref[...] = states[part ^ r]


def out_kernel(
    place, local_ref, through_ref, mine_ref, recv2_ref, recv3_ref, recv1_ref, w_ref, term_ref, *refs
):
    part = place[1]
    me = place[2]
    sent_refs, states = refs[:-1], refs[-1]
    groups = local_ref.shape[0]
    states[part] = mine_ref[...]
    for r, ref in ((1, recv1_ref), (2, recv2_ref), (3, recv3_ref)):
        states[part ^ r] = ref[...]
    normed = []
    for h in range(groups):
        result = local_ref[h].astype(F32) + dot(through_ref[h], states[h])
        normed.append(
            (
                result * lax.rsqrt(jnp.mean(result * result, axis=-1, keepdims=True) + 1e-05)
            ).astype(BF16)
        )
    normed = jnp.concatenate(normed, axis=1)
    width = term_ref.shape[1]
    count = len(sent_refs) + 1
    for r in range(count):
        begin = pl.multiple_of(lax.rem(me + r, count) * width, width)
        term = dot(normed, w_ref[:, pl.ds(begin, width)])
        if r == 0:
            term_ref[...] = term
        else:
            sent_refs[r - 1][...] = term.astype(BF16)


def hidden_kernel(stream_ref, term_ref, *refs):
    total = term_ref[...]
    for ref in refs[:-1]:
        total = total + ref[...].astype(F32)
    refs[-1][...] = (stream_ref[...].astype(F32) + total).astype(BF16)


def project_kernel(place, w_ref, *refs):
    me = place[2]
    blocks, (q_ref, kv_ref) = refs[:-2], refs[-2:]
    count = len(blocks)
    rows, width = blocks[0].shape
    values = [ref[...].astype(F32) for ref in blocks]
    squares = sum(jnp.sum(v * v, axis=-1, keepdims=True) for v in values)
    scale = lax.rsqrt(squares / (count * width) + 1e-05)
    total = None
    for n, r in enumerate((0, 2, 1, 3)):
        begin = pl.multiple_of(lax.rem(me + count - r, count) * width, width)
        part = dot((values[n] * scale).astype(BF16), w_ref[pl.ds(begin, width), :])
        total = part if total is None else total + part
    groups = q_ref.shape[1] // WIDTH
    for h in range(groups):
        base = h * 3 * WIDTH
        span = slice(h * WIDTH, (h + 1) * WIDTH)
        q_ref[:, span] = to_unit(total[:, base : base + WIDTH]).astype(BF16)
        kv_ref[:, span] = to_unit(total[:, base + WIDTH : base + 2 * WIDTH]).astype(BF16)
        kv_ref[:, groups * WIDTH + h * WIDTH : groups * WIDTH + (h + 1) * WIDTH] = total[
            :, base + 2 * WIDTH : base + 3 * WIDTH
        ].astype(BF16)


def window_part(query_place, key_chip, core, q_ref, own_ref, other_ref, sums):
    rows = q_ref.shape[0]
    groups = q_ref.shape[1] // WIDTH
    row, column = iotas(rows, 2 * rows)
    query_place = query_place * rows + row
    own_place = (2 * key_chip + core) * rows + column
    other_place = (2 * key_chip + 1 - core) * rows + column - rows
    key_place = jnp.where(column < rows, own_place, other_place)
    allowed = (key_place <= query_place) & (key_place > query_place - WINDOW) & (key_place >= 0)
    ones = jnp.ones((2 * rows, WIDTH), BF16)
    for h in range(groups):
        span = slice(h * WIDTH, (h + 1) * WIDTH)
        value_span = slice((groups + h) * WIDTH, (groups + h + 1) * WIDTH)
        keys = jnp.concatenate([own_ref[:, span], other_ref[:, span]], axis=0)
        values = jnp.concatenate([own_ref[:, value_span], other_ref[:, value_span]], axis=0)
        scores = SCORE_SCALE * dot(q_ref[:, span], keys, (1, 1))
        weights = jnp.where(allowed, jnp.exp(scores), 0.0).astype(BF16)
        part = dot(weights, jnp.concatenate([values, ones], axis=1))
        sums[h] = part if sums[h] is None else sums[h] + part


def sum_spans(groups):
    return [slice(2 * h * WIDTH, 2 * (h + 1) * WIDTH) for h in range(groups)]


def back_kernel(place, hidden_ref, q_ref, *refs):
    blocks, (back_ref, keep_ref) = refs[:-2], refs[-2:]
    seq = place[0]
    rows = q_ref.shape[0]
    groups = q_ref.shape[1] // WIDTH
    sums = [None] * groups
    for n in range(len(blocks) // 2):
        window_part(
            seq + 4, (seq >> 1) - 1 - n, seq & 1, q_ref, blocks[2 * n], blocks[2 * n + 1], sums
        )
    _, column = iotas(rows, WIDTH)
    totals = jnp.zeros((rows, WIDTH), BF16)
    for h in range(groups):
        back_ref[:, h * WIDTH : (h + 1) * WIDTH] = sums[h][:, :WIDTH].astype(BF16)
        total = sums[h][:, WIDTH:]
        high = total.astype(BF16)
        low = (total - high.astype(F32)).astype(BF16)
        totals = jnp.where(column == 2 * h, high, jnp.where(column == 2 * h + 1, low, totals))
    back_ref[:, groups * WIDTH :] = totals
    keep_ref[...] = hidden_ref[...]


def home_kernel(place, q_ref, *refs):
    blocks, sums_ref = refs[:-1], refs[-1]
    seq = place[0]
    groups = q_ref.shape[1] // WIDTH
    sums = [None] * groups
    for n in range(len(blocks) // 2):
        window_part(
            seq, (seq >> 1) - n, seq & 1, q_ref, blocks[2 * n], blocks[2 * n + 1], sums
        )
    for h, span in enumerate(sum_spans(groups)):
        sums_ref[:, span] = sums[h]


def last_kernel(sums_ref, back_ref, out_ref):
    groups = out_ref.shape[1] // WIDTH
    totals = back_ref[:, groups * WIDTH :].astype(F32)
    for h in range(groups):
        far = totals[:, 2 * h : 2 * h + 1] + totals[:, 2 * h + 1 : 2 * h + 2]
        span = slice(h * WIDTH, (h + 1) * WIDTH)
        mixed = sums_ref[:, 2 * h * WIDTH : (2 * h + 1) * WIDTH] + back_ref[:, span].astype(F32)
        total = sums_ref[:, (2 * h + 1) * WIDTH : (2 * h + 2) * WIDTH] + far
        out_ref[:, span] = (mixed / total).astype(BF16)


def call(kernel, outs, smem=0, scratch=(), spaces=None, limit=LIMIT):
    def run(*args):
        places = [SMEM] * smem + (spaces or [VMEM] * (len(args) - smem))
        return pl.pallas_call(
            kernel,
            out_shape=[jax.ShapeDtypeStruct(shape, kind) for shape, kind in outs],
            in_specs=[pl.BlockSpec(memory_space=place) for place in places],
            out_specs=[pl.BlockSpec(memory_space=VMEM)] * len(outs),
            scratch_shapes=list(scratch),
            compiler_params=pltpu.CompilerParams(vmem_limit_bytes=limit),
        )(*args)

    return run


def moved(array, axis, distance):
    size = lax.axis_size(axis)
    return lax.ppermute(
        array, axis, [(i, i + distance) for i in range(size) if 0 <= i + distance < size]
    )


def turned(array, axis, distance):
    size = lax.axis_size(axis)
    return lax.ppermute(array, axis, [(i, (i + distance) % size) for i in range(size)])


def crossed(array, mask):
    return lax.ppermute(array, "seq", [(i, i ^ mask) for i in range(lax.axis_size("seq"))])


def rotated(array, distance):
    return lax.ppermute(
        array,
        "seq",
        [(i, (i & -16) + ((i + 4 * distance) & 15)) for i in range(lax.axis_size("seq"))],
    )


def body(queries, keys, values, gate_log, beta, stream, w_out, w_qkv):
    rows, wide = queries.shape
    groups = gate_log.shape[1]
    seq = lax.axis_index("seq")
    head = lax.axis_index("head")
    heads = lax.axis_size("head")
    place = jnp.stack([seq, seq & 3, head, (seq >> 2) & 3]).astype(jnp.int32)
    pair_shape = ((WIDTH, 2 * WIDTH), F32)
    pay_shape = ((WIDTH + 16, 2 * WIDTH), BF16)
    state_shape = ((WIDTH, WIDTH), BF16)
    row_shape = ((rows, wide), BF16)
    four_pairs = pltpu.VMEM((4, WIDTH, 2 * WIDTH), F32)
    four_states = pltpu.VMEM((4, WIDTH, WIDTH), BF16)

    gates = gate_log.T
    unit_keys, writes, erasers, own, pay1, pay2, pay3 = call(
        map_kernel,
        [row_shape] + [((groups, rows, WIDTH), BF16)] * 2 + [pair_shape] + [pay_shape] * 3,
        1,
        [pltpu.VMEM((rows, wide), BF16)] * 2 + [four_pairs, pltpu.SemaphoreType.DMA((2,))],
        [VMEM, VMEM] + [pltpu.HBM] * 2,
        CHUNK_LIMIT,
    )(place, gates, beta.T, keys, values)
    pay2, pay3, pay1 = crossed(pay2, 2), crossed(pay3, 3), crossed(pay1, 1)
    local, through = call(query_kernel, [((groups, rows, WIDTH), BF16)] * 2)(
        gates, queries, unit_keys, writes, erasers
    )
    own, local, through = lax.optimization_barrier((own, local, through))
    before, everything, pay = call(
        group_kernel, [((3, WIDTH, 2 * WIDTH), F32), pair_shape, pay_shape], 1, [four_pairs]
    )(place, own, pay2, pay3, pay1)
    row2, row1, row3 = [rotated(pay, d) for d in (2, 1, 3)]
    everything, w_qkv = lax.optimization_barrier((everything, w_qkv))
    w_qkv, everything = call(
        fetch_wide_kernel,
        [(w_qkv.shape, BF16), pair_shape],
        0,
        [pltpu.SemaphoreType.DMA],
        [VMEM, pltpu.HBM],
        FETCH_LIMIT,
    )(everything, w_qkv)
    before_row, pay = call(row_kernel, [pair_shape, pay_shape], 1, [four_pairs] * 2)(
        place, everything, row2, row1, row3
    )
    row2, row1, row3 = [moved(pay, "seq", 16 * d) for d in (2, 1, 3)]
    before_row, w_out, stream = lax.optimization_barrier((before_row, w_out, stream))
    w_out, stream, maps = call(
        fetch_kernel,
        [(w_out.shape, BF16), row_shape, ((4, WIDTH, 2 * WIDTH), F32)],
        1,
        [pltpu.SemaphoreType.DMA((2,))],
        [VMEM, VMEM, pltpu.HBM, pltpu.HBM],
        FETCH_LIMIT,
    )(place, before_row, before, w_out, stream)
    mine, out1, out2, out3 = call(state_kernel, [state_shape] * 4, 1, [four_states])(
        place, row2, row1, row3, maps
    )
    terms = call(
        out_kernel,
        [((rows, wide), F32)] + [row_shape] * (heads - 1),
        1,
        [four_states],
    )(
        place,
        local,
        through,
        mine,
        crossed(out2, 2),
        crossed(out3, 3),
        crossed(out1, 1),
        w_out,
    )
    received = [turned(terms[r], "head", r) for r in (2, 1, 3)]
    (hidden,) = call(hidden_kernel, [row_shape])(stream, terms[0], *received)
    other2, other1, other3 = [turned(hidden, "head", r) for r in (2, 1, 3)]
    unit_queries, pack = call(project_kernel, [row_shape, ((rows, 2 * wide), BF16)], 1)(
        place, w_qkv, hidden, other2, other1, other3
    )
    first, visitors = lax.optimization_barrier(
        (moved(pack, "seq", 2), moved(unit_queries, "seq", -2))
    )
    second, visitors = lax.optimization_barrier(
        (moved(first, "seq", 2), moved(visitors, "seq", -2))
    )
    home = [
        pack, crossed(pack, 1), first, crossed(first, 1), second, crossed(second, 1)
    ]
    back, kept = call(back_kernel, [((rows, wide + WIDTH), BF16), row_shape], 1)(
        place, hidden, visitors, *home[2:]
    )
    returned = moved(back, "seq", 4)
    (sums,) = call(home_kernel, [((rows, 2 * wide), F32)], 1)(place, unit_queries, *home)
    (attended,) = call(last_kernel, [row_shape])(sums, returned)
    return (kept, attended)


def solution(mesh):
    in_specs = (
        P("seq", "head"),
        P("seq", "head"),
        P("seq", "head"),
        P("seq", "head"),
        P("seq", "head"),
        P("seq", None),
        P("head", None),
        P(None, "head"),
    )
    out_specs = (P("seq", "head"), P("seq", "head"))
    return jax.shard_map(body, mesh=mesh, in_specs=in_specs, out_specs=out_specs, check_vma=False)
```

```python
import functools

import jax
import jax.numpy as jnp
from jax import lax
from jax.experimental import pallas as pl
from jax.experimental.pallas import tpu as pltpu
from jax.sharding import PartitionSpec as P

WINDOW = 1024
WIDTH = 128
SCORE_SCALE = 10.0
F32 = jnp.float32
BF16 = jnp.bfloat16
HIGHEST = lax.Precision.HIGHEST
VMEM = pltpu.VMEM
SMEM = pltpu.SMEM
LIMIT = 16 * 1024 * 1024
FETCH_LIMIT = 44 * 1024 * 1024
CHUNK_LIMIT = 54448 * 1024


def dot(left, right, contract=(1, 0), precision=None):
    return lax.dot_general(
        left,
        right,
        (((contract[0],), (contract[1],)), ((), ())),
        precision=precision,
        preferred_element_type=F32,
    )


def exact(left, right, contract=(1, 0)):
    return dot(left, right, contract, HIGHEST)


def iotas(rows, columns):
    return (
        lax.broadcasted_iota(jnp.int32, (rows, columns), 0),
        lax.broadcasted_iota(jnp.int32, (rows, columns), 1),
    )


def fine(left, right, contract=(1, 0)):
    left_high = left.astype(BF16)
    right_high = right.astype(BF16)
    left_low = (left - left_high.astype(F32)).astype(BF16)
    right_low = (right - right_high.astype(F32)).astype(BF16)
    return (
        dot(left_high, right_high, contract)
        + dot(left_high, right_low, contract)
        + dot(left_low, right_high, contract)
    )


def split_diagonal(matrix):
    row, column = iotas(WIDTH, WIDTH)
    high = matrix.astype(BF16)
    return high, jnp.where(row == column, matrix - high.astype(F32), 0.0)


def compose(left, right):
    left_t, left_o = left
    right_t, right_o = right
    left_high, left_rest = split_diagonal(left_t)
    right_high, right_rest = split_diagonal(right_t)
    left_column = jnp.sum(left_rest, axis=1, keepdims=True)
    right_row = jnp.sum(right_rest, axis=0, keepdims=True)
    offset = dot(left_high, right_o.astype(BF16)) + left_column * right_o + left_o
    product = dot(left_high, right_high) + left_column * right_t + left_high.astype(F32) * right_row
    return product, offset


def apply(left, state):
    left_t, left_o = left
    left_high, left_rest = split_diagonal(left_t)
    left_column = jnp.sum(left_rest, axis=1, keepdims=True)
    return dot(left_high, state.astype(BF16)) + left_column * state + left_o


def store_payload(ref, pair):
    row, _ = iotas(16, 2 * WIDTH)
    transition, offset = pair
    high, rest = split_diagonal(transition)
    ref[0:WIDTH, 0:WIDTH] = high
    ref[0:WIDTH, WIDTH : 2 * WIDTH] = offset.astype(BF16)
    line = jnp.sum(rest, axis=0, keepdims=True)
    line = jnp.concatenate([line, jnp.zeros_like(line)], axis=1)
    ref[WIDTH : WIDTH + 16, :] = jnp.where(row == 0, line, 0.0).astype(BF16)


def load_payload(ref):
    row, column = iotas(WIDTH, WIDTH)
    line = ref[WIDTH : WIDTH + 16, 0:WIDTH].astype(F32)
    line = jnp.sum(line, axis=0, keepdims=True)
    transition = ref[0:WIDTH, 0:WIDTH].astype(F32)
    transition = transition + jnp.where(row == column, line, 0.0)
    return transition, ref[0:WIDTH, WIDTH : 2 * WIDTH].astype(F32)


def joined(pair):
    return jnp.concatenate(pair, axis=1)


def parted(array):
    return array[:, :WIDTH], array[:, WIDTH:]


def to_unit(vectors):
    return vectors * lax.rsqrt(jnp.sum(vectors * vectors, axis=-1, keepdims=True) + 1e-06)


def lower_inverses(couplings):
    rows = couplings[0].shape[0]
    row, column = iotas(rows, rows)
    identity = (row == column).astype(F32)
    inside = (row >> 3) == (column >> 3)
    powers = [jnp.where(inside, c, 0.0) for c in couplings]
    results = [identity - p for p in powers]
    span = 2
    while span < 8:
        powers = [fine(p, p) for p in powers]
        results = [fine(r, identity + p) for r, p in zip(results, powers)]
        span *= 2
    shift = 3
    while (1 << shift) < rows:
        level = ((row >> (shift + 1)) == (column >> (shift + 1))) & ((row >> shift) > (column >> shift))
        crossing = [fine(r, jnp.where(level, c, 0.0)) for r, c in zip(results, couplings)]
        results = [r - fine(x, r) for r, x in zip(results, crossing)]
        shift += 1
    return results


def decays(gb_ref):
    rows = gb_ref.shape[1]
    groups = gb_ref.shape[0] // 2
    row, column = iotas(rows, rows)
    gates = gb_ref[0:groups, :]
    causal = row >= column
    summed = exact(causal.astype(F32), gates, (1, 1))
    summed_row = exact(gates, (row <= column).astype(F32))
    spreads = [summed[:, h : h + 1] - summed_row[h : h + 1, :] for h in range(groups)]
    return summed, [
        jnp.where(causal, jnp.exp(jnp.where(causal, spread, 0.0)), 0.0) for spread in spreads
    ]


def map_kernel(
    place, gb_ref, k_hbm, v_hbm, keys_ref, writes_ref, erasers_ref, own_ref, pay1_ref, pay2_ref, pay3_ref, k_ref, v_ref, pairs, sems
):
    part = place[1]
    rows = gb_ref.shape[1]
    groups = gb_ref.shape[0] // 2
    loads = [
        pltpu.make_async_copy(k_hbm, k_ref, sems.at[0]),
        pltpu.make_async_copy(v_hbm, v_ref, sems.at[1]),
    ]
    for load in loads:
        load.start()
    row, column = iotas(rows, rows)
    summed, decay = decays(gb_ref)
    betas = exact((row == column).astype(F32), gb_ref[groups:, :], (1, 1))
    loads[0].wait()
    keys, couplings = [], []
    for h in range(groups):
        span = slice(h * WIDTH, (h + 1) * WIDTH)
        key = to_unit(k_ref[:, span].astype(F32)).astype(BF16)
        keys_ref[:, span] = key
        both = dot(key, key, (1, 1))
        couplings.append(jnp.where(row > column, betas[:, h : h + 1] * decay[h] * both, 0.0))
        keys.append(key.astype(F32))
    inverses = lower_inverses(couplings)
    loads[1].wait()
    for h in range(groups):
        span = slice(h * WIDTH, (h + 1) * WIDTH)
        along = summed[:, h : h + 1]
        last = summed[rows - 1 : rows, h : h + 1]
        beta = betas[:, h : h + 1]
        value = v_ref[:, span].astype(F32)
        made = fine(
            inverses[h],
            jnp.concatenate([beta * value, (beta * jnp.exp(along)) * keys[h]], axis=1),
        ).astype(BF16)
        writes_ref[h], erasers_ref[h] = parted(made)
        ended = (jnp.exp(last - along) * keys[h]).astype(BF16)
        effect = dot(ended, made, (0, 0))
        identity = iotas(WIDTH, WIDTH)
        kept = jnp.where(identity[0] == identity[1], jnp.exp(last), 0.0)
        pairs[h, :, 0:WIDTH] = kept - effect[:, WIDTH:]
        pairs[h, :, WIDTH:] = effect[:, :WIDTH]
    own_ref[...] = pairs[part]
    for r, ref in ((1, pay1_ref), (2, pay2_ref), (3, pay3_ref)):
        store_payload(ref, parted(pairs[part ^ r]))


def query_kernel(gb_ref, q_ref, keys_ref, writes_ref, erasers_ref, local_ref, through_ref):
    groups = gb_ref.shape[0] // 2
    summed, decay = decays(gb_ref)
    for h in range(groups):
        span = slice(h * WIDTH, (h + 1) * WIDTH)
        query = to_unit(q_ref[:, span].astype(F32)).astype(BF16)
        mixing = (dot(query, keys_ref[:, span], (1, 1)) * decay[h]).astype(BF16)
        inner = dot(mixing, joined((writes_ref[h], erasers_ref[h])))
        local_ref[h] = inner[:, :WIDTH].astype(BF16)
        decayed = jnp.exp(summed[:, h : h + 1]) * query.astype(F32)
        through_ref[h] = (decayed - inner[:, WIDTH:]).astype(BF16)


def prefixes(blocks):
    two = compose(blocks[1], blocks[0])
    return two, compose(blocks[2], two), compose(compose(blocks[3], blocks[2]), two)


def group_kernel(place, own_ref, recv2_ref, recv3_ref, recv1_ref, before_ref, all_ref, pay_ref, pairs):
    part = place[1]
    pairs[part] = own_ref[...]
    for r, ref in ((1, recv1_ref), (2, recv2_ref), (3, recv3_ref)):
        pairs[part ^ r] = joined(load_payload(ref))
    two, three, total = prefixes([parted(pairs[n]) for n in range(4)])
    store_payload(pay_ref, total)
    all_ref[...] = joined(total)
    before_ref[0] = pairs[0]
    before_ref[1] = joined(two)
    before_ref[2] = joined(three)


def fetch_wide_kernel(token_ref, source_ref, fetched_ref, token_out, sem):
    load = pltpu.make_async_copy(source_ref, fetched_ref, sem)
    load.start()
    token_out[...] = token_ref[...]
    load.wait()


def fetch_kernel(
    place, before_row_ref, before_ref, weight_ref, stream_ref, weight_out, stream_out, maps_ref, sems
):
    width = stream_out.shape[1]
    begin = pl.multiple_of(place[2] * width, width)
    loads = [
        pltpu.make_async_copy(weight_ref, weight_out, sems.at[0]),
        pltpu.make_async_copy(stream_ref.at[:, pl.ds(begin, width)], stream_out, sems.at[1]),
    ]
    for load in loads:
        load.start()
    maps_ref[0] = before_row_ref[...]
    for n in range(3):
        maps_ref[n + 1] = joined(compose(parted(before_ref[n]), parted(before_row_ref[...])))
    for load in loads:
        load.wait()


def row_kernel(place, all_ref, recv2_ref, recv1_ref, recv3_ref, before_ref, pay_ref, pairs, starts):
    group = place[3]
    pairs[group] = all_ref[...]
    for d, ref in ((1, recv1_ref), (2, recv2_ref), (3, recv3_ref)):
        pairs[group ^ d] = joined(load_payload(ref))
    two, three, total = prefixes([parted(pairs[n]) for n in range(4)])
    store_payload(pay_ref, total)
    row, column = iotas(WIDTH, 2 * WIDTH)
    starts[0] = (row == column).astype(F32)
    starts[1] = pairs[0]
    starts[2] = joined(two)
    starts[3] = joined(three)
    before_ref[...] = starts[group]


def state_kernel(
    place, recv2_ref, recv1_ref, recv3_ref, maps_ref, mine_ref, out1_ref, out2_ref, out3_ref, rows, states
):
    part, line = place[1], place[4]
    rows[line] = jnp.zeros(rows.shape[1:], F32)
    for r, ref in ((1, recv1_ref), (2, recv2_ref), (3, recv3_ref)):
        rows[line ^ r] = joined(load_payload(ref))
    state = jnp.where(line > 0, rows[0][:, WIDTH:], 0.0)
    for n in (1, 2):
        state = jnp.where(line > n, apply(parted(rows[n]), state), state)
    for n in range(4):
        states[n] = apply(parted(maps_ref[n]), state).astype(BF16)
    mine_ref[...] = states[part]
    for r, ref in ((1, out1_ref), (2, out2_ref), (3, out3_ref)):
        ref[...] = states[part ^ r]


def out_kernel(
    place, local_ref, through_ref, mine_ref, recv2_ref, recv3_ref, recv1_ref, w_ref, term_ref, *refs
):
    part = place[1]
    me = place[2]
    sent_refs, states = refs[:-1], refs[-1]
    groups = local_ref.shape[0]
    states[part] = mine_ref[...]
    for r, ref in ((1, recv1_ref), (2, recv2_ref), (3, recv3_ref)):
        states[part ^ r] = ref[...]
    normed = []
    for h in range(groups):
        result = local_ref[h].astype(F32) + dot(through_ref[h], states[h])
        normed.append(
            (
                result * lax.rsqrt(jnp.mean(result * result, axis=-1, keepdims=True) + 1e-05)
            ).astype(BF16)
        )
    normed = jnp.concatenate(normed, axis=1)
    width = term_ref.shape[1]
    count = len(sent_refs) + 1
    for r in range(count):
        begin = pl.multiple_of((me ^ r) * width, width)
        term = dot(normed, w_ref[:, pl.ds(begin, width)])
        if r == 0:
            term_ref[...] = term
        else:
            sent_refs[r - 1][...] = term.astype(BF16)


def hidden_kernel(stream_ref, term_ref, *refs):
    total = term_ref[...]
    for ref in refs[:-1]:
        total = total + ref[...].astype(F32)
    refs[-1][...] = (stream_ref[...].astype(F32) + total).astype(BF16)


def project_kernel(place, w_ref, *refs):
    me = place[2]
    blocks, (q_ref, kv_ref) = refs[:-2], refs[-2:]
    count = len(blocks)
    rows, width = blocks[0].shape
    values = [ref[...].astype(F32) for ref in blocks]
    squares = sum(jnp.sum(v * v, axis=-1, keepdims=True) for v in values)
    scale = lax.rsqrt(squares / (count * width) + 1e-05)
    total = None
    for n, r in enumerate((0, 2, 1, 3)):
        begin = pl.multiple_of((me ^ r) * width, width)
        part = dot((values[n] * scale).astype(BF16), w_ref[pl.ds(begin, width), :])
        total = part if total is None else total + part
    groups = q_ref.shape[1] // WIDTH
    for h in range(groups):
        base = h * 3 * WIDTH
        span = slice(h * WIDTH, (h + 1) * WIDTH)
        q_ref[:, span] = to_unit(total[:, base : base + WIDTH]).astype(BF16)
        kv_ref[:, span] = to_unit(total[:, base + WIDTH : base + 2 * WIDTH]).astype(BF16)
        kv_ref[:, groups * WIDTH + h * WIDTH : groups * WIDTH + (h + 1) * WIDTH] = total[
            :, base + 2 * WIDTH : base + 3 * WIDTH
        ].astype(BF16)


def window_part(query_place, key_chip, core, q_ref, own_ref, other_ref, sums):
    rows = q_ref.shape[0]
    groups = q_ref.shape[1] // WIDTH
    row, column = iotas(rows, 2 * rows)
    query_place = query_place * rows + row
    own_place = (2 * key_chip + core) * rows + column
    other_place = (2 * key_chip + 1 - core) * rows + column - rows
    key_place = jnp.where(column < rows, own_place, other_place)
    allowed = (key_place <= query_place) & (key_place > query_place - WINDOW) & (key_place >= 0)
    ones = jnp.ones((2 * rows, WIDTH), BF16)
    for h in range(groups):
        span = slice(h * WIDTH, (h + 1) * WIDTH)
        value_span = slice((groups + h) * WIDTH, (groups + h + 1) * WIDTH)
        keys = jnp.concatenate([own_ref[:, span], other_ref[:, span]], axis=0)
        values = jnp.concatenate([own_ref[:, value_span], other_ref[:, value_span]], axis=0)
        scores = SCORE_SCALE * dot(q_ref[:, span], keys, (1, 1))
        weights = jnp.where(allowed, jnp.exp(scores), 0.0).astype(BF16)
        part = dot(weights, jnp.concatenate([values, ones], axis=1))
        sums[h] = part if sums[h] is None else sums[h] + part


def sum_spans(groups):
    return [slice(2 * h * WIDTH, 2 * (h + 1) * WIDTH) for h in range(groups)]


def back_kernel(place, hidden_ref, q_ref, *refs):
    blocks, (back_ref, keep_ref) = refs[:-2], refs[-2:]
    seq = place[0]
    rows = q_ref.shape[0]
    groups = q_ref.shape[1] // WIDTH
    sums = [None] * groups
    for n in range(len(blocks) // 2):
        window_part(
            seq + 4, (seq >> 1) - 1 - n, seq & 1, q_ref, blocks[2 * n], blocks[2 * n + 1], sums
        )
    _, column = iotas(rows, WIDTH)
    totals = jnp.zeros((rows, WIDTH), BF16)
    for h in range(groups):
        back_ref[:, h * WIDTH : (h + 1) * WIDTH] = sums[h][:, :WIDTH].astype(BF16)
        total = sums[h][:, WIDTH:]
        high = total.astype(BF16)
        low = (total - high.astype(F32)).astype(BF16)
        totals = jnp.where(column == 2 * h, high, jnp.where(column == 2 * h + 1, low, totals))
    back_ref[:, groups * WIDTH :] = totals
    keep_ref[...] = hidden_ref[...]


def home_kernel(place, q_ref, *refs):
    blocks, sums_ref = refs[:-1], refs[-1]
    seq = place[0]
    groups = q_ref.shape[1] // WIDTH
    sums = [None] * groups
    for n in range(len(blocks) // 2):
        window_part(
            seq, (seq >> 1) - n, seq & 1, q_ref, blocks[2 * n], blocks[2 * n + 1], sums
        )
    for h, span in enumerate(sum_spans(groups)):
        sums_ref[:, span] = sums[h]


def last_kernel(sums_ref, back_ref, out_ref):
    groups = out_ref.shape[1] // WIDTH
    totals = back_ref[:, groups * WIDTH :].astype(F32)
    for h in range(groups):
        far = totals[:, 2 * h : 2 * h + 1] + totals[:, 2 * h + 1 : 2 * h + 2]
        span = slice(h * WIDTH, (h + 1) * WIDTH)
        mixed = sums_ref[:, 2 * h * WIDTH : (2 * h + 1) * WIDTH] + back_ref[:, span].astype(F32)
        total = sums_ref[:, (2 * h + 1) * WIDTH : (2 * h + 2) * WIDTH] + far
        out_ref[:, span] = (mixed / total).astype(BF16)


def call(kernel, outs, smem=0, scratch=(), spaces=None, limit=LIMIT):
    def run(*args):
        places = [SMEM] * smem + (spaces or [VMEM] * (len(args) - smem))
        return pl.pallas_call(
            kernel,
            out_shape=[jax.ShapeDtypeStruct(shape, kind) for shape, kind in outs],
            in_specs=[pl.BlockSpec(memory_space=place) for place in places],
            out_specs=[pl.BlockSpec(memory_space=VMEM)] * len(outs),
            scratch_shapes=list(scratch),
            compiler_params=pltpu.CompilerParams(vmem_limit_bytes=limit),
        )(*args)

    return run


def moved(array, axis, distance):
    size = lax.axis_size(axis)
    return lax.ppermute(
        array, axis, [(i, i + distance) for i in range(size) if 0 <= i + distance < size]
    )


def crossed(array, mask, axis="seq"):
    return lax.ppermute(array, axis, [(i, i ^ mask) for i in range(lax.axis_size(axis))])


def body(queries, keys, values, gate_log, beta, stream, w_out, w_qkv):
    rows, wide = queries.shape
    groups = gate_log.shape[1]
    seq = lax.axis_index("seq")
    head = lax.axis_index("head")
    heads = lax.axis_size("head")
    place = jnp.stack([seq, seq & 3, head, (seq >> 2) & 3, seq >> 4]).astype(jnp.int32)
    pair_shape = ((WIDTH, 2 * WIDTH), F32)
    pay_shape = ((WIDTH + 16, 2 * WIDTH), BF16)
    state_shape = ((WIDTH, WIDTH), BF16)
    row_shape = ((rows, wide), BF16)
    four_pairs = pltpu.VMEM((4, WIDTH, 2 * WIDTH), F32)
    four_states = pltpu.VMEM((4, WIDTH, WIDTH), BF16)

    gates = jnp.concatenate([gate_log.T, beta.T], axis=0)
    unit_keys, writes, erasers, own, pay1, pay2, pay3 = call(
        map_kernel,
        [row_shape] + [((groups, rows, WIDTH), BF16)] * 2 + [pair_shape] + [pay_shape] * 3,
        1,
        [pltpu.VMEM((rows, wide), BF16)] * 2 + [four_pairs, pltpu.SemaphoreType.DMA((2,))],
        [VMEM] + [pltpu.HBM] * 2,
        CHUNK_LIMIT,
    )(place, gates, keys, values)
    pay2, pay3, pay1 = crossed(pay2, 2), crossed(pay3, 3), crossed(pay1, 1)
    local, through = call(query_kernel, [((groups, rows, WIDTH), BF16)] * 2)(
        gates, queries, unit_keys, writes, erasers
    )
    own, local, through = lax.optimization_barrier((own, local, through))
    before, everything, pay = call(
        group_kernel, [((3, WIDTH, 2 * WIDTH), F32), pair_shape, pay_shape], 1, [four_pairs]
    )(place, own, pay2, pay3, pay1)
    row2, row1, row3 = [crossed(pay, 4 * d) for d in (2, 1, 3)]
    everything, w_qkv = lax.optimization_barrier((everything, w_qkv))
    w_qkv, everything = call(
        fetch_wide_kernel,
        [(w_qkv.shape, BF16), pair_shape],
        0,
        [pltpu.SemaphoreType.DMA],
        [VMEM, pltpu.HBM],
        FETCH_LIMIT,
    )(everything, w_qkv)
    before_row, pay = call(row_kernel, [pair_shape, pay_shape], 1, [four_pairs] * 2)(
        place, everything, row2, row1, row3
    )
    row2, row1, row3 = [crossed(pay, 16 * d) for d in (2, 1, 3)]
    before_row, w_out, stream = lax.optimization_barrier((before_row, w_out, stream))
    w_out, stream, maps = call(
        fetch_kernel,
        [(w_out.shape, BF16), row_shape, ((4, WIDTH, 2 * WIDTH), F32)],
        1,
        [pltpu.SemaphoreType.DMA((2,))],
        [VMEM, VMEM, pltpu.HBM, pltpu.HBM],
        FETCH_LIMIT,
    )(place, before_row, before, w_out, stream)
    mine, out1, out2, out3 = call(state_kernel, [state_shape] * 4, 1, [four_pairs, four_states])(
        place, row2, row1, row3, maps
    )
    terms = call(
        out_kernel,
        [((rows, wide), F32)] + [row_shape] * (heads - 1),
        1,
        [four_states],
    )(
        place,
        local,
        through,
        mine,
        crossed(out2, 2),
        crossed(out3, 3),
        crossed(out1, 1),
        w_out,
    )
    received = [crossed(terms[r], r, "head") for r in (2, 1, 3)]
    (hidden,) = call(hidden_kernel, [row_shape])(stream, terms[0], *received)
    other2, other1, other3 = [crossed(hidden, r, "head") for r in (2, 1, 3)]
    unit_queries, pack = call(project_kernel, [row_shape, ((rows, 2 * wide), BF16)], 1)(
        place, w_qkv, hidden, other2, other1, other3
    )
    first, visitors = lax.optimization_barrier(
        (moved(pack, "seq", 2), moved(unit_queries, "seq", -2))
    )
    second, visitors = lax.optimization_barrier(
        (moved(first, "seq", 2), moved(visitors, "seq", -2))
    )
    home = [
        pack, crossed(pack, 1), first, crossed(first, 1), second, crossed(second, 1)
    ]
    back, kept = call(back_kernel, [((rows, wide + WIDTH), BF16), row_shape], 1)(
        place, hidden, visitors, *home[2:]
    )
    returned = moved(back, "seq", 4)
    (sums,) = call(home_kernel, [((rows, 2 * wide), F32)], 1)(place, unit_queries, *home)
    (attended,) = call(last_kernel, [row_shape])(sums, returned)
    return (kept, attended)


def solution(mesh):
    in_specs = (
        P("seq", "head"),
        P("seq", "head"),
        P("seq", "head"),
        P("seq", "head"),
        P("seq", "head"),
        P("seq", None),
        P("head", None),
        P(None, "head"),
    )
    out_specs = (P("seq", "head"), P("seq", "head"))
    return jax.shard_map(body, mesh=mesh, in_specs=in_specs, out_specs=out_specs, check_vma=False)
```

```python
import functools

import jax
import jax.numpy as jnp
from jax import lax
from jax.experimental import pallas as pl
from jax.experimental.pallas import tpu as pltpu
from jax.sharding import PartitionSpec as P

WINDOW = 1024
WIDTH = 128
SCORE_SCALE = 10.0
F32 = jnp.float32
BF16 = jnp.bfloat16
HIGHEST = lax.Precision.HIGHEST
VMEM = pltpu.VMEM
SMEM = pltpu.SMEM
LIMIT = 16 * 1024 * 1024
FETCH_LIMIT = 44 * 1024 * 1024
CHUNK_LIMIT = 54448 * 1024


def dot(left, right, contract=(1, 0), precision=None):
    return lax.dot_general(
        left,
        right,
        (((contract[0],), (contract[1],)), ((), ())),
        precision=precision,
        preferred_element_type=F32,
    )


def exact(left, right, contract=(1, 0)):
    return dot(left, right, contract, HIGHEST)


def iotas(rows, columns):
    return (
        lax.broadcasted_iota(jnp.int32, (rows, columns), 0),
        lax.broadcasted_iota(jnp.int32, (rows, columns), 1),
    )


def fine(left, right):
    left_high = left.astype(BF16)
    right_high = right.astype(BF16)
    left_low = (left - left_high.astype(F32)).astype(BF16)
    right_low = (right - right_high.astype(F32)).astype(BF16)
    wide = right.shape[1]
    both = dot(left_high, jnp.concatenate([right_high, right_low], axis=1))
    return both[:, :wide] + both[:, wide:] + dot(left_low, right_high)


def split_diagonal(matrix):
    row, column = iotas(WIDTH, WIDTH)
    high = matrix.astype(BF16)
    return high, jnp.where(row == column, matrix - high.astype(F32), 0.0)


def compose(left, right):
    left_t, left_o = left
    right_t, right_o = right
    left_high, left_rest = split_diagonal(left_t)
    right_high, right_rest = split_diagonal(right_t)
    left_column = jnp.sum(left_rest, axis=1, keepdims=True)
    right_row = jnp.sum(right_rest, axis=0, keepdims=True)
    offset = dot(left_high, right_o.astype(BF16)) + left_column * right_o + left_o
    product = dot(left_high, right_high) + left_column * right_t + left_high.astype(F32) * right_row
    return product, offset


def apply(left, state):
    left_t, left_o = left
    left_high, left_rest = split_diagonal(left_t)
    left_column = jnp.sum(left_rest, axis=1, keepdims=True)
    return dot(left_high, state.astype(BF16)) + left_column * state + left_o


def store_payload(ref, pair):
    row, _ = iotas(16, 2 * WIDTH)
    transition, offset = pair
    high, rest = split_diagonal(transition)
    ref[0:WIDTH, 0:WIDTH] = high
    ref[0:WIDTH, WIDTH : 2 * WIDTH] = offset.astype(BF16)
    line = jnp.sum(rest, axis=0, keepdims=True)
    line = jnp.concatenate([line, jnp.zeros_like(line)], axis=1)
    ref[WIDTH : WIDTH + 16, :] = jnp.where(row == 0, line, 0.0).astype(BF16)


def load_payload(ref):
    row, column = iotas(WIDTH, WIDTH)
    line = ref[WIDTH : WIDTH + 16, 0:WIDTH].astype(F32)
    line = jnp.sum(line, axis=0, keepdims=True)
    transition = ref[0:WIDTH, 0:WIDTH].astype(F32)
    transition = transition + jnp.where(row == column, line, 0.0)
    return transition, ref[0:WIDTH, WIDTH : 2 * WIDTH].astype(F32)


def joined(pair):
    return jnp.concatenate(pair, axis=1)


def parted(array):
    return array[:, :WIDTH], array[:, WIDTH:]


def to_unit(vectors):
    return vectors * lax.rsqrt(jnp.sum(vectors * vectors, axis=-1, keepdims=True) + 1e-06)


def lower_inverses(couplings):
    rows = couplings[0].shape[0]
    row, column = iotas(rows, rows)
    identity = (row == column).astype(F32)
    inside = (row >> 3) == (column >> 3)
    powers = [jnp.where(inside, c, 0.0) for c in couplings]
    results = [identity - p for p in powers]
    span = 2
    while span < 8:
        powers = [fine(p, p) for p in powers]
        results = [fine(r, identity + p) for r, p in zip(results, powers)]
        span *= 2
    shift = 3
    while (1 << shift) < rows:
        level = ((row >> (shift + 1)) == (column >> (shift + 1))) & ((row >> shift) > (column >> shift))
        crossing = [fine(r, jnp.where(level, c, 0.0)) for r, c in zip(results, couplings)]
        results = [r - fine(x, r) for r, x in zip(results, crossing)]
        shift += 1
    return results


def decays(gb_ref):
    rows = gb_ref.shape[1]
    groups = gb_ref.shape[0] // 2
    row, column = iotas(rows, rows)
    both = gb_ref[...]
    high = both.astype(BF16)
    rest = both - high.astype(F32)
    middle = rest.astype(BF16)
    low = (rest - middle.astype(F32)).astype(BF16)
    sums = dot(jnp.concatenate([high, middle, low], axis=0), (row <= column).astype(BF16))
    count = 2 * groups
    summed_row = sums[:count] + sums[count : 2 * count] + sums[2 * count :]
    columns = jnp.concatenate([summed_row[:groups], both[groups:]], axis=0).T
    causal = row >= column
    spreads = [columns[:, h : h + 1] - summed_row[h : h + 1, :] for h in range(groups)]
    return columns, [
        jnp.where(causal, jnp.exp(jnp.where(causal, spread, 0.0)), 0.0) for spread in spreads
    ]


def map_kernel(
    place, gb_ref, k_hbm, v_hbm, keys_ref, writes_ref, erasers_ref, own_ref, pay1_ref, pay2_ref, pay3_ref, k_ref, v_ref, pairs, sems
):
    part = place[1]
    rows = gb_ref.shape[1]
    groups = gb_ref.shape[0] // 2
    loads = [
        pltpu.make_async_copy(k_hbm, k_ref, sems.at[0]),
        pltpu.make_async_copy(v_hbm, v_ref, sems.at[1]),
    ]
    for load in loads:
        load.start()
    row, column = iotas(rows, rows)
    summed, decay = decays(gb_ref)
    betas = summed[:, groups:]
    loads[0].wait()
    keys, couplings = [], []
    for h in range(groups):
        span = slice(h * WIDTH, (h + 1) * WIDTH)
        key = to_unit(k_ref[:, span].astype(F32)).astype(BF16)
        keys_ref[:, span] = key
        both = dot(key, key, (1, 1))
        couplings.append(jnp.where(row > column, betas[:, h : h + 1] * decay[h] * both, 0.0))
        keys.append(key.astype(F32))
    inverses = lower_inverses(couplings)
    loads[1].wait()
    for h in range(groups):
        span = slice(h * WIDTH, (h + 1) * WIDTH)
        along = summed[:, h : h + 1]
        last = summed[rows - 1 : rows, h : h + 1]
        beta = betas[:, h : h + 1]
        value = v_ref[:, span].astype(F32)
        made = fine(
            inverses[h],
            jnp.concatenate([beta * value, (beta * jnp.exp(along)) * keys[h]], axis=1),
        ).astype(BF16)
        writes_ref[h], erasers_ref[h] = parted(made)
        ended = (jnp.exp(last - along) * keys[h]).astype(BF16)
        effect = dot(ended, made, (0, 0))
        identity = iotas(WIDTH, WIDTH)
        kept = jnp.where(identity[0] == identity[1], jnp.exp(last), 0.0)
        pairs[h, :, 0:WIDTH] = kept - effect[:, WIDTH:]
        pairs[h, :, WIDTH:] = effect[:, :WIDTH]
    own_ref[...] = pairs[part]
    for r, ref in ((1, pay1_ref), (2, pay2_ref), (3, pay3_ref)):
        store_payload(ref, parted(pairs[part ^ r]))


def query_kernel(gb_ref, q_ref, keys_ref, writes_ref, erasers_ref, local_ref, through_ref):
    groups = gb_ref.shape[0] // 2
    summed, decay = decays(gb_ref)
    for h in range(groups):
        span = slice(h * WIDTH, (h + 1) * WIDTH)
        query = to_unit(q_ref[:, span].astype(F32)).astype(BF16)
        mixing = (dot(query, keys_ref[:, span], (1, 1)) * decay[h]).astype(BF16)
        inner = dot(mixing, joined((writes_ref[h], erasers_ref[h])))
        local_ref[h] = inner[:, :WIDTH].astype(BF16)
        decayed = jnp.exp(summed[:, h : h + 1]) * query.astype(F32)
        through_ref[h] = (decayed - inner[:, WIDTH:]).astype(BF16)


def prefixes(blocks):
    two = compose(blocks[1], blocks[0])
    return two, compose(blocks[2], two), compose(compose(blocks[3], blocks[2]), two)


def group_kernel(place, own_ref, recv2_ref, recv3_ref, recv1_ref, before_ref, all_ref, pay_ref, pairs):
    part = place[1]
    pairs[part] = own_ref[...]
    for r, ref in ((1, recv1_ref), (2, recv2_ref), (3, recv3_ref)):
        pairs[part ^ r] = joined(load_payload(ref))
    two, three, total = prefixes([parted(pairs[n]) for n in range(4)])
    store_payload(pay_ref, total)
    all_ref[...] = joined(total)
    before_ref[0] = pairs[0]
    before_ref[1] = joined(two)
    before_ref[2] = joined(three)


def fetch_wide_kernel(token_ref, source_ref, fetched_ref, token_out, sem):
    load = pltpu.make_async_copy(source_ref, fetched_ref, sem)
    load.start()
    token_out[...] = token_ref[...]
    load.wait()


def fetch_kernel(
    place, before_row_ref, before_ref, weight_ref, stream_ref, weight_out, stream_out, maps_ref, sems
):
    width = stream_out.shape[1]
    begin = pl.multiple_of(place[2] * width, width)
    loads = [
        pltpu.make_async_copy(weight_ref, weight_out, sems.at[0]),
        pltpu.make_async_copy(stream_ref.at[:, pl.ds(begin, width)], stream_out, sems.at[1]),
    ]
    for load in loads:
        load.start()
    maps_ref[0] = before_row_ref[...]
    for n in range(3):
        maps_ref[n + 1] = joined(compose(parted(before_ref[n]), parted(before_row_ref[...])))
    for load in loads:
        load.wait()


def row_kernel(place, all_ref, recv1_ref, recv3_ref, recv2_ref, before_ref, pay_ref, pairs, starts):
    group = place[3]
    pairs[group] = all_ref[...]
    for d, ref in ((1, recv1_ref), (2, recv2_ref), (3, recv3_ref)):
        pairs[group ^ d] = joined(load_payload(ref))
    two, three, total = prefixes([parted(pairs[n]) for n in range(4)])
    store_payload(pay_ref, total)
    row, column = iotas(WIDTH, 2 * WIDTH)
    starts[0] = (row == column).astype(F32)
    starts[1] = pairs[0]
    starts[2] = joined(two)
    starts[3] = joined(three)
    before_ref[...] = starts[group]


def state_kernel(
    place, recv2_ref, recv1_ref, recv3_ref, maps_ref, mine_ref, out1_ref, out2_ref, out3_ref, rows, states
):
    part, line = place[1], place[4]
    rows[line] = jnp.zeros(rows.shape[1:], F32)
    for r, ref in ((1, recv1_ref), (2, recv2_ref), (3, recv3_ref)):
        rows[line ^ r] = joined(load_payload(ref))
    state = jnp.where(line > 0, rows[0][:, WIDTH:], 0.0)
    for n in (1, 2):
        state = jnp.where(line > n, apply(parted(rows[n]), state), state)
    for n in range(4):
        states[n] = apply(parted(maps_ref[n]), state).astype(BF16)
    mine_ref[...] = states[part]
    for r, ref in ((1, out1_ref), (2, out2_ref), (3, out3_ref)):
        ref[...] = states[part ^ r]


def out_kernel(
    place, local_ref, through_ref, mine_ref, recv2_ref, recv3_ref, recv1_ref, w_ref, term_ref, *refs
):
    part = place[1]
    me = place[2]
    sent_refs, states = refs[:-1], refs[-1]
    groups = local_ref.shape[0]
    states[part] = mine_ref[...]
    for r, ref in ((1, recv1_ref), (2, recv2_ref), (3, recv3_ref)):
        states[part ^ r] = ref[...]
    normed = []
    for h in range(groups):
        result = local_ref[h].astype(F32) + dot(through_ref[h], states[h])
        normed.append(
            (
                result * lax.rsqrt(jnp.mean(result * result, axis=-1, keepdims=True) + 1e-05)
            ).astype(BF16)
        )
    normed = jnp.concatenate(normed, axis=1)
    width = term_ref.shape[1]
    count = len(sent_refs) + 1
    for r in range(count):
        begin = pl.multiple_of((me ^ r) * width, width)
        term = dot(normed, w_ref[:, pl.ds(begin, width)])
        if r == 0:
            term_ref[...] = term
        else:
            sent_refs[r - 1][...] = term.astype(BF16)


def hidden_kernel(stream_ref, term_ref, *refs):
    total = term_ref[...]
    for ref in refs[:-1]:
        total = total + ref[...].astype(F32)
    refs[-1][...] = (stream_ref[...].astype(F32) + total).astype(BF16)


def project_kernel(place, w_ref, *refs):
    me = place[2]
    blocks, (q_ref, kv_ref) = refs[:-2], refs[-2:]
    count = len(blocks)
    rows, width = blocks[0].shape
    values = [ref[...].astype(F32) for ref in blocks]
    squares = sum(jnp.sum(v * v, axis=-1, keepdims=True) for v in values)
    scale = lax.rsqrt(squares / (count * width) + 1e-05)
    total = None
    for n, r in enumerate((0, 2, 1, 3)):
        begin = pl.multiple_of((me ^ r) * width, width)
        part = dot((values[n] * scale).astype(BF16), w_ref[pl.ds(begin, width), :])
        total = part if total is None else total + part
    groups = q_ref.shape[1] // WIDTH
    for h in range(groups):
        base = h * 3 * WIDTH
        span = slice(h * WIDTH, (h + 1) * WIDTH)
        q_ref[:, span] = to_unit(total[:, base : base + WIDTH]).astype(BF16)
        kv_ref[:, span] = to_unit(total[:, base + WIDTH : base + 2 * WIDTH]).astype(BF16)
        kv_ref[:, groups * WIDTH + h * WIDTH : groups * WIDTH + (h + 1) * WIDTH] = total[
            :, base + 2 * WIDTH : base + 3 * WIDTH
        ].astype(BF16)


def window_part(query_place, key_chip, core, q_ref, own_ref, other_ref, sums):
    rows = q_ref.shape[0]
    groups = q_ref.shape[1] // WIDTH
    row, column = iotas(rows, 2 * rows)
    query_place = query_place * rows + row
    own_place = (2 * key_chip + core) * rows + column
    other_place = (2 * key_chip + 1 - core) * rows + column - rows
    key_place = jnp.where(column < rows, own_place, other_place)
    allowed = (key_place <= query_place) & (key_place > query_place - WINDOW) & (key_place >= 0)
    ones = jnp.ones((2 * rows, WIDTH), BF16)
    for h in range(groups):
        span = slice(h * WIDTH, (h + 1) * WIDTH)
        value_span = slice((groups + h) * WIDTH, (groups + h + 1) * WIDTH)
        keys = jnp.concatenate([own_ref[:, span], other_ref[:, span]], axis=0)
        values = jnp.concatenate([own_ref[:, value_span], other_ref[:, value_span]], axis=0)
        scores = SCORE_SCALE * dot(q_ref[:, span], keys, (1, 1))
        weights = jnp.where(allowed, jnp.exp(scores), 0.0).astype(BF16)
        part = dot(weights, jnp.concatenate([values, ones], axis=1))
        sums[h] = part if sums[h] is None else sums[h] + part


def sum_spans(groups):
    return [slice(2 * h * WIDTH, 2 * (h + 1) * WIDTH) for h in range(groups)]


def away_kernel(place, hidden_ref, q_ref, own_ref, other_ref, sums_ref, keep_ref):
    seq = place[0]
    groups = q_ref.shape[1] // WIDTH
    sums = [None] * groups
    window_part(seq + 4, (seq >> 1) - 1, seq & 1, q_ref, own_ref, other_ref, sums)
    for h, span in enumerate(sum_spans(groups)):
        sums_ref[:, span] = sums[h]
    keep_ref[...] = hidden_ref[...]


def back_kernel(place, q_ref, sums_ref, own_ref, other_ref, back_ref):
    seq = place[0]
    rows = q_ref.shape[0]
    groups = q_ref.shape[1] // WIDTH
    sums = [sums_ref[:, span] for span in sum_spans(groups)]
    window_part(seq + 4, (seq >> 1) - 2, seq & 1, q_ref, own_ref, other_ref, sums)
    _, column = iotas(rows, WIDTH)
    totals = jnp.zeros((rows, WIDTH), BF16)
    for h in range(groups):
        back_ref[:, h * WIDTH : (h + 1) * WIDTH] = sums[h][:, :WIDTH].astype(BF16)
        total = sums[h][:, WIDTH:]
        high = total.astype(BF16)
        low = (total - high.astype(F32)).astype(BF16)
        totals = jnp.where(column == 2 * h, high, jnp.where(column == 2 * h + 1, low, totals))
    back_ref[:, groups * WIDTH :] = totals


def home_kernel(place, q_ref, *refs):
    blocks, sums_ref = refs[:-1], refs[-1]
    seq = place[0]
    groups = q_ref.shape[1] // WIDTH
    sums = [None] * groups
    for n in range(len(blocks) // 2):
        window_part(
            seq, (seq >> 1) - n, seq & 1, q_ref, blocks[2 * n], blocks[2 * n + 1], sums
        )
    for h, span in enumerate(sum_spans(groups)):
        sums_ref[:, span] = sums[h]


def last_kernel(sums_ref, back_ref, out_ref):
    groups = out_ref.shape[1] // WIDTH
    totals = back_ref[:, groups * WIDTH :].astype(F32)
    for h in range(groups):
        far = totals[:, 2 * h : 2 * h + 1] + totals[:, 2 * h + 1 : 2 * h + 2]
        span = slice(h * WIDTH, (h + 1) * WIDTH)
        mixed = sums_ref[:, 2 * h * WIDTH : (2 * h + 1) * WIDTH] + back_ref[:, span].astype(F32)
        total = sums_ref[:, (2 * h + 1) * WIDTH : (2 * h + 2) * WIDTH] + far
        out_ref[:, span] = (mixed / total).astype(BF16)


def call(kernel, outs, smem=0, scratch=(), spaces=None, limit=LIMIT):
    def run(*args):
        places = [SMEM] * smem + (spaces or [VMEM] * (len(args) - smem))
        return pl.pallas_call(
            kernel,
            out_shape=[jax.ShapeDtypeStruct(shape, kind) for shape, kind in outs],
            in_specs=[pl.BlockSpec(memory_space=place) for place in places],
            out_specs=[pl.BlockSpec(memory_space=VMEM)] * len(outs),
            scratch_shapes=list(scratch),
            compiler_params=pltpu.CompilerParams(vmem_limit_bytes=limit),
        )(*args)

    return run


def moved(array, axis, distance):
    size = lax.axis_size(axis)
    return lax.ppermute(
        array, axis, [(i, i + distance) for i in range(size) if 0 <= i + distance < size]
    )


def crossed(array, mask, axis="seq"):
    return lax.ppermute(array, axis, [(i, i ^ mask) for i in range(lax.axis_size(axis))])


def body(queries, keys, values, gate_log, beta, stream, w_out, w_qkv):
    rows, wide = queries.shape
    groups = gate_log.shape[1]
    seq = lax.axis_index("seq")
    head = lax.axis_index("head")
    heads = lax.axis_size("head")
    place = jnp.stack([seq, seq & 3, head, (seq >> 2) & 3, seq >> 4]).astype(jnp.int32)
    pair_shape = ((WIDTH, 2 * WIDTH), F32)
    pay_shape = ((WIDTH + 16, 2 * WIDTH), BF16)
    state_shape = ((WIDTH, WIDTH), BF16)
    row_shape = ((rows, wide), BF16)
    four_pairs = pltpu.VMEM((4, WIDTH, 2 * WIDTH), F32)
    four_states = pltpu.VMEM((4, WIDTH, WIDTH), BF16)

    gates = jnp.concatenate([gate_log.T, beta.T], axis=0)
    unit_keys, writes, erasers, own, pay1, pay2, pay3 = call(
        map_kernel,
        [row_shape] + [((groups, rows, WIDTH), BF16)] * 2 + [pair_shape] + [pay_shape] * 3,
        1,
        [pltpu.VMEM((rows, wide), BF16)] * 2 + [four_pairs, pltpu.SemaphoreType.DMA((2,))],
        [VMEM] + [pltpu.HBM] * 2,
        CHUNK_LIMIT,
    )(place, gates, keys, values)
    pay2, pay3, pay1 = crossed(pay2, 2), crossed(pay3, 3), crossed(pay1, 1)
    local, through = call(query_kernel, [((groups, rows, WIDTH), BF16)] * 2)(
        gates, queries, unit_keys, writes, erasers
    )
    own, local, through = lax.optimization_barrier((own, local, through))
    before, everything, pay = call(
        group_kernel, [((3, WIDTH, 2 * WIDTH), F32), pair_shape, pay_shape], 1, [four_pairs]
    )(place, own, pay2, pay3, pay1)
    row1, row3, row2 = [crossed(pay, 4 * d) for d in (1, 3, 2)]
    everything, w_qkv = lax.optimization_barrier((everything, w_qkv))
    w_qkv, everything = call(
        fetch_wide_kernel,
        [(w_qkv.shape, BF16), pair_shape],
        0,
        [pltpu.SemaphoreType.DMA],
        [VMEM, pltpu.HBM],
        FETCH_LIMIT,
    )(everything, w_qkv)
    before_row, pay = call(row_kernel, [pair_shape, pay_shape], 1, [four_pairs] * 2)(
        place, everything, row1, row3, row2
    )
    row2, row1, row3 = [crossed(pay, 16 * d) for d in (2, 1, 3)]
    before_row, w_out, stream = lax.optimization_barrier((before_row, w_out, stream))
    w_out, stream, maps = call(
        fetch_kernel,
        [(w_out.shape, BF16), row_shape, ((4, WIDTH, 2 * WIDTH), F32)],
        1,
        [pltpu.SemaphoreType.DMA((2,))],
        [VMEM, VMEM, pltpu.HBM, pltpu.HBM],
        FETCH_LIMIT,
    )(place, before_row, before, w_out, stream)
    mine, out1, out2, out3 = call(state_kernel, [state_shape] * 4, 1, [four_pairs, four_states])(
        place, row2, row1, row3, maps
    )
    terms = call(
        out_kernel,
        [((rows, wide), F32)] + [row_shape] * (heads - 1),
        1,
        [four_states],
    )(
        place,
        local,
        through,
        mine,
        crossed(out2, 2),
        crossed(out3, 3),
        crossed(out1, 1),
        w_out,
    )
    received = [crossed(terms[r], r, "head") for r in (2, 1, 3)]
    (hidden,) = call(hidden_kernel, [row_shape])(stream, terms[0], *received)
    other2, other1, other3 = [crossed(hidden, r, "head") for r in (2, 1, 3)]
    unit_queries, pack = call(project_kernel, [row_shape, ((rows, 2 * wide), BF16)], 1)(
        place, w_qkv, hidden, other2, other1, other3
    )
    first, visitors = lax.optimization_barrier(
        (moved(pack, "seq", 2), moved(unit_queries, "seq", -2))
    )
    second, visitors = lax.optimization_barrier(
        (moved(first, "seq", 2), moved(visitors, "seq", -2))
    )
    home = [
        pack, crossed(pack, 1), first, crossed(first, 1), second, crossed(second, 1)
    ]
    sums_shape = ((rows, 2 * wide), F32)
    away, kept = call(away_kernel, [sums_shape, row_shape], 1)(
        place, hidden, visitors, home[2], home[3]
    )
    (back,) = call(back_kernel, [((rows, wide + WIDTH), BF16)], 1)(
        place, visitors, away, home[4], home[5]
    )
    returned = moved(back, "seq", 4)
    (sums,) = call(home_kernel, [((rows, 2 * wide), F32)], 1)(place, unit_queries, *home)
    (attended,) = call(last_kernel, [row_shape])(sums, returned)
    return (kept, attended)


def solution(mesh):
    in_specs = (
        P("seq", "head"),
        P("seq", "head"),
        P("seq", "head"),
        P("seq", "head"),
        P("seq", "head"),
        P("seq", None),
        P("head", None),
        P(None, "head"),
    )
    out_specs = (P("seq", "head"), P("seq", "head"))
    return jax.shard_map(body, mesh=mesh, in_specs=in_specs, out_specs=out_specs, check_vma=False)
```

```python
import functools

import jax
import jax.numpy as jnp
from jax import lax
from jax.experimental import pallas as pl
from jax.experimental.pallas import tpu as pltpu
from jax.sharding import PartitionSpec as P

WINDOW = 1024
WIDTH = 128
SCORE_SCALE = 10.0
F32 = jnp.float32
BF16 = jnp.bfloat16
HIGHEST = lax.Precision.HIGHEST
VMEM = pltpu.VMEM
SMEM = pltpu.SMEM
LIMIT = 16 * 1024 * 1024
FETCH_LIMIT = 44 * 1024 * 1024
CHUNK_LIMIT = 54448 * 1024


def dot(left, right, contract=(1, 0), precision=None):
    return lax.dot_general(
        left,
        right,
        (((contract[0],), (contract[1],)), ((), ())),
        precision=precision,
        preferred_element_type=F32,
    )


def exact(left, right, contract=(1, 0)):
    return dot(left, right, contract, HIGHEST)


def iotas(rows, columns):
    return (
        lax.broadcasted_iota(jnp.int32, (rows, columns), 0),
        lax.broadcasted_iota(jnp.int32, (rows, columns), 1),
    )


def fine(left, right):
    left_high = left.astype(BF16)
    right_high = right.astype(BF16)
    left_low = (left - left_high.astype(F32)).astype(BF16)
    right_low = (right - right_high.astype(F32)).astype(BF16)
    wide = right.shape[1]
    both = dot(left_high, jnp.concatenate([right_high, right_low], axis=1))
    return both[:, :wide] + both[:, wide:] + dot(left_low, right_high)


def split_diagonal(matrix):
    row, column = iotas(WIDTH, WIDTH)
    high = matrix.astype(BF16)
    return high, jnp.where(row == column, matrix - high.astype(F32), 0.0)


def compose(left, right):
    left_t, left_o = left
    right_t, right_o = right
    left_high, left_rest = split_diagonal(left_t)
    right_high, right_rest = split_diagonal(right_t)
    left_column = jnp.sum(left_rest, axis=1, keepdims=True)
    right_row = jnp.sum(right_rest, axis=0, keepdims=True)
    offset = dot(left_high, right_o.astype(BF16)) + left_column * right_o + left_o
    product = dot(left_high, right_high) + left_column * right_t + left_high.astype(F32) * right_row
    return product, offset


def apply(left, state):
    left_t, left_o = left
    left_high, left_rest = split_diagonal(left_t)
    left_column = jnp.sum(left_rest, axis=1, keepdims=True)
    return dot(left_high, state.astype(BF16)) + left_column * state + left_o


def store_payload(ref, pair):
    row, _ = iotas(16, 2 * WIDTH)
    transition, offset = pair
    high, rest = split_diagonal(transition)
    ref[0:WIDTH, 0:WIDTH] = high
    ref[0:WIDTH, WIDTH : 2 * WIDTH] = offset.astype(BF16)
    line = jnp.sum(rest, axis=0, keepdims=True)
    line = jnp.concatenate([line, jnp.zeros_like(line)], axis=1)
    ref[WIDTH : WIDTH + 16, :] = jnp.where(row == 0, line, 0.0).astype(BF16)


def load_payload(ref):
    row, column = iotas(WIDTH, WIDTH)
    line = ref[WIDTH : WIDTH + 16, 0:WIDTH].astype(F32)
    line = jnp.sum(line, axis=0, keepdims=True)
    transition = ref[0:WIDTH, 0:WIDTH].astype(F32)
    transition = transition + jnp.where(row == column, line, 0.0)
    return transition, ref[0:WIDTH, WIDTH : 2 * WIDTH].astype(F32)


def joined(pair):
    return jnp.concatenate(pair, axis=1)


def parted(array):
    return array[:, :WIDTH], array[:, WIDTH:]


def to_unit(vectors):
    return vectors * lax.rsqrt(jnp.sum(vectors * vectors, axis=-1, keepdims=True) + 1e-06)


def lower_inverses(couplings):
    rows = couplings[0].shape[0]
    row, column = iotas(rows, rows)
    identity = (row == column).astype(F32)
    inside = (row >> 3) == (column >> 3)
    powers = [jnp.where(inside, c, 0.0) for c in couplings]
    results = [identity - p for p in powers]
    span = 2
    while span < 8:
        powers = [fine(p, p) for p in powers]
        results = [fine(r, identity + p) for r, p in zip(results, powers)]
        span *= 2
    shift = 3
    while (1 << shift) < rows:
        level = ((row >> (shift + 1)) == (column >> (shift + 1))) & ((row >> shift) > (column >> shift))
        crossing = [fine(r, jnp.where(level, c, 0.0)) for r, c in zip(results, couplings)]
        results = [r - fine(x, r) for r, x in zip(results, crossing)]
        shift += 1
    return results


def decays(gb_ref):
    rows = gb_ref.shape[1]
    groups = gb_ref.shape[0] // 2
    row, column = iotas(rows, rows)
    both = gb_ref[...]
    high = both.astype(BF16)
    rest = both - high.astype(F32)
    middle = rest.astype(BF16)
    low = (rest - middle.astype(F32)).astype(BF16)
    sums = dot(jnp.concatenate([high, middle, low], axis=0), (row <= column).astype(BF16))
    count = 2 * groups
    summed_row = sums[:count] + sums[count : 2 * count] + sums[2 * count :]
    columns = jnp.concatenate([summed_row[:groups], both[groups:]], axis=0).T
    causal = row >= column
    spreads = [columns[:, h : h + 1] - summed_row[h : h + 1, :] for h in range(groups)]
    return columns, [
        jnp.where(causal, jnp.exp(jnp.where(causal, spread, 0.0)), 0.0) for spread in spreads
    ]


def map_kernel(
    place, gb_ref, k_hbm, v_hbm, keys_ref, writes_ref, erasers_ref, own_ref, pay1_ref, pay2_ref, pay3_ref, k_ref, v_ref, pairs, sems
):
    part = place[1]
    rows = gb_ref.shape[1]
    groups = gb_ref.shape[0] // 2
    loads = [
        pltpu.make_async_copy(k_hbm, k_ref, sems.at[0]),
        pltpu.make_async_copy(v_hbm, v_ref, sems.at[1]),
    ]
    for load in loads:
        load.start()
    row, column = iotas(rows, rows)
    summed, decay = decays(gb_ref)
    betas = summed[:, groups:]
    loads[0].wait()
    keys, couplings = [], []
    for h in range(groups):
        span = slice(h * WIDTH, (h + 1) * WIDTH)
        key = to_unit(k_ref[:, span].astype(F32)).astype(BF16)
        keys_ref[:, span] = key
        both = dot(key, key, (1, 1))
        couplings.append(jnp.where(row > column, betas[:, h : h + 1] * decay[h] * both, 0.0))
        keys.append(key.astype(F32))
    inverses = lower_inverses(couplings)
    loads[1].wait()
    for h in range(groups):
        span = slice(h * WIDTH, (h + 1) * WIDTH)
        along = summed[:, h : h + 1]
        last = summed[rows - 1 : rows, h : h + 1]
        beta = betas[:, h : h + 1]
        value = v_ref[:, span].astype(F32)
        made = fine(
            inverses[h],
            jnp.concatenate([beta * value, (beta * jnp.exp(along)) * keys[h]], axis=1),
        ).astype(BF16)
        writes_ref[h], erasers_ref[h] = parted(made)
        ended = (jnp.exp(last - along) * keys[h]).astype(BF16)
        effect = dot(ended, made, (0, 0))
        identity = iotas(WIDTH, WIDTH)
        kept = jnp.where(identity[0] == identity[1], jnp.exp(last), 0.0)
        pairs[h, :, 0:WIDTH] = kept - effect[:, WIDTH:]
        pairs[h, :, WIDTH:] = effect[:, :WIDTH]
    own_ref[...] = pairs[part]
    for r, ref in ((1, pay1_ref), (2, pay2_ref), (3, pay3_ref)):
        store_payload(ref, parted(pairs[part ^ r]))


def query_kernel(gb_ref, q_ref, keys_ref, writes_ref, erasers_ref, local_ref, through_ref):
    groups = gb_ref.shape[0] // 2
    summed, decay = decays(gb_ref)
    for h in range(groups):
        span = slice(h * WIDTH, (h + 1) * WIDTH)
        query = to_unit(q_ref[:, span].astype(F32)).astype(BF16)
        mixing = (dot(query, keys_ref[:, span], (1, 1)) * decay[h]).astype(BF16)
        inner = dot(mixing, joined((writes_ref[h], erasers_ref[h])))
        local_ref[h] = inner[:, :WIDTH].astype(BF16)
        decayed = jnp.exp(summed[:, h : h + 1]) * query.astype(F32)
        through_ref[h] = (decayed - inner[:, WIDTH:]).astype(BF16)


def prefixes(blocks):
    two = compose(blocks[1], blocks[0])
    return two, compose(blocks[2], two), compose(compose(blocks[3], blocks[2]), two)


def group_kernel(place, own_ref, recv2_ref, recv3_ref, recv1_ref, before_ref, all_ref, pay_ref, pairs):
    part = place[1]
    pairs[part] = own_ref[...]
    for r, ref in ((1, recv1_ref), (2, recv2_ref), (3, recv3_ref)):
        pairs[part ^ r] = joined(load_payload(ref))
    two, three, total = prefixes([parted(pairs[n]) for n in range(4)])
    store_payload(pay_ref, total)
    all_ref[...] = joined(total)
    before_ref[0] = pairs[0]
    before_ref[1] = joined(two)
    before_ref[2] = joined(three)


def fetch_wide_kernel(token_ref, source_ref, fetched_ref, token_out, sem):
    load = pltpu.make_async_copy(source_ref, fetched_ref, sem)
    load.start()
    token_out[...] = token_ref[...]
    load.wait()


def fetch_kernel(
    place, before_row_ref, before_ref, weight_ref, stream_ref, weight_out, stream_out, maps_ref, sems
):
    width = stream_out.shape[1]
    begin = pl.multiple_of(place[2] * width, width)
    loads = [
        pltpu.make_async_copy(weight_ref, weight_out, sems.at[0]),
        pltpu.make_async_copy(stream_ref.at[:, pl.ds(begin, width)], stream_out, sems.at[1]),
    ]
    for load in loads:
        load.start()
    maps_ref[0] = before_row_ref[...]
    for n in range(3):
        maps_ref[n + 1] = joined(compose(parted(before_ref[n]), parted(before_row_ref[...])))
    for load in loads:
        load.wait()


def row_kernel(place, all_ref, recv1_ref, recv3_ref, recv2_ref, before_ref, pay_ref, pairs, starts):
    group = place[3]
    pairs[group] = all_ref[...]
    for d, ref in ((1, recv1_ref), (2, recv2_ref), (3, recv3_ref)):
        pairs[group ^ d] = joined(load_payload(ref))
    two, three, total = prefixes([parted(pairs[n]) for n in range(4)])
    store_payload(pay_ref, total)
    row, column = iotas(WIDTH, 2 * WIDTH)
    starts[0] = (row == column).astype(F32)
    starts[1] = pairs[0]
    starts[2] = joined(two)
    starts[3] = joined(three)
    before_ref[...] = starts[group]


def state_kernel(
    place, recv2_ref, recv1_ref, recv3_ref, maps_ref, mine_ref, out1_ref, out2_ref, out3_ref, rows, states
):
    part, line = place[1], place[4]
    rows[line] = jnp.zeros(rows.shape[1:], F32)
    for r, ref in ((1, recv1_ref), (2, recv2_ref), (3, recv3_ref)):
        rows[line ^ r] = joined(load_payload(ref))
    state = jnp.where(line > 0, rows[0][:, WIDTH:], 0.0)
    for n in (1, 2):
        state = jnp.where(line > n, apply(parted(rows[n]), state), state)
    for n in range(4):
        states[n] = apply(parted(maps_ref[n]), state).astype(BF16)
    mine_ref[...] = states[part]
    for r, ref in ((1, out1_ref), (2, out2_ref), (3, out3_ref)):
        ref[...] = states[part ^ r]


def out_kernel(
    place, local_ref, through_ref, mine_ref, recv2_ref, recv3_ref, recv1_ref, w_ref, term_ref, *refs
):
    part = place[1]
    me = place[2]
    sent_refs, states = refs[:-1], refs[-1]
    groups = local_ref.shape[0]
    states[part] = mine_ref[...]
    for r, ref in ((1, recv1_ref), (2, recv2_ref), (3, recv3_ref)):
        states[part ^ r] = ref[...]
    normed = []
    for h in range(groups):
        result = local_ref[h].astype(F32) + dot(through_ref[h], states[h])
        normed.append(
            (
                result * lax.rsqrt(jnp.mean(result * result, axis=-1, keepdims=True) + 1e-05)
            ).astype(BF16)
        )
    normed = jnp.concatenate(normed, axis=1)
    width = term_ref.shape[1]
    count = len(sent_refs) + 1
    for r in range(count):
        begin = pl.multiple_of((me ^ r) * width, width)
        term = dot(normed, w_ref[:, pl.ds(begin, width)])
        if r == 0:
            term_ref[...] = term
        else:
            sent_refs[r - 1][...] = term.astype(BF16)


def hidden_kernel(stream_ref, term_ref, *refs):
    total = term_ref[...]
    for ref in refs[:-1]:
        total = total + ref[...].astype(F32)
    refs[-1][...] = (stream_ref[...].astype(F32) + total).astype(BF16)


def own_kernel(place, hidden_ref, w_ref, part_ref):
    width = hidden_ref.shape[1]
    begin = pl.multiple_of(place[2] * width, width)
    part_ref[...] = dot(hidden_ref[...], w_ref[pl.ds(begin, width), :])


def product_of(place, w_ref, blocks, first, size):
    me = place[2]
    width = blocks[0].shape[1]
    total = None
    for block, r in zip(blocks, (2, 1, 3)):
        begin = pl.multiple_of((me ^ r) * width, width)
        part = dot(block[...], w_ref[pl.ds(begin, width), first : first + size])
        total = part if total is None else total + part
    return total


def pair_kernel(place, w_ref, part_ref, hidden_ref, block2_ref, block1_ref, block3_ref, kv_ref, scale_ref):
    blocks = [block2_ref, block1_ref, block3_ref]
    squares = 0.0
    for ref in [hidden_ref] + blocks:
        value = ref[...].astype(F32)
        squares = squares + jnp.sum(value * value, axis=-1, keepdims=True)
    rows, width = hidden_ref.shape
    scale = lax.rsqrt(squares / (4 * width) + 1e-05)
    scale_ref[...] = jnp.broadcast_to(scale, scale_ref.shape)
    groups = width // WIDTH
    for h in range(groups):
        begin = (3 * h + 1) * WIDTH
        total = part_ref[:, begin : begin + 2 * WIDTH] + product_of(place, w_ref, blocks, begin, 2 * WIDTH)
        total = total * scale
        kv_ref[:, h * WIDTH : (h + 1) * WIDTH] = to_unit(total[:, :WIDTH]).astype(BF16)
        kv_ref[:, (groups + h) * WIDTH : (groups + h + 1) * WIDTH] = total[:, WIDTH:].astype(BF16)


def unit_kernel(place, w_ref, part_ref, scale_ref, block2_ref, block1_ref, block3_ref, q_ref):
    blocks = [block2_ref, block1_ref, block3_ref]
    for h in range(q_ref.shape[1] // WIDTH):
        begin = 3 * h * WIDTH
        total = part_ref[:, begin : begin + WIDTH] + product_of(place, w_ref, blocks, begin, WIDTH)
        q_ref[:, h * WIDTH : (h + 1) * WIDTH] = to_unit(total * scale_ref[...]).astype(BF16)


def window_part(query_place, key_chip, core, q_ref, own_ref, other_ref, sums):
    rows = q_ref.shape[0]
    groups = q_ref.shape[1] // WIDTH
    row, column = iotas(rows, 2 * rows)
    query_place = query_place * rows + row
    own_place = (2 * key_chip + core) * rows + column
    other_place = (2 * key_chip + 1 - core) * rows + column - rows
    key_place = jnp.where(column < rows, own_place, other_place)
    allowed = (key_place <= query_place) & (key_place > query_place - WINDOW) & (key_place >= 0)
    ones = jnp.ones((2 * rows, WIDTH), BF16)
    for h in range(groups):
        span = slice(h * WIDTH, (h + 1) * WIDTH)
        value_span = slice((groups + h) * WIDTH, (groups + h + 1) * WIDTH)
        keys = jnp.concatenate([own_ref[:, span], other_ref[:, span]], axis=0)
        values = jnp.concatenate([own_ref[:, value_span], other_ref[:, value_span]], axis=0)
        scores = SCORE_SCALE * dot(q_ref[:, span], keys, (1, 1))
        weights = jnp.where(allowed, jnp.exp(scores), 0.0).astype(BF16)
        part = dot(weights, jnp.concatenate([values, ones], axis=1))
        sums[h] = part if sums[h] is None else sums[h] + part


def sum_spans(groups):
    return [slice(2 * h * WIDTH, 2 * (h + 1) * WIDTH) for h in range(groups)]


def away_kernel(place, hidden_ref, q_ref, own_ref, other_ref, sums_ref, keep_ref):
    seq = place[0]
    groups = q_ref.shape[1] // WIDTH
    sums = [None] * groups
    window_part(seq + 4, (seq >> 1) - 1, seq & 1, q_ref, own_ref, other_ref, sums)
    for h, span in enumerate(sum_spans(groups)):
        sums_ref[:, span] = sums[h]
    keep_ref[...] = hidden_ref[...]


def back_kernel(place, q_ref, sums_ref, own_ref, other_ref, back_ref):
    seq = place[0]
    rows = q_ref.shape[0]
    groups = q_ref.shape[1] // WIDTH
    sums = [sums_ref[:, span] for span in sum_spans(groups)]
    window_part(seq + 4, (seq >> 1) - 2, seq & 1, q_ref, own_ref, other_ref, sums)
    row, column = iotas(rows, WIDTH)
    line, _ = iotas(16, WIDTH)
    for h in range(groups):
        span = slice(h * WIDTH, (h + 1) * WIDTH)
        back_ref[0:rows, span] = sums[h][:, :WIDTH].astype(BF16)
        total = jnp.sum(jnp.where(row == column, sums[h][:, WIDTH:], 0.0), axis=0, keepdims=True)
        high = total.astype(BF16).astype(F32)
        totals = jnp.where(line == 0, high, jnp.where(line == 1, total - high, 0.0))
        back_ref[rows : rows + 16, span] = totals.astype(BF16)


def home_kernel(place, q_ref, *refs):
    blocks, sums_ref = refs[:-1], refs[-1]
    seq = place[0]
    groups = q_ref.shape[1] // WIDTH
    sums = [None] * groups
    for n in range(len(blocks) // 2):
        window_part(
            seq, (seq >> 1) - n, seq & 1, q_ref, blocks[2 * n], blocks[2 * n + 1], sums
        )
    for h, span in enumerate(sum_spans(groups)):
        sums_ref[:, span] = sums[h]


def last_kernel(sums_ref, back_ref, out_ref):
    groups = out_ref.shape[1] // WIDTH
    rows = out_ref.shape[0]
    row, column = iotas(rows, WIDTH)
    for h in range(groups):
        span = slice(h * WIDTH, (h + 1) * WIDTH)
        line = jnp.sum(back_ref[rows : rows + 16, span].astype(F32), axis=0, keepdims=True)
        far = jnp.sum(jnp.where(row == column, line, 0.0), axis=1, keepdims=True)
        mixed = sums_ref[:, 2 * h * WIDTH : (2 * h + 1) * WIDTH] + back_ref[0:rows, span].astype(F32)
        total = sums_ref[:, (2 * h + 1) * WIDTH : (2 * h + 2) * WIDTH] + far
        out_ref[:, span] = (mixed / total).astype(BF16)


def call(kernel, outs, smem=0, scratch=(), spaces=None, limit=LIMIT):
    def run(*args):
        places = [SMEM] * smem + (spaces or [VMEM] * (len(args) - smem))
        return pl.pallas_call(
            kernel,
            out_shape=[jax.ShapeDtypeStruct(shape, kind) for shape, kind in outs],
            in_specs=[pl.BlockSpec(memory_space=place) for place in places],
            out_specs=[pl.BlockSpec(memory_space=VMEM)] * len(outs),
            scratch_shapes=list(scratch),
            compiler_params=pltpu.CompilerParams(vmem_limit_bytes=limit),
        )(*args)

    return run


def moved(array, axis, distance):
    size = lax.axis_size(axis)
    return lax.ppermute(
        array, axis, [(i, i + distance) for i in range(size) if 0 <= i + distance < size]
    )


def crossed(array, mask, axis="seq"):
    return lax.ppermute(array, axis, [(i, i ^ mask) for i in range(lax.axis_size(axis))])


def body(queries, keys, values, gate_log, beta, stream, w_out, w_qkv):
    rows, wide = queries.shape
    groups = gate_log.shape[1]
    seq = lax.axis_index("seq")
    head = lax.axis_index("head")
    heads = lax.axis_size("head")
    place = jnp.stack([seq, seq & 3, head, (seq >> 2) & 3, seq >> 4]).astype(jnp.int32)
    pair_shape = ((WIDTH, 2 * WIDTH), F32)
    pay_shape = ((WIDTH + 16, 2 * WIDTH), BF16)
    state_shape = ((WIDTH, WIDTH), BF16)
    row_shape = ((rows, wide), BF16)
    four_pairs = pltpu.VMEM((4, WIDTH, 2 * WIDTH), F32)
    four_states = pltpu.VMEM((4, WIDTH, WIDTH), BF16)

    gates = jnp.concatenate([gate_log.T, beta.T], axis=0)
    unit_keys, writes, erasers, own, pay1, pay2, pay3 = call(
        map_kernel,
        [row_shape] + [((groups, rows, WIDTH), BF16)] * 2 + [pair_shape] + [pay_shape] * 3,
        1,
        [pltpu.VMEM((rows, wide), BF16)] * 2 + [four_pairs, pltpu.SemaphoreType.DMA((2,))],
        [VMEM] + [pltpu.HBM] * 2,
        CHUNK_LIMIT,
    )(place, gates, keys, values)
    pay2, pay3, pay1 = crossed(pay2, 2), crossed(pay3, 3), crossed(pay1, 1)
    local, through = call(query_kernel, [((groups, rows, WIDTH), BF16)] * 2)(
        gates, queries, unit_keys, writes, erasers
    )
    own, local, through = lax.optimization_barrier((own, local, through))
    before, everything, pay = call(
        group_kernel, [((3, WIDTH, 2 * WIDTH), F32), pair_shape, pay_shape], 1, [four_pairs]
    )(place, own, pay2, pay3, pay1)
    row1, row3, row2 = [crossed(pay, 4 * d) for d in (1, 3, 2)]
    everything, w_qkv = lax.optimization_barrier((everything, w_qkv))
    w_qkv, everything = call(
        fetch_wide_kernel,
        [(w_qkv.shape, BF16), pair_shape],
        0,
        [pltpu.SemaphoreType.DMA],
        [VMEM, pltpu.HBM],
        FETCH_LIMIT,
    )(everything, w_qkv)
    before_row, pay = call(row_kernel, [pair_shape, pay_shape], 1, [four_pairs] * 2)(
        place, everything, row1, row3, row2
    )
    row2, row1, row3 = [crossed(pay, 16 * d) for d in (2, 1, 3)]
    before_row, w_out, stream = lax.optimization_barrier((before_row, w_out, stream))
    w_out, stream, maps = call(
        fetch_kernel,
        [(w_out.shape, BF16), row_shape, ((4, WIDTH, 2 * WIDTH), F32)],
        1,
        [pltpu.SemaphoreType.DMA((2,))],
        [VMEM, VMEM, pltpu.HBM, pltpu.HBM],
        FETCH_LIMIT,
    )(place, before_row, before, w_out, stream)
    mine, out1, out2, out3 = call(state_kernel, [state_shape] * 4, 1, [four_pairs, four_states])(
        place, row2, row1, row3, maps
    )
    terms = call(
        out_kernel,
        [((rows, wide), F32)] + [row_shape] * (heads - 1),
        1,
        [four_states],
    )(
        place,
        local,
        through,
        mine,
        crossed(out2, 2),
        crossed(out3, 3),
        crossed(out1, 1),
        w_out,
    )
    received = [crossed(terms[r], r, "head") for r in (2, 1, 3)]
    (hidden,) = call(hidden_kernel, [row_shape])(stream, terms[0], *received)
    other2, other1, other3 = [crossed(hidden, r, "head") for r in (2, 1, 3)]
    (part,) = call(own_kernel, [((rows, w_qkv.shape[1]), F32)], 1)(place, hidden, w_qkv)
    others = (other2, other1, other3)
    pack, scale = call(pair_kernel, [((rows, 2 * wide), BF16), ((rows, WIDTH), F32)], 1)(
        place, w_qkv, part, hidden, *others
    )
    (unit_queries,) = call(unit_kernel, [row_shape], 1)(place, w_qkv, part, scale, *others)
    first, visitors = lax.optimization_barrier(
        (moved(pack, "seq", 2), moved(unit_queries, "seq", -2))
    )
    second, visitors = lax.optimization_barrier(
        (moved(first, "seq", 2), moved(visitors, "seq", -2))
    )
    home = [
        pack, crossed(pack, 1), first, crossed(first, 1), second, crossed(second, 1)
    ]
    sums_shape = ((rows, 2 * wide), F32)
    away, kept = call(away_kernel, [sums_shape, row_shape], 1)(
        place, hidden, visitors, home[2], home[3]
    )
    (back,) = call(back_kernel, [((rows + 16, wide), BF16)], 1)(
        place, visitors, away, home[4], home[5]
    )
    returned = moved(back, "seq", 4)
    (sums,) = call(home_kernel, [((rows, 2 * wide), F32)], 1)(place, unit_queries, *home)
    (attended,) = call(last_kernel, [row_shape])(sums, returned)
    return (kept, attended)


def solution(mesh):
    in_specs = (
        P("seq", "head"),
        P("seq", "head"),
        P("seq", "head"),
        P("seq", "head"),
        P("seq", "head"),
        P("seq", None),
        P("head", None),
        P(None, "head"),
    )
    out_specs = (P("seq", "head"), P("seq", "head"))
    return jax.shard_map(body, mesh=mesh, in_specs=in_specs, out_specs=out_specs, check_vma=False)
```

```python
import functools

import jax
import jax.numpy as jnp
from jax import lax
from jax.experimental import pallas as pl
from jax.experimental.pallas import tpu as pltpu
from jax.sharding import PartitionSpec as P

WINDOW = 1024
WIDTH = 128
SCORE_SCALE = 10.0
F32 = jnp.float32
BF16 = jnp.bfloat16
HIGHEST = lax.Precision.HIGHEST
VMEM = pltpu.VMEM
SMEM = pltpu.SMEM
LIMIT = 16 * 1024 * 1024
FETCH_LIMIT = 44 * 1024 * 1024
CHUNK_LIMIT = 54448 * 1024


def dot(left, right, contract=(1, 0), precision=None):
    return lax.dot_general(
        left,
        right,
        (((contract[0],), (contract[1],)), ((), ())),
        precision=precision,
        preferred_element_type=F32,
    )


def exact(left, right, contract=(1, 0)):
    return dot(left, right, contract, HIGHEST)


def iotas(rows, columns):
    return (
        lax.broadcasted_iota(jnp.int32, (rows, columns), 0),
        lax.broadcasted_iota(jnp.int32, (rows, columns), 1),
    )


def fine(left, right):
    left_high = left.astype(BF16)
    right_high = right.astype(BF16)
    left_low = (left - left_high.astype(F32)).astype(BF16)
    right_low = (right - right_high.astype(F32)).astype(BF16)
    wide = right.shape[1]
    both = dot(left_high, jnp.concatenate([right_high, right_low], axis=1))
    return both[:, :wide] + both[:, wide:] + dot(left_low, right_high)


def split_diagonal(matrix):
    row, column = iotas(WIDTH, WIDTH)
    high = matrix.astype(BF16)
    return high, jnp.where(row == column, matrix - high.astype(F32), 0.0)


def compose(left, right):
    left_t, left_o = left
    right_t, right_o = right
    left_high, left_rest = split_diagonal(left_t)
    right_high, right_rest = split_diagonal(right_t)
    left_column = jnp.sum(left_rest, axis=1, keepdims=True)
    right_row = jnp.sum(right_rest, axis=0, keepdims=True)
    offset = dot(left_high, right_o.astype(BF16)) + left_column * right_o + left_o
    product = dot(left_high, right_high) + left_column * right_t + left_high.astype(F32) * right_row
    return product, offset


def apply(left, state):
    left_t, left_o = left
    left_high, left_rest = split_diagonal(left_t)
    left_column = jnp.sum(left_rest, axis=1, keepdims=True)
    return dot(left_high, state.astype(BF16)) + left_column * state + left_o


def store_payload(ref, pair):
    row, _ = iotas(16, 2 * WIDTH)
    transition, offset = pair
    high, rest = split_diagonal(transition)
    ref[0:WIDTH, 0:WIDTH] = high
    ref[0:WIDTH, WIDTH : 2 * WIDTH] = offset.astype(BF16)
    line = jnp.sum(rest, axis=0, keepdims=True)
    line = jnp.concatenate([line, jnp.zeros_like(line)], axis=1)
    ref[WIDTH : WIDTH + 16, :] = jnp.where(row == 0, line, 0.0).astype(BF16)


def load_payload(ref):
    row, column = iotas(WIDTH, WIDTH)
    line = ref[WIDTH : WIDTH + 16, 0:WIDTH].astype(F32)
    line = jnp.sum(line, axis=0, keepdims=True)
    transition = ref[0:WIDTH, 0:WIDTH].astype(F32)
    transition = transition + jnp.where(row == column, line, 0.0)
    return transition, ref[0:WIDTH, WIDTH : 2 * WIDTH].astype(F32)


def joined(pair):
    return jnp.concatenate(pair, axis=1)


def parted(array):
    return array[:, :WIDTH], array[:, WIDTH:]


def to_unit(vectors):
    return vectors * lax.rsqrt(jnp.sum(vectors * vectors, axis=-1, keepdims=True) + 1e-06)


def lower_inverses(couplings):
    rows = couplings[0].shape[0]
    row, column = iotas(rows, rows)
    identity = (row == column).astype(F32)
    inside = (row >> 3) == (column >> 3)
    powers = [jnp.where(inside, c, 0.0) for c in couplings]
    results = [identity - p for p in powers]
    span = 2
    while span < 8:
        powers = [fine(p, p) for p in powers]
        results = [fine(r, identity + p) for r, p in zip(results, powers)]
        span *= 2
    shift = 3
    while (1 << shift) < rows:
        level = ((row >> (shift + 1)) == (column >> (shift + 1))) & ((row >> shift) > (column >> shift))
        crossing = [fine(r, jnp.where(level, c, 0.0)) for r, c in zip(results, couplings)]
        results = [r - fine(x, r) for r, x in zip(results, crossing)]
        shift += 1
    return results


def decays(gb_ref):
    rows = gb_ref.shape[1]
    groups = gb_ref.shape[0] // 2
    row, column = iotas(rows, rows)
    both = gb_ref[...]
    high = both.astype(BF16)
    rest = both - high.astype(F32)
    middle = rest.astype(BF16)
    low = (rest - middle.astype(F32)).astype(BF16)
    sums = dot(jnp.concatenate([high, middle, low], axis=0), (row <= column).astype(BF16))
    count = 2 * groups
    summed_row = sums[:count] + sums[count : 2 * count] + sums[2 * count :]
    columns = jnp.concatenate([summed_row[:groups], both[groups:]], axis=0).T
    causal = row >= column
    spreads = [columns[:, h : h + 1] - summed_row[h : h + 1, :] for h in range(groups)]
    return columns, [
        jnp.where(causal, jnp.exp(jnp.where(causal, spread, 0.0)), 0.0) for spread in spreads
    ]


def map_kernel(
    place, gb_ref, k_hbm, v_hbm, keys_ref, writes_ref, erasers_ref, own_ref, pay1_ref, pay2_ref, pay3_ref, k_ref, v_ref, pairs, sems
):
    part = place[1]
    rows = gb_ref.shape[1]
    groups = gb_ref.shape[0] // 2
    loads = [
        pltpu.make_async_copy(k_hbm, k_ref, sems.at[0]),
        pltpu.make_async_copy(v_hbm, v_ref, sems.at[1]),
    ]
    for load in loads:
        load.start()
    row, column = iotas(rows, rows)
    summed, decay = decays(gb_ref)
    betas = summed[:, groups:]
    loads[0].wait()
    keys, couplings = [], []
    for h in range(groups):
        span = slice(h * WIDTH, (h + 1) * WIDTH)
        key = to_unit(k_ref[:, span].astype(F32)).astype(BF16)
        keys_ref[:, span] = key
        both = dot(key, key, (1, 1))
        couplings.append(jnp.where(row > column, betas[:, h : h + 1] * decay[h] * both, 0.0))
        keys.append(key.astype(F32))
    inverses = lower_inverses(couplings)
    loads[1].wait()
    for h in range(groups):
        span = slice(h * WIDTH, (h + 1) * WIDTH)
        along = summed[:, h : h + 1]
        last = summed[rows - 1 : rows, h : h + 1]
        beta = betas[:, h : h + 1]
        value = v_ref[:, span].astype(F32)
        made = fine(
            inverses[h],
            jnp.concatenate([beta * value, (beta * jnp.exp(along)) * keys[h]], axis=1),
        ).astype(BF16)
        writes_ref[h], erasers_ref[h] = parted(made)
        ended = (jnp.exp(last - along) * keys[h]).astype(BF16)
        effect = dot(ended, made, (0, 0))
        identity = iotas(WIDTH, WIDTH)
        kept = jnp.where(identity[0] == identity[1], jnp.exp(last), 0.0)
        pairs[h, :, 0:WIDTH] = kept - effect[:, WIDTH:]
        pairs[h, :, WIDTH:] = effect[:, :WIDTH]
    own_ref[...] = pairs[part]
    for r, ref in ((1, pay1_ref), (2, pay2_ref), (3, pay3_ref)):
        store_payload(ref, parted(pairs[part ^ r]))


def query_kernel(gb_ref, q_ref, keys_ref, writes_ref, erasers_ref, local_ref, through_ref):
    groups = gb_ref.shape[0] // 2
    summed, decay = decays(gb_ref)
    for h in range(groups):
        span = slice(h * WIDTH, (h + 1) * WIDTH)
        query = to_unit(q_ref[:, span].astype(F32)).astype(BF16)
        mixing = (dot(query, keys_ref[:, span], (1, 1)) * decay[h]).astype(BF16)
        inner = dot(mixing, joined((writes_ref[h], erasers_ref[h])))
        local_ref[h] = inner[:, :WIDTH].astype(BF16)
        decayed = jnp.exp(summed[:, h : h + 1]) * query.astype(F32)
        through_ref[h] = (decayed - inner[:, WIDTH:]).astype(BF16)


def prefixes(blocks):
    two = compose(blocks[1], blocks[0])
    return two, compose(blocks[2], two), compose(compose(blocks[3], blocks[2]), two)


def group_kernel(place, own_ref, recv2_ref, recv3_ref, recv1_ref, before_ref, all_ref, pay_ref, pairs):
    part = place[1]
    pairs[part] = own_ref[...]
    for r, ref in ((1, recv1_ref), (2, recv2_ref), (3, recv3_ref)):
        pairs[part ^ r] = joined(load_payload(ref))
    two, three, total = prefixes([parted(pairs[n]) for n in range(4)])
    store_payload(pay_ref, total)
    all_ref[...] = joined(total)
    before_ref[0] = pairs[0]
    before_ref[1] = joined(two)
    before_ref[2] = joined(three)


def fetch_wide_kernel(token_ref, source_ref, fetched_ref, token_out, sem):
    load = pltpu.make_async_copy(source_ref, fetched_ref, sem)
    load.start()
    token_out[...] = token_ref[...]
    load.wait()


def fetch_kernel(
    place, before_row_ref, before_ref, weight_ref, stream_ref, weight_out, stream_out, maps_ref, sems
):
    width = stream_out.shape[1]
    begin = pl.multiple_of(place[2] * width, width)
    loads = [
        pltpu.make_async_copy(weight_ref, weight_out, sems.at[0]),
        pltpu.make_async_copy(stream_ref.at[:, pl.ds(begin, width)], stream_out, sems.at[1]),
    ]
    for load in loads:
        load.start()
    maps_ref[0] = before_row_ref[...]
    for n in range(3):
        maps_ref[n + 1] = joined(compose(parted(before_ref[n]), parted(before_row_ref[...])))
    for load in loads:
        load.wait()


def row_kernel(place, all_ref, recv2_ref, recv1_ref, recv3_ref, before_ref, pay_ref, pairs, starts):
    group = place[3]
    pairs[group] = all_ref[...]
    for d, ref in ((1, recv1_ref), (2, recv2_ref), (3, recv3_ref)):
        pairs[group ^ d] = joined(load_payload(ref))
    two, three, total = prefixes([parted(pairs[n]) for n in range(4)])
    store_payload(pay_ref, total)
    row, column = iotas(WIDTH, 2 * WIDTH)
    starts[0] = (row == column).astype(F32)
    starts[1] = pairs[0]
    starts[2] = joined(two)
    starts[3] = joined(three)
    before_ref[...] = starts[group]


def state_kernel(
    place, recv2_ref, recv1_ref, recv3_ref, maps_ref, mine_ref, out1_ref, out2_ref, out3_ref, rows, states
):
    part, line = place[1], place[4]
    rows[line] = jnp.zeros(rows.shape[1:], F32)
    for r, ref in ((1, recv1_ref), (2, recv2_ref), (3, recv3_ref)):
        rows[line ^ r] = joined(load_payload(ref))
    state = jnp.where(line > 0, rows[0][:, WIDTH:], 0.0)
    for n in (1, 2):
        state = jnp.where(line > n, apply(parted(rows[n]), state), state)
    for n in range(4):
        states[n] = apply(parted(maps_ref[n]), state).astype(BF16)
    mine_ref[...] = states[part]
    for r, ref in ((1, out1_ref), (2, out2_ref), (3, out3_ref)):
        ref[...] = states[part ^ r]


def out_kernel(
    place, local_ref, through_ref, mine_ref, recv2_ref, recv3_ref, recv1_ref, w_ref, term_ref, *refs
):
    part = place[1]
    me = place[2]
    sent_refs, states = refs[:-1], refs[-1]
    groups = local_ref.shape[0]
    states[part] = mine_ref[...]
    for r, ref in ((1, recv1_ref), (2, recv2_ref), (3, recv3_ref)):
        states[part ^ r] = ref[...]
    normed = []
    for h in range(groups):
        result = local_ref[h].astype(F32) + dot(through_ref[h], states[h])
        normed.append(
            (
                result * lax.rsqrt(jnp.mean(result * result, axis=-1, keepdims=True) + 1e-05)
            ).astype(BF16)
        )
    normed = jnp.concatenate(normed, axis=1)
    width = term_ref.shape[1]
    count = len(sent_refs) + 1
    for r in range(count):
        begin = pl.multiple_of((me ^ r) * width, width)
        term = dot(normed, w_ref[:, pl.ds(begin, width)])
        if r == 0:
            term_ref[...] = term
        else:
            sent_refs[r - 1][...] = term.astype(BF16)


def hidden_kernel(stream_ref, term_ref, *refs):
    total = term_ref[...]
    for ref in refs[:-1]:
        total = total + ref[...].astype(F32)
    refs[-1][...] = (stream_ref[...].astype(F32) + total).astype(BF16)


def own_kernel(place, hidden_ref, w_ref, part_ref):
    width = hidden_ref.shape[1]
    begin = pl.multiple_of(place[2] * width, width)
    part_ref[...] = dot(hidden_ref[...], w_ref[pl.ds(begin, width), :])


def project_kernel(place, w_ref, part_ref, hidden_ref, block2_ref, block1_ref, block3_ref, q_ref, kv_ref):
    me = place[2]
    blocks = [block2_ref, block1_ref, block3_ref]
    rows, width = hidden_ref.shape
    total = part_ref[...]
    for block, r in zip(blocks, (2, 1, 3)):
        begin = pl.multiple_of((me ^ r) * width, width)
        total = total + dot(block[...], w_ref[pl.ds(begin, width), :])
    squares = 0.0
    for ref in [hidden_ref] + blocks:
        value = ref[...].astype(F32)
        squares = squares + jnp.sum(value * value, axis=-1, keepdims=True)
    total = total * lax.rsqrt(squares / (4 * width) + 1e-05)
    groups = width // WIDTH
    for h in range(groups):
        base = h * 3 * WIDTH
        span = slice(h * WIDTH, (h + 1) * WIDTH)
        q_ref[:, span] = to_unit(total[:, base : base + WIDTH]).astype(BF16)
        kv_ref[:, span] = to_unit(total[:, base + WIDTH : base + 2 * WIDTH]).astype(BF16)
        kv_ref[:, (groups + h) * WIDTH : (groups + h + 1) * WIDTH] = total[
            :, base + 2 * WIDTH : base + 3 * WIDTH
        ].astype(BF16)


def window_part(query_place, key_chip, core, q_ref, own_ref, other_ref, sums):
    rows = q_ref.shape[0]
    groups = q_ref.shape[1] // WIDTH
    row, column = iotas(rows, 2 * rows)
    query_place = query_place * rows + row
    own_place = (2 * key_chip + core) * rows + column
    other_place = (2 * key_chip + 1 - core) * rows + column - rows
    key_place = jnp.where(column < rows, own_place, other_place)
    allowed = (key_place <= query_place) & (key_place > query_place - WINDOW) & (key_place >= 0)
    ones = jnp.ones((2 * rows, WIDTH), BF16)
    for h in range(groups):
        span = slice(h * WIDTH, (h + 1) * WIDTH)
        value_span = slice((groups + h) * WIDTH, (groups + h + 1) * WIDTH)
        keys = jnp.concatenate([own_ref[:, span], other_ref[:, span]], axis=0)
        values = jnp.concatenate([own_ref[:, value_span], other_ref[:, value_span]], axis=0)
        scores = SCORE_SCALE * dot(q_ref[:, span], keys, (1, 1))
        weights = jnp.where(allowed, jnp.exp(scores), 0.0).astype(BF16)
        part = dot(weights, jnp.concatenate([values, ones], axis=1))
        sums[h] = part if sums[h] is None else sums[h] + part


def sum_spans(groups):
    return [slice(2 * h * WIDTH, 2 * (h + 1) * WIDTH) for h in range(groups)]


def away_kernel(place, hidden_ref, q_ref, own_ref, other_ref, sums_ref, keep_ref):
    seq = place[0]
    groups = q_ref.shape[1] // WIDTH
    sums = [None] * groups
    window_part(seq + 4, (seq >> 1) - 1, seq & 1, q_ref, own_ref, other_ref, sums)
    for h, span in enumerate(sum_spans(groups)):
        sums_ref[:, span] = sums[h]
    keep_ref[...] = hidden_ref[...]


def back_kernel(place, q_ref, sums_ref, own_ref, other_ref, back_ref):
    seq = place[0]
    rows = q_ref.shape[0]
    groups = q_ref.shape[1] // WIDTH
    sums = [sums_ref[:, span] for span in sum_spans(groups)]
    window_part(seq + 4, (seq >> 1) - 2, seq & 1, q_ref, own_ref, other_ref, sums)
    row, column = iotas(rows, WIDTH)
    line, _ = iotas(16, WIDTH)
    for h in range(groups):
        span = slice(h * WIDTH, (h + 1) * WIDTH)
        back_ref[0:rows, span] = sums[h][:, :WIDTH].astype(BF16)
        total = jnp.sum(jnp.where(row == column, sums[h][:, WIDTH:], 0.0), axis=0, keepdims=True)
        high = total.astype(BF16).astype(F32)
        totals = jnp.where(line == 0, high, jnp.where(line == 1, total - high, 0.0))
        back_ref[rows : rows + 16, span] = totals.astype(BF16)


def home_kernel(place, q_ref, *refs):
    blocks, sums_ref = refs[:-1], refs[-1]
    seq = place[0]
    groups = q_ref.shape[1] // WIDTH
    sums = [None] * groups
    for n in range(len(blocks) // 2):
        window_part(
            seq, (seq >> 1) - n, seq & 1, q_ref, blocks[2 * n], blocks[2 * n + 1], sums
        )
    for h, span in enumerate(sum_spans(groups)):
        sums_ref[:, span] = sums[h]


def last_kernel(sums_ref, back_ref, out_ref):
    groups = out_ref.shape[1] // WIDTH
    rows = out_ref.shape[0]
    row, column = iotas(rows, WIDTH)
    for h in range(groups):
        span = slice(h * WIDTH, (h + 1) * WIDTH)
        line = jnp.sum(back_ref[rows : rows + 16, span].astype(F32), axis=0, keepdims=True)
        far = jnp.sum(jnp.where(row == column, line, 0.0), axis=1, keepdims=True)
        mixed = sums_ref[:, 2 * h * WIDTH : (2 * h + 1) * WIDTH] + back_ref[0:rows, span].astype(F32)
        total = sums_ref[:, (2 * h + 1) * WIDTH : (2 * h + 2) * WIDTH] + far
        out_ref[:, span] = (mixed / total).astype(BF16)


def call(kernel, outs, smem=0, scratch=(), spaces=None, limit=LIMIT):
    def run(*args):
        places = [SMEM] * smem + (spaces or [VMEM] * (len(args) - smem))
        return pl.pallas_call(
            kernel,
            out_shape=[jax.ShapeDtypeStruct(shape, kind) for shape, kind in outs],
            in_specs=[pl.BlockSpec(memory_space=place) for place in places],
            out_specs=[pl.BlockSpec(memory_space=VMEM)] * len(outs),
            scratch_shapes=list(scratch),
            compiler_params=pltpu.CompilerParams(vmem_limit_bytes=limit),
        )(*args)

    return run


def moved(array, axis, distance):
    size = lax.axis_size(axis)
    return lax.ppermute(
        array, axis, [(i, i + distance) for i in range(size) if 0 <= i + distance < size]
    )


def crossed(array, mask, axis="seq"):
    return lax.ppermute(array, axis, [(i, i ^ mask) for i in range(lax.axis_size(axis))])


def body(queries, keys, values, gate_log, beta, stream, w_out, w_qkv):
    rows, wide = queries.shape
    groups = gate_log.shape[1]
    seq = lax.axis_index("seq")
    head = lax.axis_index("head")
    heads = lax.axis_size("head")
    place = jnp.stack([seq, seq & 3, head, (seq >> 2) & 3, seq >> 4]).astype(jnp.int32)
    pair_shape = ((WIDTH, 2 * WIDTH), F32)
    pay_shape = ((WIDTH + 16, 2 * WIDTH), BF16)
    state_shape = ((WIDTH, WIDTH), BF16)
    row_shape = ((rows, wide), BF16)
    four_pairs = pltpu.VMEM((4, WIDTH, 2 * WIDTH), F32)
    four_states = pltpu.VMEM((4, WIDTH, WIDTH), BF16)

    gates = jnp.concatenate([gate_log.T, beta.T], axis=0)
    unit_keys, writes, erasers, own, pay1, pay2, pay3 = call(
        map_kernel,
        [row_shape] + [((groups, rows, WIDTH), BF16)] * 2 + [pair_shape] + [pay_shape] * 3,
        1,
        [pltpu.VMEM((rows, wide), BF16)] * 2 + [four_pairs, pltpu.SemaphoreType.DMA((2,))],
        [VMEM] + [pltpu.HBM] * 2,
        CHUNK_LIMIT,
    )(place, gates, keys, values)
    pay2, pay3, pay1 = crossed(pay2, 2), crossed(pay3, 3), crossed(pay1, 1)
    local, through = call(query_kernel, [((groups, rows, WIDTH), BF16)] * 2)(
        gates, queries, unit_keys, writes, erasers
    )
    own, local, through = lax.optimization_barrier((own, local, through))
    before, everything, pay = call(
        group_kernel, [((3, WIDTH, 2 * WIDTH), F32), pair_shape, pay_shape], 1, [four_pairs]
    )(place, own, pay2, pay3, pay1)
    row2, row1, row3 = [crossed(pay, 4 * d) for d in (2, 1, 3)]
    everything, w_qkv = lax.optimization_barrier((everything, w_qkv))
    w_qkv, everything = call(
        fetch_wide_kernel,
        [(w_qkv.shape, BF16), pair_shape],
        0,
        [pltpu.SemaphoreType.DMA],
        [VMEM, pltpu.HBM],
        FETCH_LIMIT,
    )(everything, w_qkv)
    before_row, pay = call(row_kernel, [pair_shape, pay_shape], 1, [four_pairs] * 2)(
        place, everything, row2, row1, row3
    )
    row2, row1, row3 = [crossed(pay, 16 * d) for d in (2, 1, 3)]
    before_row, w_out, stream = lax.optimization_barrier((before_row, w_out, stream))
    w_out, stream, maps = call(
        fetch_kernel,
        [(w_out.shape, BF16), row_shape, ((4, WIDTH, 2 * WIDTH), F32)],
        1,
        [pltpu.SemaphoreType.DMA((2,))],
        [VMEM, VMEM, pltpu.HBM, pltpu.HBM],
        FETCH_LIMIT,
    )(place, before_row, before, w_out, stream)
    mine, out1, out2, out3 = call(state_kernel, [state_shape] * 4, 1, [four_pairs, four_states])(
        place, row2, row1, row3, maps
    )
    terms = call(
        out_kernel,
        [((rows, wide), F32)] + [row_shape] * (heads - 1),
        1,
        [four_states],
    )(
        place,
        local,
        through,
        mine,
        crossed(out2, 2),
        crossed(out3, 3),
        crossed(out1, 1),
        w_out,
    )
    received = [crossed(terms[r], r, "head") for r in (2, 1, 3)]
    (hidden,) = call(hidden_kernel, [row_shape])(stream, terms[0], *received)
    other2, other1, other3 = [crossed(hidden, r, "head") for r in (2, 1, 3)]
    (part,) = call(own_kernel, [((rows, w_qkv.shape[1]), F32)], 1)(place, hidden, w_qkv)
    unit_queries, pack = call(project_kernel, [row_shape, ((rows, 2 * wide), BF16)], 1)(
        place, w_qkv, part, hidden, other2, other1, other3
    )
    first, visitors = lax.optimization_barrier(
        (moved(pack, "seq", 2), moved(unit_queries, "seq", -2))
    )
    second, visitors = lax.optimization_barrier(
        (moved(first, "seq", 2), moved(visitors, "seq", -2))
    )
    home = [
        pack, crossed(pack, 1), first, crossed(first, 1), second, crossed(second, 1)
    ]
    sums_shape = ((rows, 2 * wide), F32)
    away, kept = call(away_kernel, [sums_shape, row_shape], 1)(
        place, hidden, visitors, home[2], home[3]
    )
    (back,) = call(back_kernel, [((rows + 16, wide), BF16)], 1)(
        place, visitors, away, home[4], home[5]
    )
    returned = moved(back, "seq", 4)
    (sums,) = call(home_kernel, [((rows, 2 * wide), F32)], 1)(place, unit_queries, *home)
    (attended,) = call(last_kernel, [row_shape])(sums, returned)
    return (kept, attended)


def solution(mesh):
    in_specs = (
        P("seq", "head"),
        P("seq", "head"),
        P("seq", "head"),
        P("seq", "head"),
        P("seq", "head"),
        P("seq", None),
        P("head", None),
        P(None, "head"),
    )
    out_specs = (P("seq", "head"), P("seq", "head"))
    return jax.shard_map(body, mesh=mesh, in_specs=in_specs, out_specs=out_specs, check_vma=False)
```

```python
import functools

import jax
import jax.numpy as jnp
from jax import lax
from jax.experimental import pallas as pl
from jax.experimental.pallas import tpu as pltpu
from jax.sharding import PartitionSpec as P

WINDOW = 1024
WIDTH = 128
SCORE_SCALE = 10.0
F32 = jnp.float32
BF16 = jnp.bfloat16
HIGHEST = lax.Precision.HIGHEST
VMEM = pltpu.VMEM
SMEM = pltpu.SMEM
LIMIT = 16 * 1024 * 1024
FETCH_LIMIT = 44 * 1024 * 1024
CHUNK_LIMIT = 54448 * 1024


def dot(left, right, contract=(1, 0), precision=None):
    return lax.dot_general(
        left,
        right,
        (((contract[0],), (contract[1],)), ((), ())),
        precision=precision,
        preferred_element_type=F32,
    )


def exact(left, right, contract=(1, 0)):
    return dot(left, right, contract, HIGHEST)


def iotas(rows, columns):
    return (
        lax.broadcasted_iota(jnp.int32, (rows, columns), 0),
        lax.broadcasted_iota(jnp.int32, (rows, columns), 1),
    )


def fine(left, right):
    left_high = left.astype(BF16)
    right_high = right.astype(BF16)
    left_low = (left - left_high.astype(F32)).astype(BF16)
    right_low = (right - right_high.astype(F32)).astype(BF16)
    wide = right.shape[1]
    both = dot(left_high, jnp.concatenate([right_high, right_low], axis=1))
    return both[:, :wide] + both[:, wide:] + dot(left_low, right_high)


def split_diagonal(matrix):
    row, column = iotas(WIDTH, WIDTH)
    high = matrix.astype(BF16)
    return high, jnp.where(row == column, matrix - high.astype(F32), 0.0)


def compose(left, right):
    left_t, left_o = left
    right_t, right_o = right
    left_high, left_rest = split_diagonal(left_t)
    right_high, right_rest = split_diagonal(right_t)
    left_column = jnp.sum(left_rest, axis=1, keepdims=True)
    right_row = jnp.sum(right_rest, axis=0, keepdims=True)
    offset = dot(left_high, right_o.astype(BF16)) + left_column * right_o + left_o
    product = dot(left_high, right_high) + left_column * right_t + left_high.astype(F32) * right_row
    return product, offset


def apply(left, state):
    left_t, left_o = left
    left_high, left_rest = split_diagonal(left_t)
    left_column = jnp.sum(left_rest, axis=1, keepdims=True)
    return dot(left_high, state.astype(BF16)) + left_column * state + left_o


def store_payload(ref, pair):
    row, _ = iotas(16, 2 * WIDTH)
    transition, offset = pair
    high, rest = split_diagonal(transition)
    ref[0:WIDTH, 0:WIDTH] = high
    ref[0:WIDTH, WIDTH : 2 * WIDTH] = offset.astype(BF16)
    line = jnp.sum(rest, axis=0, keepdims=True)
    line = jnp.concatenate([line, jnp.zeros_like(line)], axis=1)
    ref[WIDTH : WIDTH + 16, :] = jnp.where(row == 0, line, 0.0).astype(BF16)


def load_payload(ref):
    row, column = iotas(WIDTH, WIDTH)
    line = ref[WIDTH : WIDTH + 16, 0:WIDTH].astype(F32)
    line = jnp.sum(line, axis=0, keepdims=True)
    transition = ref[0:WIDTH, 0:WIDTH].astype(F32)
    transition = transition + jnp.where(row == column, line, 0.0)
    return transition, ref[0:WIDTH, WIDTH : 2 * WIDTH].astype(F32)


def joined(pair):
    return jnp.concatenate(pair, axis=1)


def parted(array):
    return array[:, :WIDTH], array[:, WIDTH:]


def to_unit(vectors):
    return vectors * lax.rsqrt(jnp.sum(vectors * vectors, axis=-1, keepdims=True) + 1e-06)


def lower_inverses(couplings):
    rows = couplings[0].shape[0]
    row, column = iotas(rows, rows)
    identity = (row == column).astype(F32)
    inside = (row >> 3) == (column >> 3)
    powers = [jnp.where(inside, c, 0.0) for c in couplings]
    results = [identity - p for p in powers]
    span = 2
    while span < 8:
        powers = [fine(p, p) for p in powers]
        results = [fine(r, identity + p) for r, p in zip(results, powers)]
        span *= 2
    shift = 3
    while (1 << shift) < rows:
        level = ((row >> (shift + 1)) == (column >> (shift + 1))) & ((row >> shift) > (column >> shift))
        crossing = [fine(r, jnp.where(level, c, 0.0)) for r, c in zip(results, couplings)]
        results = [r - fine(x, r) for r, x in zip(results, crossing)]
        shift += 1
    return results


def decays(gb_ref):
    rows = gb_ref.shape[1]
    groups = gb_ref.shape[0] // 2
    row, column = iotas(rows, rows)
    both = gb_ref[...]
    high = both.astype(BF16)
    rest = both - high.astype(F32)
    middle = rest.astype(BF16)
    low = (rest - middle.astype(F32)).astype(BF16)
    sums = dot(jnp.concatenate([high, middle, low], axis=0), (row <= column).astype(BF16))
    count = 2 * groups
    summed_row = sums[:count] + sums[count : 2 * count] + sums[2 * count :]
    columns = jnp.concatenate([summed_row[:groups], both[groups:]], axis=0).T
    causal = row >= column
    spreads = [columns[:, h : h + 1] - summed_row[h : h + 1, :] for h in range(groups)]
    return columns, [
        jnp.where(causal, jnp.exp(jnp.where(causal, spread, 0.0)), 0.0) for spread in spreads
    ]


def map_kernel(
    place, gb_ref, k_hbm, v_hbm, keys_ref, writes_ref, erasers_ref, own_ref, pay1_ref, pay2_ref, pay3_ref, k_ref, v_ref, pairs, sems
):
    part = place[1]
    rows = gb_ref.shape[1]
    groups = gb_ref.shape[0] // 2
    loads = [
        pltpu.make_async_copy(k_hbm, k_ref, sems.at[0]),
        pltpu.make_async_copy(v_hbm, v_ref, sems.at[1]),
    ]
    for load in loads:
        load.start()
    row, column = iotas(rows, rows)
    summed, decay = decays(gb_ref)
    betas = summed[:, groups:]
    loads[0].wait()
    keys, couplings = [], []
    for h in range(groups):
        span = slice(h * WIDTH, (h + 1) * WIDTH)
        key = to_unit(k_ref[:, span].astype(F32)).astype(BF16)
        keys_ref[:, span] = key
        both = dot(key, key, (1, 1))
        couplings.append(jnp.where(row > column, betas[:, h : h + 1] * decay[h] * both, 0.0))
        keys.append(key.astype(F32))
    inverses = lower_inverses(couplings)
    loads[1].wait()
    for h in range(groups):
        span = slice(h * WIDTH, (h + 1) * WIDTH)
        along = summed[:, h : h + 1]
        last = summed[rows - 1 : rows, h : h + 1]
        beta = betas[:, h : h + 1]
        value = v_ref[:, span].astype(F32)
        made = fine(
            inverses[h],
            jnp.concatenate([beta * value, (beta * jnp.exp(along)) * keys[h]], axis=1),
        ).astype(BF16)
        writes_ref[h], erasers_ref[h] = parted(made)
        ended = (jnp.exp(last - along) * keys[h]).astype(BF16)
        effect = dot(ended, made, (0, 0))
        identity = iotas(WIDTH, WIDTH)
        kept = jnp.where(identity[0] == identity[1], jnp.exp(last), 0.0)
        pairs[h, :, 0:WIDTH] = kept - effect[:, WIDTH:]
        pairs[h, :, WIDTH:] = effect[:, :WIDTH]
    own_ref[...] = pairs[part]
    for r, ref in ((1, pay1_ref), (2, pay2_ref), (3, pay3_ref)):
        store_payload(ref, parted(pairs[part ^ r]))


def query_kernel(gb_ref, q_ref, keys_ref, writes_ref, erasers_ref, local_ref, through_ref):
    groups = gb_ref.shape[0] // 2
    summed, decay = decays(gb_ref)
    for h in range(groups):
        span = slice(h * WIDTH, (h + 1) * WIDTH)
        query = to_unit(q_ref[:, span].astype(F32)).astype(BF16)
        mixing = (dot(query, keys_ref[:, span], (1, 1)) * decay[h]).astype(BF16)
        inner = dot(mixing, joined((writes_ref[h], erasers_ref[h])))
        local_ref[h] = inner[:, :WIDTH].astype(BF16)
        decayed = jnp.exp(summed[:, h : h + 1]) * query.astype(F32)
        through_ref[h] = (decayed - inner[:, WIDTH:]).astype(BF16)


def prefixes(blocks):
    two = compose(blocks[1], blocks[0])
    return two, compose(blocks[2], two), compose(compose(blocks[3], blocks[2]), two)


def group_kernel(place, own_ref, recv2_ref, recv3_ref, recv1_ref, before_ref, all_ref, pay_ref, pairs):
    part = place[1]
    pairs[part] = own_ref[...]
    for r, ref in ((1, recv1_ref), (2, recv2_ref), (3, recv3_ref)):
        pairs[part ^ r] = joined(load_payload(ref))
    two, three, total = prefixes([parted(pairs[n]) for n in range(4)])
    store_payload(pay_ref, total)
    all_ref[...] = joined(total)
    before_ref[0] = pairs[0]
    before_ref[1] = joined(two)
    before_ref[2] = joined(three)


def fetch_wide_kernel(token_ref, source_ref, fetched_ref, token_out, sem):
    load = pltpu.make_async_copy(source_ref, fetched_ref, sem)
    load.start()
    token_out[...] = token_ref[...]
    load.wait()


def fetch_kernel(
    place, before_row_ref, before_ref, weight_ref, stream_ref, weight_out, stream_out, maps_ref, sems
):
    width = stream_out.shape[1]
    begin = pl.multiple_of(place[2] * width, width)
    loads = [
        pltpu.make_async_copy(weight_ref, weight_out, sems.at[0]),
        pltpu.make_async_copy(stream_ref.at[:, pl.ds(begin, width)], stream_out, sems.at[1]),
    ]
    for load in loads:
        load.start()
    maps_ref[0] = before_row_ref[...]
    for n in range(3):
        maps_ref[n + 1] = joined(compose(parted(before_ref[n]), parted(before_row_ref[...])))
    for load in loads:
        load.wait()


def row_kernel(place, all_ref, recv2_ref, recv3_ref, recv1_ref, before_ref, pay_ref, pairs, starts):
    group = place[3]
    pairs[group] = all_ref[...]
    for d, ref in ((1, recv1_ref), (2, recv2_ref), (3, recv3_ref)):
        pairs[group ^ d] = joined(load_payload(ref))
    two, three, total = prefixes([parted(pairs[n]) for n in range(4)])
    store_payload(pay_ref, total)
    row, column = iotas(WIDTH, 2 * WIDTH)
    starts[0] = (row == column).astype(F32)
    starts[1] = pairs[0]
    starts[2] = joined(two)
    starts[3] = joined(three)
    before_ref[...] = starts[group]


def state_kernel(
    place, recv2_ref, recv1_ref, recv3_ref, maps_ref, mine_ref, out1_ref, out2_ref, out3_ref, rows, states
):
    part, line = place[1], place[4]
    rows[line] = jnp.zeros(rows.shape[1:], F32)
    for r, ref in ((1, recv1_ref), (2, recv2_ref), (3, recv3_ref)):
        rows[line ^ r] = joined(load_payload(ref))
    state = jnp.where(line > 0, rows[0][:, WIDTH:], 0.0)
    for n in (1, 2):
        state = jnp.where(line > n, apply(parted(rows[n]), state), state)
    for n in range(4):
        states[n] = apply(parted(maps_ref[n]), state).astype(BF16)
    mine_ref[...] = states[part]
    for r, ref in ((1, out1_ref), (2, out2_ref), (3, out3_ref)):
        ref[...] = states[part ^ r]


def out_kernel(
    place, local_ref, through_ref, mine_ref, recv2_ref, recv3_ref, recv1_ref, w_ref, term_ref, *refs
):
    part = place[1]
    me = place[2]
    sent_refs, states = refs[:-1], refs[-1]
    groups = local_ref.shape[0]
    states[part] = mine_ref[...]
    for r, ref in ((1, recv1_ref), (2, recv2_ref), (3, recv3_ref)):
        states[part ^ r] = ref[...]
    normed = []
    for h in range(groups):
        result = local_ref[h].astype(F32) + dot(through_ref[h], states[h])
        normed.append(
            (
                result * lax.rsqrt(jnp.mean(result * result, axis=-1, keepdims=True) + 1e-05)
            ).astype(BF16)
        )
    normed = jnp.concatenate(normed, axis=1)
    width = term_ref.shape[1]
    count = len(sent_refs) + 1
    for r in range(count):
        begin = pl.multiple_of((me ^ r) * width, width)
        term = dot(normed, w_ref[:, pl.ds(begin, width)])
        if r == 0:
            term_ref[...] = term
        else:
            sent_refs[r - 1][...] = term.astype(BF16)


def hidden_kernel(stream_ref, term_ref, *refs):
    total = term_ref[...]
    for ref in refs[:-1]:
        total = total + ref[...].astype(F32)
    refs[-1][...] = (stream_ref[...].astype(F32) + total).astype(BF16)


def own_kernel(place, hidden_ref, w_ref, part_ref):
    width = hidden_ref.shape[1]
    begin = pl.multiple_of(place[2] * width, width)
    part_ref[...] = dot(hidden_ref[...], w_ref[pl.ds(begin, width), :])


def project_kernel(place, w_ref, part_ref, hidden_ref, block2_ref, block1_ref, block3_ref, q_ref, kv_ref):
    me = place[2]
    blocks = [block2_ref, block1_ref, block3_ref]
    rows, width = hidden_ref.shape
    total = part_ref[...]
    for block, r in zip(blocks, (2, 1, 3)):
        begin = pl.multiple_of((me ^ r) * width, width)
        total = total + dot(block[...], w_ref[pl.ds(begin, width), :])
    squares = 0.0
    for ref in [hidden_ref] + blocks:
        value = ref[...].astype(F32)
        squares = squares + jnp.sum(value * value, axis=-1, keepdims=True)
    total = total * lax.rsqrt(squares / (4 * width) + 1e-05)
    groups = width // WIDTH
    for h in range(groups):
        base = h * 3 * WIDTH
        span = slice(h * WIDTH, (h + 1) * WIDTH)
        q_ref[:, span] = to_unit(total[:, base : base + WIDTH]).astype(BF16)
        kv_ref[:, span] = to_unit(total[:, base + WIDTH : base + 2 * WIDTH]).astype(BF16)
        kv_ref[:, (groups + h) * WIDTH : (groups + h + 1) * WIDTH] = total[
            :, base + 2 * WIDTH : base + 3 * WIDTH
        ].astype(BF16)


def window_part(query_place, key_chip, core, q_ref, own_ref, other_ref, sums):
    rows = q_ref.shape[0]
    groups = q_ref.shape[1] // WIDTH
    row, column = iotas(rows, 2 * rows)
    query_place = query_place * rows + row
    own_place = (2 * key_chip + core) * rows + column
    other_place = (2 * key_chip + 1 - core) * rows + column - rows
    key_place = jnp.where(column < rows, own_place, other_place)
    allowed = (key_place <= query_place) & (key_place > query_place - WINDOW) & (key_place >= 0)
    ones = jnp.ones((2 * rows, WIDTH), BF16)
    for h in range(groups):
        span = slice(h * WIDTH, (h + 1) * WIDTH)
        value_span = slice((groups + h) * WIDTH, (groups + h + 1) * WIDTH)
        keys = jnp.concatenate([own_ref[:, span], other_ref[:, span]], axis=0)
        values = jnp.concatenate([own_ref[:, value_span], other_ref[:, value_span]], axis=0)
        scores = SCORE_SCALE * dot(q_ref[:, span], keys, (1, 1))
        weights = jnp.where(allowed, jnp.exp(scores), 0.0).astype(BF16)
        part = dot(weights, jnp.concatenate([values, ones], axis=1))
        sums[h] = part if sums[h] is None else sums[h] + part


def sum_spans(groups):
    return [slice(2 * h * WIDTH, 2 * (h + 1) * WIDTH) for h in range(groups)]


def away_kernel(place, hidden_ref, q_ref, own_ref, other_ref, sums_ref, keep_ref):
    seq = place[0]
    groups = q_ref.shape[1] // WIDTH
    sums = [None] * groups
    window_part(seq + 4, (seq >> 1) - 1, seq & 1, q_ref, own_ref, other_ref, sums)
    for h, span in enumerate(sum_spans(groups)):
        sums_ref[:, span] = sums[h]
    keep_ref[...] = hidden_ref[...]


def back_kernel(place, q_ref, sums_ref, own_ref, other_ref, back_ref):
    seq = place[0]
    rows = q_ref.shape[0]
    groups = q_ref.shape[1] // WIDTH
    sums = [sums_ref[:, span] for span in sum_spans(groups)]
    window_part(seq + 4, (seq >> 1) - 2, seq & 1, q_ref, own_ref, other_ref, sums)
    row, column = iotas(rows, WIDTH)
    line, _ = iotas(16, WIDTH)
    for h in range(groups):
        span = slice(h * WIDTH, (h + 1) * WIDTH)
        back_ref[0:rows, span] = sums[h][:, :WIDTH].astype(BF16)
        total = jnp.sum(jnp.where(row == column, sums[h][:, WIDTH:], 0.0), axis=0, keepdims=True)
        high = total.astype(BF16).astype(F32)
        totals = jnp.where(line == 0, high, jnp.where(line == 1, total - high, 0.0))
        back_ref[rows : rows + 16, span] = totals.astype(BF16)


def home_kernel(place, q_ref, *refs):
    blocks, sums_ref = refs[:-1], refs[-1]
    seq = place[0]
    groups = q_ref.shape[1] // WIDTH
    sums = [None] * groups
    for n in range(len(blocks) // 2):
        window_part(
            seq, (seq >> 1) - n, seq & 1, q_ref, blocks[2 * n], blocks[2 * n + 1], sums
        )
    for h, span in enumerate(sum_spans(groups)):
        sums_ref[:, span] = sums[h]


def last_kernel(sums_ref, back_ref, out_ref):
    groups = out_ref.shape[1] // WIDTH
    rows = out_ref.shape[0]
    row, column = iotas(rows, WIDTH)
    for h in range(groups):
        span = slice(h * WIDTH, (h + 1) * WIDTH)
        line = jnp.sum(back_ref[rows : rows + 16, span].astype(F32), axis=0, keepdims=True)
        far = jnp.sum(jnp.where(row == column, line, 0.0), axis=1, keepdims=True)
        mixed = sums_ref[:, 2 * h * WIDTH : (2 * h + 1) * WIDTH] + back_ref[0:rows, span].astype(F32)
        total = sums_ref[:, (2 * h + 1) * WIDTH : (2 * h + 2) * WIDTH] + far
        out_ref[:, span] = (mixed / total).astype(BF16)


def call(kernel, outs, smem=0, scratch=(), spaces=None, limit=LIMIT):
    def run(*args):
        places = [SMEM] * smem + (spaces or [VMEM] * (len(args) - smem))
        return pl.pallas_call(
            kernel,
            out_shape=[jax.ShapeDtypeStruct(shape, kind) for shape, kind in outs],
            in_specs=[pl.BlockSpec(memory_space=place) for place in places],
            out_specs=[pl.BlockSpec(memory_space=VMEM)] * len(outs),
            scratch_shapes=list(scratch),
            compiler_params=pltpu.CompilerParams(vmem_limit_bytes=limit),
        )(*args)

    return run


def moved(array, axis, distance):
    size = lax.axis_size(axis)
    return lax.ppermute(
        array, axis, [(i, i + distance) for i in range(size) if 0 <= i + distance < size]
    )


def crossed(array, mask, axis="seq"):
    return lax.ppermute(array, axis, [(i, i ^ mask) for i in range(lax.axis_size(axis))])


def body(queries, keys, values, gate_log, beta, stream, w_out, w_qkv):
    rows, wide = queries.shape
    groups = gate_log.shape[1]
    seq = lax.axis_index("seq")
    head = lax.axis_index("head")
    heads = lax.axis_size("head")
    place = jnp.stack([seq, seq & 3, head, (seq >> 2) & 3, seq >> 4]).astype(jnp.int32)
    pair_shape = ((WIDTH, 2 * WIDTH), F32)
    pay_shape = ((WIDTH + 16, 2 * WIDTH), BF16)
    state_shape = ((WIDTH, WIDTH), BF16)
    row_shape = ((rows, wide), BF16)
    four_pairs = pltpu.VMEM((4, WIDTH, 2 * WIDTH), F32)
    four_states = pltpu.VMEM((4, WIDTH, WIDTH), BF16)

    gates = jnp.concatenate([gate_log.T, beta.T], axis=0)
    unit_keys, writes, erasers, own, pay1, pay2, pay3 = call(
        map_kernel,
        [row_shape] + [((groups, rows, WIDTH), BF16)] * 2 + [pair_shape] + [pay_shape] * 3,
        1,
        [pltpu.VMEM((rows, wide), BF16)] * 2 + [four_pairs, pltpu.SemaphoreType.DMA((2,))],
        [VMEM] + [pltpu.HBM] * 2,
        CHUNK_LIMIT,
    )(place, gates, keys, values)
    pay2, pay3, pay1 = crossed(pay2, 2), crossed(pay3, 3), crossed(pay1, 1)
    local, through = call(query_kernel, [((groups, rows, WIDTH), BF16)] * 2)(
        gates, queries, unit_keys, writes, erasers
    )
    own, local, through = lax.optimization_barrier((own, local, through))
    before, everything, pay = call(
        group_kernel, [((3, WIDTH, 2 * WIDTH), F32), pair_shape, pay_shape], 1, [four_pairs]
    )(place, own, pay2, pay3, pay1)
    row2, row3, row1 = [crossed(pay, 4 * d) for d in (2, 3, 1)]
    everything, w_qkv = lax.optimization_barrier((everything, w_qkv))
    w_qkv, everything = call(
        fetch_wide_kernel,
        [(w_qkv.shape, BF16), pair_shape],
        0,
        [pltpu.SemaphoreType.DMA],
        [VMEM, pltpu.HBM],
        FETCH_LIMIT,
    )(everything, w_qkv)
    before_row, pay = call(row_kernel, [pair_shape, pay_shape], 1, [four_pairs] * 2)(
        place, everything, row2, row3, row1
    )
    row2, row1, row3 = [crossed(pay, 16 * d) for d in (2, 1, 3)]
    before_row, w_out, stream = lax.optimization_barrier((before_row, w_out, stream))
    w_out, stream, maps = call(
        fetch_kernel,
        [(w_out.shape, BF16), row_shape, ((4, WIDTH, 2 * WIDTH), F32)],
        1,
        [pltpu.SemaphoreType.DMA((2,))],
        [VMEM, VMEM, pltpu.HBM, pltpu.HBM],
        FETCH_LIMIT,
    )(place, before_row, before, w_out, stream)
    mine, out1, out2, out3 = call(state_kernel, [state_shape] * 4, 1, [four_pairs, four_states])(
        place, row2, row1, row3, maps
    )
    terms = call(
        out_kernel,
        [((rows, wide), F32)] + [row_shape] * (heads - 1),
        1,
        [four_states],
    )(
        place,
        local,
        through,
        mine,
        crossed(out2, 2),
        crossed(out3, 3),
        crossed(out1, 1),
        w_out,
    )
    received = [crossed(terms[r], r, "head") for r in (2, 1, 3)]
    (hidden,) = call(hidden_kernel, [row_shape])(stream, terms[0], *received)
    other2, other1, other3 = [crossed(hidden, r, "head") for r in (2, 1, 3)]
    (part,) = call(own_kernel, [((rows, w_qkv.shape[1]), F32)], 1)(place, hidden, w_qkv)
    unit_queries, pack = call(project_kernel, [row_shape, ((rows, 2 * wide), BF16)], 1)(
        place, w_qkv, part, hidden, other2, other1, other3
    )
    first, visitors = lax.optimization_barrier(
        (moved(pack, "seq", 2), moved(unit_queries, "seq", -2))
    )
    second, visitors = lax.optimization_barrier(
        (moved(first, "seq", 2), moved(visitors, "seq", -2))
    )
    home = [
        pack, crossed(pack, 1), first, crossed(first, 1), second, crossed(second, 1)
    ]
    sums_shape = ((rows, 2 * wide), F32)
    away, kept = call(away_kernel, [sums_shape, row_shape], 1)(
        place, hidden, visitors, home[2], home[3]
    )
    (back,) = call(back_kernel, [((rows + 16, wide), BF16)], 1)(
        place, visitors, away, home[4], home[5]
    )
    returned = moved(back, "seq", 4)
    (sums,) = call(home_kernel, [((rows, 2 * wide), F32)], 1)(place, unit_queries, *home)
    (attended,) = call(last_kernel, [row_shape])(sums, returned)
    return (kept, attended)


def solution(mesh):
    in_specs = (
        P("seq", "head"),
        P("seq", "head"),
        P("seq", "head"),
        P("seq", "head"),
        P("seq", "head"),
        P("seq", None),
        P("head", None),
        P(None, "head"),
    )
    out_specs = (P("seq", "head"), P("seq", "head"))
    return jax.shard_map(body, mesh=mesh, in_specs=in_specs, out_specs=out_specs, check_vma=False)
```

```python
import functools

import jax
import jax.numpy as jnp
from jax import lax
from jax.experimental import pallas as pl
from jax.experimental.pallas import tpu as pltpu
from jax.sharding import PartitionSpec as P

WINDOW = 1024
WIDTH = 128
SCORE_SCALE = 10.0
F32 = jnp.float32
BF16 = jnp.bfloat16
HIGHEST = lax.Precision.HIGHEST
VMEM = pltpu.VMEM
SMEM = pltpu.SMEM
LIMIT = 16 * 1024 * 1024
FETCH_LIMIT = 44 * 1024 * 1024
CHUNK_LIMIT = 54448 * 1024


def dot(left, right, contract=(1, 0), precision=None):
    return lax.dot_general(
        left,
        right,
        (((contract[0],), (contract[1],)), ((), ())),
        precision=precision,
        preferred_element_type=F32,
    )


def exact(left, right, contract=(1, 0)):
    return dot(left, right, contract, HIGHEST)


def iotas(rows, columns):
    return (
        lax.broadcasted_iota(jnp.int32, (rows, columns), 0),
        lax.broadcasted_iota(jnp.int32, (rows, columns), 1),
    )


def fine(left, right):
    left_high = left.astype(BF16)
    right_high = right.astype(BF16)
    left_low = (left - left_high.astype(F32)).astype(BF16)
    right_low = (right - right_high.astype(F32)).astype(BF16)
    wide = right.shape[1]
    both = dot(left_high, jnp.concatenate([right_high, right_low], axis=1))
    return both[:, :wide] + both[:, wide:] + dot(left_low, right_high)


def split_diagonal(matrix):
    row, column = iotas(WIDTH, WIDTH)
    high = matrix.astype(BF16)
    return high, jnp.where(row == column, matrix - high.astype(F32), 0.0)


def compose(left, right):
    left_t, left_o = left
    right_t, right_o = right
    left_high, left_rest = split_diagonal(left_t)
    right_high, right_rest = split_diagonal(right_t)
    left_column = jnp.sum(left_rest, axis=1, keepdims=True)
    right_row = jnp.sum(right_rest, axis=0, keepdims=True)
    offset = dot(left_high, right_o.astype(BF16)) + left_column * right_o + left_o
    product = dot(left_high, right_high) + left_column * right_t + left_high.astype(F32) * right_row
    return product, offset


def apply(left, state):
    left_t, left_o = left
    left_high, left_rest = split_diagonal(left_t)
    left_column = jnp.sum(left_rest, axis=1, keepdims=True)
    return dot(left_high, state.astype(BF16)) + left_column * state + left_o


def store_payload(ref, pair):
    row, _ = iotas(16, 2 * WIDTH)
    transition, offset = pair
    high, rest = split_diagonal(transition)
    ref[0:WIDTH, 0:WIDTH] = high
    ref[0:WIDTH, WIDTH : 2 * WIDTH] = offset.astype(BF16)
    line = jnp.sum(rest, axis=0, keepdims=True)
    line = jnp.concatenate([line, jnp.zeros_like(line)], axis=1)
    ref[WIDTH : WIDTH + 16, :] = jnp.where(row == 0, line, 0.0).astype(BF16)


def load_payload(ref):
    row, column = iotas(WIDTH, WIDTH)
    line = ref[WIDTH : WIDTH + 16, 0:WIDTH].astype(F32)
    line = jnp.sum(line, axis=0, keepdims=True)
    transition = ref[0:WIDTH, 0:WIDTH].astype(F32)
    transition = transition + jnp.where(row == column, line, 0.0)
    return transition, ref[0:WIDTH, WIDTH : 2 * WIDTH].astype(F32)


def joined(pair):
    return jnp.concatenate(pair, axis=1)


def parted(array):
    return array[:, :WIDTH], array[:, WIDTH:]


def to_unit(vectors):
    return vectors * lax.rsqrt(jnp.sum(vectors * vectors, axis=-1, keepdims=True) + 1e-06)


def lower_inverses(couplings):
    rows = couplings[0].shape[0]
    row, column = iotas(rows, rows)
    identity = (row == column).astype(F32)
    inside = (row >> 3) == (column >> 3)
    powers = [jnp.where(inside, c, 0.0) for c in couplings]
    results = [identity - p for p in powers]
    span = 2
    while span < 8:
        powers = [fine(p, p) for p in powers]
        results = [fine(r, identity + p) for r, p in zip(results, powers)]
        span *= 2
    shift = 3
    while (1 << shift) < rows:
        level = ((row >> (shift + 1)) == (column >> (shift + 1))) & ((row >> shift) > (column >> shift))
        crossing = [fine(r, jnp.where(level, c, 0.0)) for r, c in zip(results, couplings)]
        results = [r - fine(x, r) for r, x in zip(results, crossing)]
        shift += 1
    return results


def decays(gb_ref):
    rows = gb_ref.shape[1]
    groups = gb_ref.shape[0] // 2
    row, column = iotas(rows, rows)
    both = gb_ref[...]
    high = both.astype(BF16)
    rest = both - high.astype(F32)
    middle = rest.astype(BF16)
    low = (rest - middle.astype(F32)).astype(BF16)
    sums = dot(jnp.concatenate([high, middle, low], axis=0), (row <= column).astype(BF16))
    count = 2 * groups
    summed_row = sums[:count] + sums[count : 2 * count] + sums[2 * count :]
    columns = jnp.concatenate([summed_row[:groups], both[groups:]], axis=0).T
    causal = row >= column
    spreads = [columns[:, h : h + 1] - summed_row[h : h + 1, :] for h in range(groups)]
    return columns, [
        jnp.where(causal, jnp.exp(jnp.where(causal, spread, 0.0)), 0.0) for spread in spreads
    ]


def map_kernel(
    place, gb_ref, k_hbm, v_hbm, keys_ref, writes_ref, erasers_ref, own_ref, pay1_ref, pay2_ref, pay3_ref, k_ref, v_ref, pairs, sems
):
    part = place[1]
    rows = gb_ref.shape[1]
    groups = gb_ref.shape[0] // 2
    loads = [
        pltpu.make_async_copy(k_hbm, k_ref, sems.at[0]),
        pltpu.make_async_copy(v_hbm, v_ref, sems.at[1]),
    ]
    for load in loads:
        load.start()
    row, column = iotas(rows, rows)
    summed, decay = decays(gb_ref)
    betas = summed[:, groups:]
    loads[0].wait()
    keys, couplings = [], []
    for h in range(groups):
        span = slice(h * WIDTH, (h + 1) * WIDTH)
        key = to_unit(k_ref[:, span].astype(F32)).astype(BF16)
        keys_ref[:, span] = key
        both = dot(key, key, (1, 1))
        couplings.append(jnp.where(row > column, betas[:, h : h + 1] * decay[h] * both, 0.0))
        keys.append(key.astype(F32))
    inverses = lower_inverses(couplings)
    loads[1].wait()
    for h in range(groups):
        span = slice(h * WIDTH, (h + 1) * WIDTH)
        along = summed[:, h : h + 1]
        last = summed[rows - 1 : rows, h : h + 1]
        beta = betas[:, h : h + 1]
        value = v_ref[:, span].astype(F32)
        made = fine(
            inverses[h],
            jnp.concatenate([beta * value, (beta * jnp.exp(along)) * keys[h]], axis=1),
        ).astype(BF16)
        writes_ref[h], erasers_ref[h] = parted(made)
        ended = (jnp.exp(last - along) * keys[h]).astype(BF16)
        effect = dot(ended, made, (0, 0))
        identity = iotas(WIDTH, WIDTH)
        kept = jnp.where(identity[0] == identity[1], jnp.exp(last), 0.0)
        pairs[h, :, 0:WIDTH] = kept - effect[:, WIDTH:]
        pairs[h, :, WIDTH:] = effect[:, :WIDTH]
    own_ref[...] = pairs[part]
    for r, ref in ((1, pay1_ref), (2, pay2_ref), (3, pay3_ref)):
        store_payload(ref, parted(pairs[part ^ r]))


def query_kernel(gb_ref, q_ref, keys_ref, writes_ref, erasers_ref, local_ref, through_ref):
    groups = gb_ref.shape[0] // 2
    summed, decay = decays(gb_ref)
    for h in range(groups):
        span = slice(h * WIDTH, (h + 1) * WIDTH)
        query = to_unit(q_ref[:, span].astype(F32)).astype(BF16)
        mixing = (dot(query, keys_ref[:, span], (1, 1)) * decay[h]).astype(BF16)
        inner = dot(mixing, joined((writes_ref[h], erasers_ref[h])))
        local_ref[h] = inner[:, :WIDTH].astype(BF16)
        decayed = jnp.exp(summed[:, h : h + 1]) * query.astype(F32)
        through_ref[h] = (decayed - inner[:, WIDTH:]).astype(BF16)


def prefixes(blocks):
    two = compose(blocks[1], blocks[0])
    return two, compose(blocks[2], two), compose(compose(blocks[3], blocks[2]), two)


def group_kernel(place, own_ref, recv2_ref, recv3_ref, recv1_ref, before_ref, all_ref, pay_ref, pairs):
    part = place[1]
    pairs[part] = own_ref[...]
    for r, ref in ((1, recv1_ref), (2, recv2_ref), (3, recv3_ref)):
        pairs[part ^ r] = joined(load_payload(ref))
    two, three, total = prefixes([parted(pairs[n]) for n in range(4)])
    store_payload(pay_ref, total)
    all_ref[...] = joined(total)
    before_ref[0] = pairs[0]
    before_ref[1] = joined(two)
    before_ref[2] = joined(three)


def fetch_wide_kernel(token_ref, source_ref, fetched_ref, token_out, sem):
    load = pltpu.make_async_copy(source_ref, fetched_ref, sem)
    load.start()
    token_out[...] = token_ref[...]
    load.wait()


def fetch_kernel(
    place, before_row_ref, before_ref, weight_ref, stream_ref, weight_out, stream_out, maps_ref, sems
):
    width = stream_out.shape[1]
    begin = pl.multiple_of(place[2] * width, width)
    loads = [
        pltpu.make_async_copy(weight_ref, weight_out, sems.at[0]),
        pltpu.make_async_copy(stream_ref.at[:, pl.ds(begin, width)], stream_out, sems.at[1]),
    ]
    for load in loads:
        load.start()
    maps_ref[0] = before_row_ref[...]
    for n in range(3):
        maps_ref[n + 1] = joined(compose(parted(before_ref[n]), parted(before_row_ref[...])))
    for load in loads:
        load.wait()


def row_kernel(place, all_ref, recv2_ref, recv3_ref, recv1_ref, before_ref, pay_ref, pairs, starts):
    group = place[3]
    pairs[group] = all_ref[...]
    for d, ref in ((1, recv1_ref), (2, recv2_ref), (3, recv3_ref)):
        pairs[group ^ d] = joined(load_payload(ref))
    two, three, total = prefixes([parted(pairs[n]) for n in range(4)])
    store_payload(pay_ref, total)
    row, column = iotas(WIDTH, 2 * WIDTH)
    starts[0] = (row == column).astype(F32)
    starts[1] = pairs[0]
    starts[2] = joined(two)
    starts[3] = joined(three)
    before_ref[...] = starts[group]


def state_kernel(
    place, recv2_ref, recv1_ref, recv3_ref, maps_ref, mine_ref, out1_ref, out2_ref, out3_ref, rows, states
):
    part, line = place[1], place[4]
    rows[line] = jnp.zeros(rows.shape[1:], F32)
    for r, ref in ((1, recv1_ref), (2, recv2_ref), (3, recv3_ref)):
        rows[line ^ r] = joined(load_payload(ref))
    state = jnp.where(line > 0, rows[0][:, WIDTH:], 0.0)
    for n in (1, 2):
        state = jnp.where(line > n, apply(parted(rows[n]), state), state)
    for n in range(4):
        states[n] = apply(parted(maps_ref[n]), state).astype(BF16)
    mine_ref[...] = states[part]
    for r, ref in ((1, out1_ref), (2, out2_ref), (3, out3_ref)):
        ref[...] = states[part ^ r]


def out_kernel(
    place, local_ref, through_ref, mine_ref, recv2_ref, recv3_ref, recv1_ref, w_ref, term_ref, *refs
):
    part = place[1]
    me = place[2]
    sent_refs, states = refs[:-1], refs[-1]
    groups = local_ref.shape[0]
    states[part] = mine_ref[...]
    for r, ref in ((1, recv1_ref), (2, recv2_ref), (3, recv3_ref)):
        states[part ^ r] = ref[...]
    normed = []
    for h in range(groups):
        result = local_ref[h].astype(F32) + dot(through_ref[h], states[h])
        normed.append(
            (
                result * lax.rsqrt(jnp.mean(result * result, axis=-1, keepdims=True) + 1e-05)
            ).astype(BF16)
        )
    normed = jnp.concatenate(normed, axis=1)
    width = term_ref.shape[1]
    count = len(sent_refs) + 1
    for r in range(count):
        begin = pl.multiple_of((me ^ r) * width, width)
        term = dot(normed, w_ref[:, pl.ds(begin, width)])
        if r == 0:
            term_ref[...] = term
        else:
            sent_refs[r - 1][...] = term.astype(BF16)


def hidden_kernel(stream_ref, term_ref, *refs):
    total = term_ref[...]
    for ref in refs[:-1]:
        total = total + ref[...].astype(F32)
    refs[-1][...] = (stream_ref[...].astype(F32) + total).astype(BF16)


def own_kernel(place, hidden_ref, w_ref, part_ref):
    width = hidden_ref.shape[1]
    begin = pl.multiple_of(place[2] * width, width)
    part_ref[...] = dot(hidden_ref[...], w_ref[pl.ds(begin, width), :])


def project_kernel(place, w_ref, part_ref, hidden_ref, block2_ref, block1_ref, block3_ref, q_ref, kv_ref):
    me = place[2]
    blocks = [block2_ref, block1_ref, block3_ref]
    rows, width = hidden_ref.shape
    total = part_ref[...]
    for block, r in zip(blocks, (2, 1, 3)):
        begin = pl.multiple_of((me ^ r) * width, width)
        total = total + dot(block[...], w_ref[pl.ds(begin, width), :])
    squares = 0.0
    for ref in [hidden_ref] + blocks:
        value = ref[...].astype(F32)
        squares = squares + jnp.sum(value * value, axis=-1, keepdims=True)
    total = total * lax.rsqrt(squares / (4 * width) + 1e-05)
    groups = width // WIDTH
    for h in range(groups):
        base = h * 3 * WIDTH
        span = slice(h * WIDTH, (h + 1) * WIDTH)
        q_ref[:, span] = to_unit(total[:, base : base + WIDTH]).astype(BF16)
        kv_ref[:, span] = to_unit(total[:, base + WIDTH : base + 2 * WIDTH]).astype(BF16)
        kv_ref[:, (groups + h) * WIDTH : (groups + h + 1) * WIDTH] = total[
            :, base + 2 * WIDTH : base + 3 * WIDTH
        ].astype(BF16)


def window_part(query_place, key_chip, core, q_ref, own_ref, other_ref, sums):
    rows = q_ref.shape[0]
    groups = q_ref.shape[1] // WIDTH
    row, column = iotas(rows, 2 * rows)
    query_place = query_place * rows + row
    own_place = (2 * key_chip + core) * rows + column
    other_place = (2 * key_chip + 1 - core) * rows + column - rows
    key_place = jnp.where(column < rows, own_place, other_place)
    allowed = (key_place <= query_place) & (key_place > query_place - WINDOW) & (key_place >= 0)
    ones = jnp.ones((2 * rows, WIDTH), BF16)
    for h in range(groups):
        span = slice(h * WIDTH, (h + 1) * WIDTH)
        value_span = slice((groups + h) * WIDTH, (groups + h + 1) * WIDTH)
        keys = jnp.concatenate([own_ref[:, span], other_ref[:, span]], axis=0)
        values = jnp.concatenate([own_ref[:, value_span], other_ref[:, value_span]], axis=0)
        scores = SCORE_SCALE * dot(q_ref[:, span], keys, (1, 1))
        weights = jnp.where(allowed, jnp.exp(scores), 0.0).astype(BF16)
        part = dot(weights, jnp.concatenate([values, ones], axis=1))
        sums[h] = part if sums[h] is None else sums[h] + part


def sum_spans(groups):
    return [slice(2 * h * WIDTH, 2 * (h + 1) * WIDTH) for h in range(groups)]


def away_kernel(place, hidden_ref, q_ref, own_ref, other_ref, sums_ref, keep_ref):
    seq = place[0]
    groups = q_ref.shape[1] // WIDTH
    sums = [None] * groups
    window_part(seq + 4, (seq >> 1) - 1, seq & 1, q_ref, own_ref, other_ref, sums)
    for h, span in enumerate(sum_spans(groups)):
        sums_ref[:, span] = sums[h]
    keep_ref[...] = hidden_ref[...]


def back_kernel(place, q_ref, sums_ref, own_ref, other_ref, back_ref):
    seq = place[0]
    rows = q_ref.shape[0]
    groups = q_ref.shape[1] // WIDTH
    sums = [sums_ref[:, span] for span in sum_spans(groups)]
    window_part(seq + 4, (seq >> 1) - 2, seq & 1, q_ref, own_ref, other_ref, sums)
    row, column = iotas(rows, WIDTH)
    line, _ = iotas(16, WIDTH)
    for h in range(groups):
        span = slice(h * WIDTH, (h + 1) * WIDTH)
        back_ref[0:rows, span] = sums[h][:, :WIDTH].astype(BF16)
        total = jnp.sum(jnp.where(row == column, sums[h][:, WIDTH:], 0.0), axis=0, keepdims=True)
        high = total.astype(BF16).astype(F32)
        totals = jnp.where(line == 0, high, jnp.where(line == 1, total - high, 0.0))
        back_ref[rows : rows + 16, span] = totals.astype(BF16)


def home_kernel(place, q_ref, *refs):
    blocks, sums_ref = refs[:-1], refs[-1]
    seq = place[0]
    groups = q_ref.shape[1] // WIDTH
    sums = [None] * groups
    for n in range(len(blocks) // 2):
        window_part(
            seq, (seq >> 1) - n, seq & 1, q_ref, blocks[2 * n], blocks[2 * n + 1], sums
        )
    for h, span in enumerate(sum_spans(groups)):
        sums_ref[:, span] = sums[h]


def last_kernel(sums_ref, back_ref, out_ref):
    groups = out_ref.shape[1] // WIDTH
    rows = out_ref.shape[0]
    row, column = iotas(rows, WIDTH)
    for h in range(groups):
        span = slice(h * WIDTH, (h + 1) * WIDTH)
        line = jnp.sum(back_ref[rows : rows + 16, span].astype(F32), axis=0, keepdims=True)
        far = jnp.sum(jnp.where(row == column, line, 0.0), axis=1, keepdims=True)
        mixed = sums_ref[:, 2 * h * WIDTH : (2 * h + 1) * WIDTH] + back_ref[0:rows, span].astype(F32)
        total = sums_ref[:, (2 * h + 1) * WIDTH : (2 * h + 2) * WIDTH] + far
        out_ref[:, span] = (mixed / total).astype(BF16)


def call(kernel, outs, smem=0, scratch=(), spaces=None, limit=LIMIT):
    def run(*args):
        places = [SMEM] * smem + (spaces or [VMEM] * (len(args) - smem))
        return pl.pallas_call(
            kernel,
            out_shape=[jax.ShapeDtypeStruct(shape, kind) for shape, kind in outs],
            in_specs=[pl.BlockSpec(memory_space=place) for place in places],
            out_specs=[pl.BlockSpec(memory_space=VMEM)] * len(outs),
            scratch_shapes=list(scratch),
            compiler_params=pltpu.CompilerParams(vmem_limit_bytes=limit),
        )(*args)

    return run


def moved(array, axis, distance):
    size = lax.axis_size(axis)
    return lax.ppermute(
        array, axis, [(i, i + distance) for i in range(size) if 0 <= i + distance < size]
    )


def crossed(array, mask, axis="seq"):
    return lax.ppermute(array, axis, [(i, i ^ mask) for i in range(lax.axis_size(axis))])


def body(queries, keys, values, gate_log, beta, stream, w_out, w_qkv):
    rows, wide = queries.shape
    groups = gate_log.shape[1]
    seq = lax.axis_index("seq")
    head = lax.axis_index("head")
    heads = lax.axis_size("head")
    place = jnp.stack([seq, seq & 3, head, (seq >> 2) & 3, seq >> 4]).astype(jnp.int32)
    pair_shape = ((WIDTH, 2 * WIDTH), F32)
    pay_shape = ((WIDTH + 16, 2 * WIDTH), BF16)
    state_shape = ((WIDTH, WIDTH), BF16)
    row_shape = ((rows, wide), BF16)
    four_pairs = pltpu.VMEM((4, WIDTH, 2 * WIDTH), F32)
    four_states = pltpu.VMEM((4, WIDTH, WIDTH), BF16)

    gates = jnp.concatenate([gate_log.T, beta.T], axis=0)
    unit_keys, writes, erasers, own, pay1, pay2, pay3 = call(
        map_kernel,
        [row_shape] + [((groups, rows, WIDTH), BF16)] * 2 + [pair_shape] + [pay_shape] * 3,
        1,
        [pltpu.VMEM((rows, wide), BF16)] * 2 + [four_pairs, pltpu.SemaphoreType.DMA((2,))],
        [VMEM] + [pltpu.HBM] * 2,
        CHUNK_LIMIT,
    )(place, gates, keys, values)
    pay2, pay3, pay1 = crossed(pay2, 2), crossed(pay3, 3), crossed(pay1, 1)
    local, through = call(query_kernel, [((groups, rows, WIDTH), BF16)] * 2)(
        gates, queries, unit_keys, writes, erasers
    )
    own, local, through = lax.optimization_barrier((own, local, through))
    before, everything, pay = call(
        group_kernel, [((3, WIDTH, 2 * WIDTH), F32), pair_shape, pay_shape], 1, [four_pairs]
    )(place, own, pay2, pay3, pay1)
    row2, row3, row1 = [crossed(pay, 4 * d) for d in (2, 3, 1)]
    everything, w_qkv = lax.optimization_barrier((everything, w_qkv))
    w_qkv, everything = call(
        fetch_wide_kernel,
        [(w_qkv.shape, BF16), pair_shape],
        0,
        [pltpu.SemaphoreType.DMA],
        [VMEM, pltpu.HBM],
        FETCH_LIMIT,
    )(everything, w_qkv)
    before_row, pay = call(row_kernel, [pair_shape, pay_shape], 1, [four_pairs] * 2)(
        place, everything, row2, row3, row1
    )
    row2, row1, row3 = [crossed(pay, 16 * d) for d in (2, 1, 3)]
    before_row, w_out, stream = lax.optimization_barrier((before_row, w_out, stream))
    w_out, stream, maps = call(
        fetch_kernel,
        [(w_out.shape, BF16), row_shape, ((4, WIDTH, 2 * WIDTH), F32)],
        1,
        [pltpu.SemaphoreType.DMA((2,))],
        [VMEM, VMEM, pltpu.HBM, pltpu.HBM],
        FETCH_LIMIT,
    )(place, before_row, before, w_out, stream)
    mine, out1, out2, out3 = call(state_kernel, [state_shape] * 4, 1, [four_pairs, four_states])(
        place, row2, row1, row3, maps
    )
    terms = call(
        out_kernel,
        [((rows, wide), F32)] + [row_shape] * (heads - 1),
        1,
        [four_states],
    )(
        place,
        local,
        through,
        mine,
        crossed(out2, 2),
        crossed(out3, 3),
        crossed(out1, 1),
        w_out,
    )
    received = [crossed(terms[r], r, "head") for r in (2, 1, 3)]
    (hidden,) = call(hidden_kernel, [row_shape])(stream, terms[0], *received)
    other2, other1, other3 = [crossed(hidden, r, "head") for r in (2, 1, 3)]
    (part,) = call(own_kernel, [((rows, w_qkv.shape[1]), F32)], 1)(place, hidden, w_qkv)
    unit_queries, pack = call(project_kernel, [row_shape, ((rows, 2 * wide), BF16)], 1)(
        place, w_qkv, part, hidden, other2, other1, other3
    )
    first, visitors = moved(pack, "seq", 2), moved(unit_queries, "seq", -2)
    second, visitors = lax.optimization_barrier(
        (moved(first, "seq", 2), moved(visitors, "seq", -2))
    )
    home = [
        pack, crossed(pack, 1), first, crossed(first, 1), second, crossed(second, 1)
    ]
    sums_shape = ((rows, 2 * wide), F32)
    away, kept = call(away_kernel, [sums_shape, row_shape], 1)(
        place, hidden, visitors, home[2], home[3]
    )
    (back,) = call(back_kernel, [((rows + 16, wide), BF16)], 1)(
        place, visitors, away, home[4], home[5]
    )
    returned = moved(back, "seq", 4)
    (sums,) = call(home_kernel, [((rows, 2 * wide), F32)], 1)(place, unit_queries, *home)
    (attended,) = call(last_kernel, [row_shape])(sums, returned)
    return (kept, attended)


def solution(mesh):
    in_specs = (
        P("seq", "head"),
        P("seq", "head"),
        P("seq", "head"),
        P("seq", "head"),
        P("seq", "head"),
        P("seq", None),
        P("head", None),
        P(None, "head"),
    )
    out_specs = (P("seq", "head"), P("seq", "head"))
    return jax.shard_map(body, mesh=mesh, in_specs=in_specs, out_specs=out_specs, check_vma=False)
```

```python
import functools

import jax
import jax.numpy as jnp
from jax import lax
from jax.experimental import pallas as pl
from jax.experimental.pallas import tpu as pltpu
from jax.sharding import PartitionSpec as P

WINDOW = 1024
WIDTH = 128
SCORE_SCALE = 10.0
F32 = jnp.float32
BF16 = jnp.bfloat16
HIGHEST = lax.Precision.HIGHEST
VMEM = pltpu.VMEM
SMEM = pltpu.SMEM
LIMIT = 16 * 1024 * 1024
FETCH_LIMIT = 44 * 1024 * 1024
CHUNK_LIMIT = 54448 * 1024


def dot(left, right, contract=(1, 0), precision=None):
    return lax.dot_general(
        left,
        right,
        (((contract[0],), (contract[1],)), ((), ())),
        precision=precision,
        preferred_element_type=F32,
    )


def exact(left, right, contract=(1, 0)):
    return dot(left, right, contract, HIGHEST)


def iotas(rows, columns):
    return (
        lax.broadcasted_iota(jnp.int32, (rows, columns), 0),
        lax.broadcasted_iota(jnp.int32, (rows, columns), 1),
    )


def fine(left, right):
    left_high = left.astype(BF16)
    right_high = right.astype(BF16)
    left_low = (left - left_high.astype(F32)).astype(BF16)
    right_low = (right - right_high.astype(F32)).astype(BF16)
    wide = right.shape[1]
    both = dot(left_high, jnp.concatenate([right_high, right_low], axis=1))
    return both[:, :wide] + both[:, wide:] + dot(left_low, right_high)


def split_diagonal(matrix):
    row, column = iotas(WIDTH, WIDTH)
    high = matrix.astype(BF16)
    return high, jnp.where(row == column, matrix - high.astype(F32), 0.0)


def compose(left, right):
    left_t, left_o = left
    right_t, right_o = right
    left_high, left_rest = split_diagonal(left_t)
    right_high, right_rest = split_diagonal(right_t)
    left_column = jnp.sum(left_rest, axis=1, keepdims=True)
    right_row = jnp.sum(right_rest, axis=0, keepdims=True)
    offset = dot(left_high, right_o.astype(BF16)) + left_column * right_o + left_o
    product = dot(left_high, right_high) + left_column * right_t + left_high.astype(F32) * right_row
    return product, offset


def apply(left, state):
    left_t, left_o = left
    left_high, left_rest = split_diagonal(left_t)
    left_column = jnp.sum(left_rest, axis=1, keepdims=True)
    return dot(left_high, state.astype(BF16)) + left_column * state + left_o


def store_payload(ref, pair):
    row, _ = iotas(16, 2 * WIDTH)
    transition, offset = pair
    high, rest = split_diagonal(transition)
    ref[0:WIDTH, 0:WIDTH] = high
    ref[0:WIDTH, WIDTH : 2 * WIDTH] = offset.astype(BF16)
    line = jnp.sum(rest, axis=0, keepdims=True)
    line = jnp.concatenate([line, jnp.zeros_like(line)], axis=1)
    ref[WIDTH : WIDTH + 16, :] = jnp.where(row == 0, line, 0.0).astype(BF16)


def load_payload(ref):
    row, column = iotas(WIDTH, WIDTH)
    line = ref[WIDTH : WIDTH + 16, 0:WIDTH].astype(F32)
    line = jnp.sum(line, axis=0, keepdims=True)
    transition = ref[0:WIDTH, 0:WIDTH].astype(F32)
    transition = transition + jnp.where(row == column, line, 0.0)
    return transition, ref[0:WIDTH, WIDTH : 2 * WIDTH].astype(F32)


def joined(pair):
    return jnp.concatenate(pair, axis=1)


def parted(array):
    return array[:, :WIDTH], array[:, WIDTH:]


def to_unit(vectors):
    return vectors * lax.rsqrt(jnp.sum(vectors * vectors, axis=-1, keepdims=True) + 1e-06)


def lower_inverses(couplings):
    rows = couplings[0].shape[0]
    row, column = iotas(rows, rows)
    identity = (row == column).astype(F32)
    inside = (row >> 3) == (column >> 3)
    powers = [jnp.where(inside, c, 0.0) for c in couplings]
    results = [identity - p for p in powers]
    span = 2
    while span < 8:
        powers = [fine(p, p) for p in powers]
        results = [fine(r, identity + p) for r, p in zip(results, powers)]
        span *= 2
    shift = 3
    while (1 << shift) < rows:
        level = ((row >> (shift + 1)) == (column >> (shift + 1))) & ((row >> shift) > (column >> shift))
        crossing = [fine(r, jnp.where(level, c, 0.0)) for r, c in zip(results, couplings)]
        results = [r - fine(x, r) for r, x in zip(results, crossing)]
        shift += 1
    return results


def decays(gb_ref):
    rows = gb_ref.shape[1]
    groups = gb_ref.shape[0] // 2
    row, column = iotas(rows, rows)
    both = gb_ref[...]
    high = both.astype(BF16)
    rest = both - high.astype(F32)
    middle = rest.astype(BF16)
    low = (rest - middle.astype(F32)).astype(BF16)
    sums = dot(jnp.concatenate([high, middle, low], axis=0), (row <= column).astype(BF16))
    count = 2 * groups
    summed_row = sums[:count] + sums[count : 2 * count] + sums[2 * count :]
    columns = jnp.concatenate([summed_row[:groups], both[groups:]], axis=0).T
    causal = row >= column
    spreads = [columns[:, h : h + 1] - summed_row[h : h + 1, :] for h in range(groups)]
    return columns, [
        jnp.where(causal, jnp.exp(jnp.where(causal, spread, 0.0)), 0.0) for spread in spreads
    ]


def map_kernel(
    place, gb_ref, k_hbm, v_hbm, keys_ref, writes_ref, erasers_ref, own_ref, pay1_ref, pay2_ref, pay3_ref, k_ref, v_ref, pairs, sems
):
    part = place[1]
    rows = gb_ref.shape[1]
    groups = gb_ref.shape[0] // 2
    loads = [
        pltpu.make_async_copy(k_hbm, k_ref, sems.at[0]),
        pltpu.make_async_copy(v_hbm, v_ref, sems.at[1]),
    ]
    for load in loads:
        load.start()
    row, column = iotas(rows, rows)
    summed, decay = decays(gb_ref)
    betas = summed[:, groups:]
    loads[0].wait()
    keys, couplings = [], []
    for h in range(groups):
        span = slice(h * WIDTH, (h + 1) * WIDTH)
        key = to_unit(k_ref[:, span].astype(F32)).astype(BF16)
        keys_ref[:, span] = key
        both = dot(key, key, (1, 1))
        couplings.append(jnp.where(row > column, betas[:, h : h + 1] * decay[h] * both, 0.0))
        keys.append(key.astype(F32))
    inverses = lower_inverses(couplings)
    loads[1].wait()
    for h in range(groups):
        span = slice(h * WIDTH, (h + 1) * WIDTH)
        along = summed[:, h : h + 1]
        last = summed[rows - 1 : rows, h : h + 1]
        beta = betas[:, h : h + 1]
        value = v_ref[:, span].astype(F32)
        made = fine(
            inverses[h],
            jnp.concatenate([beta * value, (beta * jnp.exp(along)) * keys[h]], axis=1),
        ).astype(BF16)
        writes_ref[h], erasers_ref[h] = parted(made)
        ended = (jnp.exp(last - along) * keys[h]).astype(BF16)
        effect = dot(ended, made, (0, 0))
        identity = iotas(WIDTH, WIDTH)
        kept = jnp.where(identity[0] == identity[1], jnp.exp(last), 0.0)
        pairs[h, :, 0:WIDTH] = kept - effect[:, WIDTH:]
        pairs[h, :, WIDTH:] = effect[:, :WIDTH]
    own_ref[...] = pairs[part]
    for r, ref in ((1, pay1_ref), (2, pay2_ref), (3, pay3_ref)):
        store_payload(ref, parted(pairs[part ^ r]))


def query_kernel(gb_ref, q_ref, keys_ref, writes_ref, erasers_ref, local_ref, through_ref):
    groups = gb_ref.shape[0] // 2
    summed, decay = decays(gb_ref)
    for h in range(groups):
        span = slice(h * WIDTH, (h + 1) * WIDTH)
        query = to_unit(q_ref[:, span].astype(F32)).astype(BF16)
        mixing = (dot(query, keys_ref[:, span], (1, 1)) * decay[h]).astype(BF16)
        inner = dot(mixing, joined((writes_ref[h], erasers_ref[h])))
        local_ref[h] = inner[:, :WIDTH].astype(BF16)
        decayed = jnp.exp(summed[:, h : h + 1]) * query.astype(F32)
        through_ref[h] = (decayed - inner[:, WIDTH:]).astype(BF16)


def prefixes(blocks):
    two = compose(blocks[1], blocks[0])
    return two, compose(blocks[2], two), compose(compose(blocks[3], blocks[2]), two)


def group_kernel(place, own_ref, recv2_ref, recv3_ref, recv1_ref, before_ref, all_ref, pay_ref, pairs):
    part = place[1]
    pairs[part] = own_ref[...]
    for r, ref in ((1, recv1_ref), (2, recv2_ref), (3, recv3_ref)):
        pairs[part ^ r] = joined(load_payload(ref))
    two, three, total = prefixes([parted(pairs[n]) for n in range(4)])
    store_payload(pay_ref, total)
    all_ref[...] = joined(total)
    before_ref[0] = pairs[0]
    before_ref[1] = joined(two)
    before_ref[2] = joined(three)


def fetch_wide_kernel(token_ref, source_ref, fetched_ref, token_out, sem):
    load = pltpu.make_async_copy(source_ref, fetched_ref, sem)
    load.start()
    token_out[...] = token_ref[...]
    load.wait()


def fetch_kernel(
    place, before_row_ref, before_ref, weight_ref, stream_ref, weight_out, stream_out, maps_ref, sems
):
    width = stream_out.shape[1]
    begin = pl.multiple_of(place[2] * width, width)
    loads = [
        pltpu.make_async_copy(weight_ref, weight_out, sems.at[0]),
        pltpu.make_async_copy(stream_ref.at[:, pl.ds(begin, width)], stream_out, sems.at[1]),
    ]
    for load in loads:
        load.start()
    maps_ref[0] = before_row_ref[...]
    for n in range(3):
        maps_ref[n + 1] = joined(compose(parted(before_ref[n]), parted(before_row_ref[...])))
    for load in loads:
        load.wait()


def row_kernel(place, all_ref, recv2_ref, recv3_ref, recv1_ref, before_ref, pay_ref, pairs, starts):
    group = place[3]
    pairs[group] = all_ref[...]
    for d, ref in ((1, recv1_ref), (2, recv2_ref), (3, recv3_ref)):
        pairs[group ^ d] = joined(load_payload(ref))
    two, three, total = prefixes([parted(pairs[n]) for n in range(4)])
    store_payload(pay_ref, total)
    row, column = iotas(WIDTH, 2 * WIDTH)
    starts[0] = (row == column).astype(F32)
    starts[1] = pairs[0]
    starts[2] = joined(two)
    starts[3] = joined(three)
    before_ref[...] = starts[group]


def state_kernel(
    place, recv2_ref, recv1_ref, recv3_ref, maps_ref, mine_ref, out1_ref, out2_ref, out3_ref, rows, states
):
    part, line = place[1], place[4]
    rows[line] = jnp.zeros(rows.shape[1:], F32)
    for r, ref in ((1, recv1_ref), (2, recv2_ref), (3, recv3_ref)):
        rows[line ^ r] = joined(load_payload(ref))
    state = jnp.where(line > 0, rows[0][:, WIDTH:], 0.0)
    for n in (1, 2):
        state = jnp.where(line > n, apply(parted(rows[n]), state), state)
    for n in range(4):
        states[n] = apply(parted(maps_ref[n]), state).astype(BF16)
    mine_ref[...] = states[part]
    for r, ref in ((1, out1_ref), (2, out2_ref), (3, out3_ref)):
        ref[...] = states[part ^ r]


def out_kernel(
    place, local_ref, through_ref, mine_ref, recv1_ref, recv2_ref, recv3_ref, w_ref, term_ref, *refs
):
    part = place[1]
    me = place[2]
    sent_refs, states = refs[:-1], refs[-1]
    groups = local_ref.shape[0]
    states[part] = mine_ref[...]
    for r, ref in ((1, recv1_ref), (2, recv2_ref), (3, recv3_ref)):
        states[part ^ r] = ref[...]
    normed = []
    for h in range(groups):
        result = local_ref[h].astype(F32) + dot(through_ref[h], states[h])
        normed.append(
            (
                result * lax.rsqrt(jnp.mean(result * result, axis=-1, keepdims=True) + 1e-05)
            ).astype(BF16)
        )
    normed = jnp.concatenate(normed, axis=1)
    width = term_ref.shape[1]
    count = len(sent_refs) + 1
    for r in range(count):
        begin = pl.multiple_of((me ^ r) * width, width)
        term = dot(normed, w_ref[:, pl.ds(begin, width)])
        if r == 0:
            term_ref[...] = term
        else:
            sent_refs[r - 1][...] = term.astype(BF16)


def hidden_kernel(stream_ref, term_ref, *refs):
    total = term_ref[...]
    for ref in refs[:-1]:
        total = total + ref[...].astype(F32)
    refs[-1][...] = (stream_ref[...].astype(F32) + total).astype(BF16)


def own_kernel(place, hidden_ref, w_ref, part_ref):
    width = hidden_ref.shape[1]
    begin = pl.multiple_of(place[2] * width, width)
    part_ref[...] = dot(hidden_ref[...], w_ref[pl.ds(begin, width), :])


def project_kernel(place, w_ref, part_ref, hidden_ref, block2_ref, block1_ref, block3_ref, q_ref, kv_ref):
    me = place[2]
    blocks = [block2_ref, block1_ref, block3_ref]
    rows, width = hidden_ref.shape
    total = part_ref[...]
    for block, r in zip(blocks, (2, 1, 3)):
        begin = pl.multiple_of((me ^ r) * width, width)
        total = total + dot(block[...], w_ref[pl.ds(begin, width), :])
    squares = 0.0
    for ref in [hidden_ref] + blocks:
        value = ref[...].astype(F32)
        squares = squares + jnp.sum(value * value, axis=-1, keepdims=True)
    total = total * lax.rsqrt(squares / (4 * width) + 1e-05)
    groups = width // WIDTH
    for h in range(groups):
        base = h * 3 * WIDTH
        span = slice(h * WIDTH, (h + 1) * WIDTH)
        q_ref[:, span] = to_unit(total[:, base : base + WIDTH]).astype(BF16)
        kv_ref[:, span] = to_unit(total[:, base + WIDTH : base + 2 * WIDTH]).astype(BF16)
        kv_ref[:, (groups + h) * WIDTH : (groups + h + 1) * WIDTH] = total[
            :, base + 2 * WIDTH : base + 3 * WIDTH
        ].astype(BF16)


def window_part(query_place, key_chip, core, q_ref, own_ref, other_ref, sums):
    rows = q_ref.shape[0]
    groups = q_ref.shape[1] // WIDTH
    row, column = iotas(rows, 2 * rows)
    query_place = query_place * rows + row
    own_place = (2 * key_chip + core) * rows + column
    other_place = (2 * key_chip + 1 - core) * rows + column - rows
    key_place = jnp.where(column < rows, own_place, other_place)
    allowed = (key_place <= query_place) & (key_place > query_place - WINDOW) & (key_place >= 0)
    ones = jnp.ones((2 * rows, WIDTH), BF16)
    for h in range(groups):
        span = slice(h * WIDTH, (h + 1) * WIDTH)
        value_span = slice((groups + h) * WIDTH, (groups + h + 1) * WIDTH)
        keys = jnp.concatenate([own_ref[:, span], other_ref[:, span]], axis=0)
        values = jnp.concatenate([own_ref[:, value_span], other_ref[:, value_span]], axis=0)
        scores = SCORE_SCALE * dot(q_ref[:, span], keys, (1, 1))
        weights = jnp.where(allowed, jnp.exp(scores), 0.0).astype(BF16)
        part = dot(weights, jnp.concatenate([values, ones], axis=1))
        sums[h] = part if sums[h] is None else sums[h] + part


def sum_spans(groups):
    return [slice(2 * h * WIDTH, 2 * (h + 1) * WIDTH) for h in range(groups)]


def away_kernel(place, hidden_ref, q_ref, own_ref, other_ref, sums_ref, keep_ref):
    seq = place[0]
    groups = q_ref.shape[1] // WIDTH
    sums = [None] * groups
    window_part(seq + 4, (seq >> 1) - 1, seq & 1, q_ref, own_ref, other_ref, sums)
    for h, span in enumerate(sum_spans(groups)):
        sums_ref[:, span] = sums[h]
    keep_ref[...] = hidden_ref[...]


def back_kernel(place, q_ref, sums_ref, own_ref, other_ref, back_ref):
    seq = place[0]
    rows = q_ref.shape[0]
    groups = q_ref.shape[1] // WIDTH
    sums = [sums_ref[:, span] for span in sum_spans(groups)]
    window_part(seq + 4, (seq >> 1) - 2, seq & 1, q_ref, own_ref, other_ref, sums)
    row, column = iotas(rows, WIDTH)
    line, _ = iotas(16, WIDTH)
    for h in range(groups):
        span = slice(h * WIDTH, (h + 1) * WIDTH)
        back_ref[0:rows, span] = sums[h][:, :WIDTH].astype(BF16)
        total = jnp.sum(jnp.where(row == column, sums[h][:, WIDTH:], 0.0), axis=0, keepdims=True)
        high = total.astype(BF16).astype(F32)
        totals = jnp.where(line == 0, high, jnp.where(line == 1, total - high, 0.0))
        back_ref[rows : rows + 16, span] = totals.astype(BF16)


def home_kernel(place, q_ref, *refs):
    blocks, sums_ref = refs[:-1], refs[-1]
    seq = place[0]
    groups = q_ref.shape[1] // WIDTH
    sums = [None] * groups
    for n in range(len(blocks) // 2):
        window_part(
            seq, (seq >> 1) - n, seq & 1, q_ref, blocks[2 * n], blocks[2 * n + 1], sums
        )
    for h, span in enumerate(sum_spans(groups)):
        sums_ref[:, span] = sums[h]


def last_kernel(sums_ref, back_ref, out_ref):
    groups = out_ref.shape[1] // WIDTH
    rows = out_ref.shape[0]
    row, column = iotas(rows, WIDTH)
    for h in range(groups):
        span = slice(h * WIDTH, (h + 1) * WIDTH)
        line = jnp.sum(back_ref[rows : rows + 16, span].astype(F32), axis=0, keepdims=True)
        far = jnp.sum(jnp.where(row == column, line, 0.0), axis=1, keepdims=True)
        mixed = sums_ref[:, 2 * h * WIDTH : (2 * h + 1) * WIDTH] + back_ref[0:rows, span].astype(F32)
        total = sums_ref[:, (2 * h + 1) * WIDTH : (2 * h + 2) * WIDTH] + far
        out_ref[:, span] = (mixed / total).astype(BF16)


def call(kernel, outs, smem=0, scratch=(), spaces=None, limit=LIMIT):
    def run(*args):
        places = [SMEM] * smem + (spaces or [VMEM] * (len(args) - smem))
        return pl.pallas_call(
            kernel,
            out_shape=[jax.ShapeDtypeStruct(shape, kind) for shape, kind in outs],
            in_specs=[pl.BlockSpec(memory_space=place) for place in places],
            out_specs=[pl.BlockSpec(memory_space=VMEM)] * len(outs),
            scratch_shapes=list(scratch),
            compiler_params=pltpu.CompilerParams(vmem_limit_bytes=limit),
        )(*args)

    return run


def moved(array, axis, distance):
    size = lax.axis_size(axis)
    return lax.ppermute(
        array, axis, [(i, i + distance) for i in range(size) if 0 <= i + distance < size]
    )


def crossed(array, mask, axis="seq"):
    return lax.ppermute(array, axis, [(i, i ^ mask) for i in range(lax.axis_size(axis))])


def body(queries, keys, values, gate_log, beta, stream, w_out, w_qkv):
    rows, wide = queries.shape
    groups = gate_log.shape[1]
    seq = lax.axis_index("seq")
    head = lax.axis_index("head")
    heads = lax.axis_size("head")
    place = jnp.stack([seq, seq & 3, head, (seq >> 2) & 3, seq >> 4]).astype(jnp.int32)
    pair_shape = ((WIDTH, 2 * WIDTH), F32)
    pay_shape = ((WIDTH + 16, 2 * WIDTH), BF16)
    state_shape = ((WIDTH, WIDTH), BF16)
    row_shape = ((rows, wide), BF16)
    four_pairs = pltpu.VMEM((4, WIDTH, 2 * WIDTH), F32)
    four_states = pltpu.VMEM((4, WIDTH, WIDTH), BF16)

    gates = jnp.concatenate([gate_log.T, beta.T], axis=0)
    unit_keys, writes, erasers, own, pay1, pay2, pay3 = call(
        map_kernel,
        [row_shape] + [((groups, rows, WIDTH), BF16)] * 2 + [pair_shape] + [pay_shape] * 3,
        1,
        [pltpu.VMEM((rows, wide), BF16)] * 2 + [four_pairs, pltpu.SemaphoreType.DMA((2,))],
        [VMEM] + [pltpu.HBM] * 2,
        CHUNK_LIMIT,
    )(place, gates, keys, values)
    pay2, pay3, pay1 = crossed(pay2, 2), crossed(pay3, 3), crossed(pay1, 1)
    local, through = call(query_kernel, [((groups, rows, WIDTH), BF16)] * 2)(
        gates, queries, unit_keys, writes, erasers
    )
    own, local, through = lax.optimization_barrier((own, local, through))
    before, everything, pay = call(
        group_kernel, [((3, WIDTH, 2 * WIDTH), F32), pair_shape, pay_shape], 1, [four_pairs]
    )(place, own, pay2, pay3, pay1)
    row2, row3, row1 = [crossed(pay, 4 * d) for d in (2, 3, 1)]
    everything, w_qkv = lax.optimization_barrier((everything, w_qkv))
    w_qkv, everything = call(
        fetch_wide_kernel,
        [(w_qkv.shape, BF16), pair_shape],
        0,
        [pltpu.SemaphoreType.DMA],
        [VMEM, pltpu.HBM],
        FETCH_LIMIT,
    )(everything, w_qkv)
    before_row, pay = call(row_kernel, [pair_shape, pay_shape], 1, [four_pairs] * 2)(
        place, everything, row2, row3, row1
    )
    row2, row1, row3 = [crossed(pay, 16 * d) for d in (2, 1, 3)]
    before_row, w_out, stream = lax.optimization_barrier((before_row, w_out, stream))
    w_out, stream, maps = call(
        fetch_kernel,
        [(w_out.shape, BF16), row_shape, ((4, WIDTH, 2 * WIDTH), F32)],
        1,
        [pltpu.SemaphoreType.DMA((2,))],
        [VMEM, VMEM, pltpu.HBM, pltpu.HBM],
        FETCH_LIMIT,
    )(place, before_row, before, w_out, stream)
    mine, out1, out2, out3 = call(state_kernel, [state_shape] * 4, 1, [four_pairs, four_states])(
        place, row2, row1, row3, maps
    )
    terms = call(
        out_kernel,
        [((rows, wide), F32)] + [row_shape] * (heads - 1),
        1,
        [four_states],
    )(
        place,
        local,
        through,
        mine,
        crossed(out1, 1),
        crossed(out2, 2),
        crossed(out3, 3),
        w_out,
    )
    received = [crossed(terms[r], r, "head") for r in (2, 1, 3)]
    (hidden,) = call(hidden_kernel, [row_shape])(stream, terms[0], *received)
    other2, other1, other3 = [crossed(hidden, r, "head") for r in (2, 1, 3)]
    (part,) = call(own_kernel, [((rows, w_qkv.shape[1]), F32)], 1)(place, hidden, w_qkv)
    unit_queries, pack = call(project_kernel, [row_shape, ((rows, 2 * wide), BF16)], 1)(
        place, w_qkv, part, hidden, other2, other1, other3
    )
    first, visitors = moved(pack, "seq", 2), moved(unit_queries, "seq", -2)
    second, visitors = lax.optimization_barrier(
        (moved(first, "seq", 2), moved(visitors, "seq", -2))
    )
    home = [
        pack, crossed(pack, 1), first, crossed(first, 1), second, crossed(second, 1)
    ]
    sums_shape = ((rows, 2 * wide), F32)
    away, kept = call(away_kernel, [sums_shape, row_shape], 1)(
        place, hidden, visitors, home[2], home[3]
    )
    (back,) = call(back_kernel, [((rows + 16, wide), BF16)], 1)(
        place, visitors, away, home[4], home[5]
    )
    returned = moved(back, "seq", 4)
    (sums,) = call(home_kernel, [((rows, 2 * wide), F32)], 1)(place, unit_queries, *home)
    (attended,) = call(last_kernel, [row_shape])(sums, returned)
    return (kept, attended)


def solution(mesh):
    in_specs = (
        P("seq", "head"),
        P("seq", "head"),
        P("seq", "head"),
        P("seq", "head"),
        P("seq", "head"),
        P("seq", None),
        P("head", None),
        P(None, "head"),
    )
    out_specs = (P("seq", "head"), P("seq", "head"))
    return jax.shard_map(body, mesh=mesh, in_specs=in_specs, out_specs=out_specs, check_vma=False)
```

```python
import functools

import jax
import jax.numpy as jnp
from jax import lax
from jax.experimental import pallas as pl
from jax.experimental.pallas import tpu as pltpu
from jax.sharding import PartitionSpec as P

WINDOW = 1024
WIDTH = 128
SCORE_SCALE = 10.0
F32 = jnp.float32
BF16 = jnp.bfloat16
HIGHEST = lax.Precision.HIGHEST
VMEM = pltpu.VMEM
SMEM = pltpu.SMEM
LIMIT = 16 * 1024 * 1024
FETCH_LIMIT = 44 * 1024 * 1024
CHUNK_LIMIT = 54448 * 1024


def dot(left, right, contract=(1, 0), precision=None):
    return lax.dot_general(
        left,
        right,
        (((contract[0],), (contract[1],)), ((), ())),
        precision=precision,
        preferred_element_type=F32,
    )


def exact(left, right, contract=(1, 0)):
    return dot(left, right, contract, HIGHEST)


def iotas(rows, columns):
    return (
        lax.broadcasted_iota(jnp.int32, (rows, columns), 0),
        lax.broadcasted_iota(jnp.int32, (rows, columns), 1),
    )


def fine(left, right):
    left_high = left.astype(BF16)
    right_high = right.astype(BF16)
    left_low = (left - left_high.astype(F32)).astype(BF16)
    right_low = (right - right_high.astype(F32)).astype(BF16)
    wide = right.shape[1]
    both = dot(left_high, jnp.concatenate([right_high, right_low], axis=1))
    return both[:, :wide] + both[:, wide:] + dot(left_low, right_high)


def split_diagonal(matrix):
    row, column = iotas(WIDTH, WIDTH)
    high = matrix.astype(BF16)
    return high, jnp.where(row == column, matrix - high.astype(F32), 0.0)


def compose(left, right):
    left_t, left_o = left
    right_t, right_o = right
    left_high, left_rest = split_diagonal(left_t)
    right_high, right_rest = split_diagonal(right_t)
    left_column = jnp.sum(left_rest, axis=1, keepdims=True)
    right_row = jnp.sum(right_rest, axis=0, keepdims=True)
    offset = dot(left_high, right_o.astype(BF16)) + left_column * right_o + left_o
    product = dot(left_high, right_high) + left_column * right_t + left_high.astype(F32) * right_row
    return product, offset


def apply(left, state):
    left_t, left_o = left
    left_high, left_rest = split_diagonal(left_t)
    left_column = jnp.sum(left_rest, axis=1, keepdims=True)
    return dot(left_high, state.astype(BF16)) + left_column * state + left_o


def store_payload(ref, pair):
    row, _ = iotas(16, 2 * WIDTH)
    transition, offset = pair
    high, rest = split_diagonal(transition)
    ref[0:WIDTH, 0:WIDTH] = high
    ref[0:WIDTH, WIDTH : 2 * WIDTH] = offset.astype(BF16)
    line = jnp.sum(rest, axis=0, keepdims=True)
    line = jnp.concatenate([line, jnp.zeros_like(line)], axis=1)
    ref[WIDTH : WIDTH + 16, :] = jnp.where(row == 0, line, 0.0).astype(BF16)


def load_payload(ref):
    row, column = iotas(WIDTH, WIDTH)
    line = ref[WIDTH : WIDTH + 16, 0:WIDTH].astype(F32)
    line = jnp.sum(line, axis=0, keepdims=True)
    transition = ref[0:WIDTH, 0:WIDTH].astype(F32)
    transition = transition + jnp.where(row == column, line, 0.0)
    return transition, ref[0:WIDTH, WIDTH : 2 * WIDTH].astype(F32)


def joined(pair):
    return jnp.concatenate(pair, axis=1)


def parted(array):
    return array[:, :WIDTH], array[:, WIDTH:]


def to_unit(vectors):
    return vectors * lax.rsqrt(jnp.sum(vectors * vectors, axis=-1, keepdims=True) + 1e-06)


def lower_inverses(couplings):
    rows = couplings[0].shape[0]
    row, column = iotas(rows, rows)
    identity = (row == column).astype(F32)
    inside = (row >> 3) == (column >> 3)
    powers = [jnp.where(inside, c, 0.0) for c in couplings]
    results = [identity - p for p in powers]
    span = 2
    while span < 8:
        powers = [fine(p, p) for p in powers]
        results = [fine(r, identity + p) for r, p in zip(results, powers)]
        span *= 2
    shift = 3
    while (1 << shift) < rows:
        level = ((row >> (shift + 1)) == (column >> (shift + 1))) & ((row >> shift) > (column >> shift))
        crossing = [fine(r, jnp.where(level, c, 0.0)) for r, c in zip(results, couplings)]
        results = [r - fine(x, r) for r, x in zip(results, crossing)]
        shift += 1
    return results


def decays(gb_ref):
    rows = gb_ref.shape[1]
    groups = gb_ref.shape[0] // 2
    row, column = iotas(rows, rows)
    both = gb_ref[...]
    high = both.astype(BF16)
    rest = both - high.astype(F32)
    middle = rest.astype(BF16)
    low = (rest - middle.astype(F32)).astype(BF16)
    sums = dot(jnp.concatenate([high, middle, low], axis=0), (row <= column).astype(BF16))
    count = 2 * groups
    summed_row = sums[:count] + sums[count : 2 * count] + sums[2 * count :]
    columns = jnp.concatenate([summed_row[:groups], both[groups:]], axis=0).T
    causal = row >= column
    spreads = [columns[:, h : h + 1] - summed_row[h : h + 1, :] for h in range(groups)]
    return columns, [
        jnp.where(causal, jnp.exp(jnp.where(causal, spread, 0.0)), 0.0) for spread in spreads
    ]


def map_kernel(
    place, gb_ref, k_hbm, v_hbm, keys_ref, writes_ref, erasers_ref, own_ref, pay1_ref, pay2_ref, pay3_ref, k_ref, v_ref, pairs, sems
):
    part = place[1]
    rows = gb_ref.shape[1]
    groups = gb_ref.shape[0] // 2
    loads = [
        pltpu.make_async_copy(k_hbm, k_ref, sems.at[0]),
        pltpu.make_async_copy(v_hbm, v_ref, sems.at[1]),
    ]
    for load in loads:
        load.start()
    row, column = iotas(rows, rows)
    summed, decay = decays(gb_ref)
    betas = summed[:, groups:]
    loads[0].wait()
    keys, couplings = [], []
    for h in range(groups):
        span = slice(h * WIDTH, (h + 1) * WIDTH)
        key = to_unit(k_ref[:, span].astype(F32)).astype(BF16)
        keys_ref[:, span] = key
        both = dot(key, key, (1, 1))
        couplings.append(jnp.where(row > column, betas[:, h : h + 1] * decay[h] * both, 0.0))
        keys.append(key.astype(F32))
    inverses = lower_inverses(couplings)
    loads[1].wait()
    for h in range(groups):
        span = slice(h * WIDTH, (h + 1) * WIDTH)
        along = summed[:, h : h + 1]
        last = summed[rows - 1 : rows, h : h + 1]
        beta = betas[:, h : h + 1]
        value = v_ref[:, span].astype(F32)
        made = fine(
            inverses[h],
            jnp.concatenate([beta * value, (beta * jnp.exp(along)) * keys[h]], axis=1),
        ).astype(BF16)
        writes_ref[h], erasers_ref[h] = parted(made)
        ended = (jnp.exp(last - along) * keys[h]).astype(BF16)
        effect = dot(ended, made, (0, 0))
        identity = iotas(WIDTH, WIDTH)
        kept = jnp.where(identity[0] == identity[1], jnp.exp(last), 0.0)
        pairs[h, :, 0:WIDTH] = kept - effect[:, WIDTH:]
        pairs[h, :, WIDTH:] = effect[:, :WIDTH]
    own_ref[...] = pairs[part]
    for r, ref in ((1, pay1_ref), (2, pay2_ref), (3, pay3_ref)):
        store_payload(ref, parted(pairs[part ^ r]))


def query_kernel(gb_ref, q_ref, keys_ref, writes_ref, erasers_ref, local_ref, through_ref):
    groups = gb_ref.shape[0] // 2
    summed, decay = decays(gb_ref)
    for h in range(groups):
        span = slice(h * WIDTH, (h + 1) * WIDTH)
        query = to_unit(q_ref[:, span].astype(F32)).astype(BF16)
        mixing = (dot(query, keys_ref[:, span], (1, 1)) * decay[h]).astype(BF16)
        inner = dot(mixing, joined((writes_ref[h], erasers_ref[h])))
        local_ref[h] = inner[:, :WIDTH].astype(BF16)
        decayed = jnp.exp(summed[:, h : h + 1]) * query.astype(F32)
        through_ref[h] = (decayed - inner[:, WIDTH:]).astype(BF16)


def prefixes(blocks):
    two = compose(blocks[1], blocks[0])
    return two, compose(blocks[2], two), compose(compose(blocks[3], blocks[2]), two)


def group_kernel(place, own_ref, recv2_ref, recv3_ref, recv1_ref, before_ref, all_ref, pay_ref, pairs):
    part = place[1]
    pairs[part] = own_ref[...]
    for r, ref in ((1, recv1_ref), (2, recv2_ref), (3, recv3_ref)):
        pairs[part ^ r] = joined(load_payload(ref))
    two, three, total = prefixes([parted(pairs[n]) for n in range(4)])
    store_payload(pay_ref, total)
    all_ref[...] = joined(total)
    before_ref[0] = pairs[0]
    before_ref[1] = joined(two)
    before_ref[2] = joined(three)


def fetch_wide_kernel(token_ref, source_ref, fetched_ref, token_out, sem):
    load = pltpu.make_async_copy(source_ref, fetched_ref, sem)
    load.start()
    token_out[...] = token_ref[...]
    load.wait()


def fetch_kernel(
    place, before_row_ref, before_ref, weight_ref, stream_ref, weight_out, stream_out, maps_ref, sems
):
    width = stream_out.shape[1]
    begin = pl.multiple_of(place[2] * width, width)
    loads = [
        pltpu.make_async_copy(weight_ref, weight_out, sems.at[0]),
        pltpu.make_async_copy(stream_ref.at[:, pl.ds(begin, width)], stream_out, sems.at[1]),
    ]
    for load in loads:
        load.start()
    maps_ref[0] = before_row_ref[...]
    for n in range(3):
        maps_ref[n + 1] = joined(compose(parted(before_ref[n]), parted(before_row_ref[...])))
    for load in loads:
        load.wait()


def row_kernel(place, all_ref, recv2_ref, recv3_ref, recv1_ref, before_ref, pay_ref, pairs, starts):
    group = place[3]
    pairs[group] = all_ref[...]
    for d, ref in ((1, recv1_ref), (2, recv2_ref), (3, recv3_ref)):
        pairs[group ^ d] = joined(load_payload(ref))
    two, three, total = prefixes([parted(pairs[n]) for n in range(4)])
    store_payload(pay_ref, total)
    row, column = iotas(WIDTH, 2 * WIDTH)
    starts[0] = (row == column).astype(F32)
    starts[1] = pairs[0]
    starts[2] = joined(two)
    starts[3] = joined(three)
    before_ref[...] = starts[group]


def state_kernel(
    place, recv2_ref, recv1_ref, recv3_ref, maps_ref, mine_ref, out1_ref, out2_ref, out3_ref, rows, states
):
    part, line = place[1], place[4]
    rows[line] = jnp.zeros(rows.shape[1:], F32)
    for r, ref in ((1, recv1_ref), (2, recv2_ref), (3, recv3_ref)):
        rows[line ^ r] = joined(load_payload(ref))
    state = jnp.where(line > 0, rows[0][:, WIDTH:], 0.0)
    for n in (1, 2):
        state = jnp.where(line > n, apply(parted(rows[n]), state), state)
    for n in range(4):
        states[n] = apply(parted(maps_ref[n]), state).astype(BF16)
    mine_ref[...] = states[part]
    for r, ref in ((1, out1_ref), (2, out2_ref), (3, out3_ref)):
        ref[...] = states[part ^ r]


def out_kernel(
    place, local_ref, through_ref, mine_ref, recv1_ref, recv3_ref, recv2_ref, w_ref, term_ref, *refs
):
    part = place[1]
    me = place[2]
    sent_refs, states = refs[:-1], refs[-1]
    groups = local_ref.shape[0]
    states[part] = mine_ref[...]
    for r, ref in ((1, recv1_ref), (2, recv2_ref), (3, recv3_ref)):
        states[part ^ r] = ref[...]
    normed = []
    for h in range(groups):
        result = local_ref[h].astype(F32) + dot(through_ref[h], states[h])
        normed.append(
            (
                result * lax.rsqrt(jnp.mean(result * result, axis=-1, keepdims=True) + 1e-05)
            ).astype(BF16)
        )
    normed = jnp.concatenate(normed, axis=1)
    width = term_ref.shape[1]
    count = len(sent_refs) + 1
    for r in range(count):
        begin = pl.multiple_of((me ^ r) * width, width)
        term = dot(normed, w_ref[:, pl.ds(begin, width)])
        if r == 0:
            term_ref[...] = term
        else:
            sent_refs[r - 1][...] = term.astype(BF16)


def hidden_kernel(stream_ref, term_ref, *refs):
    total = term_ref[...]
    for ref in refs[:-1]:
        total = total + ref[...].astype(F32)
    refs[-1][...] = (stream_ref[...].astype(F32) + total).astype(BF16)


def own_kernel(place, hidden_ref, w_ref, part_ref):
    width = hidden_ref.shape[1]
    begin = pl.multiple_of(place[2] * width, width)
    part_ref[...] = dot(hidden_ref[...], w_ref[pl.ds(begin, width), :])


def project_kernel(place, w_ref, part_ref, hidden_ref, block2_ref, block1_ref, block3_ref, q_ref, kv_ref):
    me = place[2]
    blocks = [block2_ref, block1_ref, block3_ref]
    rows, width = hidden_ref.shape
    total = part_ref[...]
    for block, r in zip(blocks, (2, 1, 3)):
        begin = pl.multiple_of((me ^ r) * width, width)
        total = total + dot(block[...], w_ref[pl.ds(begin, width), :])
    squares = 0.0
    for ref in [hidden_ref] + blocks:
        value = ref[...].astype(F32)
        squares = squares + jnp.sum(value * value, axis=-1, keepdims=True)
    total = total * lax.rsqrt(squares / (4 * width) + 1e-05)
    groups = width // WIDTH
    for h in range(groups):
        base = h * 3 * WIDTH
        span = slice(h * WIDTH, (h + 1) * WIDTH)
        q_ref[:, span] = to_unit(total[:, base : base + WIDTH]).astype(BF16)
        kv_ref[:, span] = to_unit(total[:, base + WIDTH : base + 2 * WIDTH]).astype(BF16)
        kv_ref[:, (groups + h) * WIDTH : (groups + h + 1) * WIDTH] = total[
            :, base + 2 * WIDTH : base + 3 * WIDTH
        ].astype(BF16)


def window_part(query_place, key_chip, core, q_ref, own_ref, other_ref, sums):
    rows = q_ref.shape[0]
    groups = q_ref.shape[1] // WIDTH
    row, column = iotas(rows, 2 * rows)
    query_place = query_place * rows + row
    own_place = (2 * key_chip + core) * rows + column
    other_place = (2 * key_chip + 1 - core) * rows + column - rows
    key_place = jnp.where(column < rows, own_place, other_place)
    allowed = (key_place <= query_place) & (key_place > query_place - WINDOW) & (key_place >= 0)
    ones = jnp.ones((2 * rows, WIDTH), BF16)
    for h in range(groups):
        span = slice(h * WIDTH, (h + 1) * WIDTH)
        value_span = slice((groups + h) * WIDTH, (groups + h + 1) * WIDTH)
        keys = jnp.concatenate([own_ref[:, span], other_ref[:, span]], axis=0)
        values = jnp.concatenate([own_ref[:, value_span], other_ref[:, value_span]], axis=0)
        scores = SCORE_SCALE * dot(q_ref[:, span], keys, (1, 1))
        weights = jnp.where(allowed, jnp.exp(scores), 0.0).astype(BF16)
        part = dot(weights, jnp.concatenate([values, ones], axis=1))
        sums[h] = part if sums[h] is None else sums[h] + part


def sum_spans(groups):
    return [slice(2 * h * WIDTH, 2 * (h + 1) * WIDTH) for h in range(groups)]


def away_kernel(place, hidden_ref, q_ref, own_ref, other_ref, sums_ref, keep_ref):
    seq = place[0]
    groups = q_ref.shape[1] // WIDTH
    sums = [None] * groups
    window_part(seq + 4, (seq >> 1) - 1, seq & 1, q_ref, own_ref, other_ref, sums)
    for h, span in enumerate(sum_spans(groups)):
        sums_ref[:, span] = sums[h]
    keep_ref[...] = hidden_ref[...]


def back_kernel(place, q_ref, sums_ref, own_ref, other_ref, back_ref):
    seq = place[0]
    rows = q_ref.shape[0]
    groups = q_ref.shape[1] // WIDTH
    sums = [sums_ref[:, span] for span in sum_spans(groups)]
    window_part(seq + 4, (seq >> 1) - 2, seq & 1, q_ref, own_ref, other_ref, sums)
    row, column = iotas(rows, WIDTH)
    line, _ = iotas(16, WIDTH)
    for h in range(groups):
        span = slice(h * WIDTH, (h + 1) * WIDTH)
        back_ref[0:rows, span] = sums[h][:, :WIDTH].astype(BF16)
        total = jnp.sum(jnp.where(row == column, sums[h][:, WIDTH:], 0.0), axis=0, keepdims=True)
        high = total.astype(BF16).astype(F32)
        totals = jnp.where(line == 0, high, jnp.where(line == 1, total - high, 0.0))
        back_ref[rows : rows + 16, span] = totals.astype(BF16)


def home_kernel(place, q_ref, *refs):
    blocks, sums_ref = refs[:-1], refs[-1]
    seq = place[0]
    groups = q_ref.shape[1] // WIDTH
    sums = [None] * groups
    for n in range(len(blocks) // 2):
        window_part(
            seq, (seq >> 1) - n, seq & 1, q_ref, blocks[2 * n], blocks[2 * n + 1], sums
        )
    for h, span in enumerate(sum_spans(groups)):
        sums_ref[:, span] = sums[h]


def last_kernel(sums_ref, back_ref, out_ref):
    groups = out_ref.shape[1] // WIDTH
    rows = out_ref.shape[0]
    row, column = iotas(rows, WIDTH)
    for h in range(groups):
        span = slice(h * WIDTH, (h + 1) * WIDTH)
        line = jnp.sum(back_ref[rows : rows + 16, span].astype(F32), axis=0, keepdims=True)
        far = jnp.sum(jnp.where(row == column, line, 0.0), axis=1, keepdims=True)
        mixed = sums_ref[:, 2 * h * WIDTH : (2 * h + 1) * WIDTH] + back_ref[0:rows, span].astype(F32)
        total = sums_ref[:, (2 * h + 1) * WIDTH : (2 * h + 2) * WIDTH] + far
        out_ref[:, span] = (mixed / total).astype(BF16)


def call(kernel, outs, smem=0, scratch=(), spaces=None, limit=LIMIT):
    def run(*args):
        places = [SMEM] * smem + (spaces or [VMEM] * (len(args) - smem))
        return pl.pallas_call(
            kernel,
            out_shape=[jax.ShapeDtypeStruct(shape, kind) for shape, kind in outs],
            in_specs=[pl.BlockSpec(memory_space=place) for place in places],
            out_specs=[pl.BlockSpec(memory_space=VMEM)] * len(outs),
            scratch_shapes=list(scratch),
            compiler_params=pltpu.CompilerParams(vmem_limit_bytes=limit),
        )(*args)

    return run


def moved(array, axis, distance):
    size = lax.axis_size(axis)
    return lax.ppermute(
        array, axis, [(i, i + distance) for i in range(size) if 0 <= i + distance < size]
    )


def crossed(array, mask, axis="seq"):
    return lax.ppermute(array, axis, [(i, i ^ mask) for i in range(lax.axis_size(axis))])


def body(queries, keys, values, gate_log, beta, stream, w_out, w_qkv):
    rows, wide = queries.shape
    groups = gate_log.shape[1]
    seq = lax.axis_index("seq")
    head = lax.axis_index("head")
    heads = lax.axis_size("head")
    place = jnp.stack([seq, seq & 3, head, (seq >> 2) & 3, seq >> 4]).astype(jnp.int32)
    pair_shape = ((WIDTH, 2 * WIDTH), F32)
    pay_shape = ((WIDTH + 16, 2 * WIDTH), BF16)
    state_shape = ((WIDTH, WIDTH), BF16)
    row_shape = ((rows, wide), BF16)
    four_pairs = pltpu.VMEM((4, WIDTH, 2 * WIDTH), F32)
    four_states = pltpu.VMEM((4, WIDTH, WIDTH), BF16)

    gates = jnp.concatenate([gate_log.T, beta.T], axis=0)
    unit_keys, writes, erasers, own, pay1, pay2, pay3 = call(
        map_kernel,
        [row_shape] + [((groups, rows, WIDTH), BF16)] * 2 + [pair_shape] + [pay_shape] * 3,
        1,
        [pltpu.VMEM((rows, wide), BF16)] * 2 + [four_pairs, pltpu.SemaphoreType.DMA((2,))],
        [VMEM] + [pltpu.HBM] * 2,
        CHUNK_LIMIT,
    )(place, gates, keys, values)
    pay2, pay3, pay1 = crossed(pay2, 2), crossed(pay3, 3), crossed(pay1, 1)
    local, through = call(query_kernel, [((groups, rows, WIDTH), BF16)] * 2)(
        gates, queries, unit_keys, writes, erasers
    )
    own, local, through = lax.optimization_barrier((own, local, through))
    before, everything, pay = call(
        group_kernel, [((3, WIDTH, 2 * WIDTH), F32), pair_shape, pay_shape], 1, [four_pairs]
    )(place, own, pay2, pay3, pay1)
    row2, row3, row1 = [crossed(pay, 4 * d) for d in (2, 3, 1)]
    everything, w_qkv = lax.optimization_barrier((everything, w_qkv))
    w_qkv, everything = call(
        fetch_wide_kernel,
        [(w_qkv.shape, BF16), pair_shape],
        0,
        [pltpu.SemaphoreType.DMA],
        [VMEM, pltpu.HBM],
        FETCH_LIMIT,
    )(everything, w_qkv)
    before_row, pay = call(row_kernel, [pair_shape, pay_shape], 1, [four_pairs] * 2)(
        place, everything, row2, row3, row1
    )
    row2, row1, row3 = [crossed(pay, 16 * d) for d in (2, 1, 3)]
    before_row, w_out, stream = lax.optimization_barrier((before_row, w_out, stream))
    w_out, stream, maps = call(
        fetch_kernel,
        [(w_out.shape, BF16), row_shape, ((4, WIDTH, 2 * WIDTH), F32)],
        1,
        [pltpu.SemaphoreType.DMA((2,))],
        [VMEM, VMEM, pltpu.HBM, pltpu.HBM],
        FETCH_LIMIT,
    )(place, before_row, before, w_out, stream)
    mine, out1, out2, out3 = call(state_kernel, [state_shape] * 4, 1, [four_pairs, four_states])(
        place, row2, row1, row3, maps
    )
    terms = call(
        out_kernel,
        [((rows, wide), F32)] + [row_shape] * (heads - 1),
        1,
        [four_states],
    )(
        place,
        local,
        through,
        mine,
        crossed(out1, 1),
        crossed(out3, 3),
        crossed(out2, 2),
        w_out,
    )
    received = [crossed(terms[r], r, "head") for r in (2, 1, 3)]
    (hidden,) = call(hidden_kernel, [row_shape])(stream, terms[0], *received)
    other2, other1, other3 = [crossed(hidden, r, "head") for r in (2, 1, 3)]
    (part,) = call(own_kernel, [((rows, w_qkv.shape[1]), F32)], 1)(place, hidden, w_qkv)
    unit_queries, pack = call(project_kernel, [row_shape, ((rows, 2 * wide), BF16)], 1)(
        place, w_qkv, part, hidden, other2, other1, other3
    )
    first, visitors = lax.optimization_barrier(
        (moved(pack, "seq", 2), moved(unit_queries, "seq", -2))
    )
    second, visitors = lax.optimization_barrier(
        (moved(first, "seq", 2), moved(visitors, "seq", -2))
    )
    home = [
        pack, crossed(pack, 1), first, crossed(first, 1), second, crossed(second, 1)
    ]
    sums_shape = ((rows, 2 * wide), F32)
    away, kept = call(away_kernel, [sums_shape, row_shape], 1)(
        place, hidden, visitors, home[2], home[3]
    )
    (back,) = call(back_kernel, [((rows + 16, wide), BF16)], 1)(
        place, visitors, away, home[4], home[5]
    )
    returned = moved(back, "seq", 4)
    (sums,) = call(home_kernel, [((rows, 2 * wide), F32)], 1)(place, unit_queries, *home)
    (attended,) = call(last_kernel, [row_shape])(sums, returned)
    return (kept, attended)


def solution(mesh):
    in_specs = (
        P("seq", "head"),
        P("seq", "head"),
        P("seq", "head"),
        P("seq", "head"),
        P("seq", "head"),
        P("seq", None),
        P("head", None),
        P(None, "head"),
    )
    out_specs = (P("seq", "head"), P("seq", "head"))
    return jax.shard_map(body, mesh=mesh, in_specs=in_specs, out_specs=out_specs, check_vma=False)
```

```python
import functools

import jax
import jax.numpy as jnp
from jax import lax
from jax.experimental import pallas as pl
from jax.experimental.pallas import tpu as pltpu
from jax.sharding import PartitionSpec as P

WINDOW = 1024
WIDTH = 128
SCORE_SCALE = 10.0
F32 = jnp.float32
BF16 = jnp.bfloat16
HIGHEST = lax.Precision.HIGHEST
VMEM = pltpu.VMEM
SMEM = pltpu.SMEM
LIMIT = 16 * 1024 * 1024
FETCH_LIMIT = 44 * 1024 * 1024
CHUNK_LIMIT = 54448 * 1024


def dot(left, right, contract=(1, 0), precision=None):
    return lax.dot_general(
        left,
        right,
        (((contract[0],), (contract[1],)), ((), ())),
        precision=precision,
        preferred_element_type=F32,
    )


def exact(left, right, contract=(1, 0)):
    return dot(left, right, contract, HIGHEST)


def iotas(rows, columns):
    return (
        lax.broadcasted_iota(jnp.int32, (rows, columns), 0),
        lax.broadcasted_iota(jnp.int32, (rows, columns), 1),
    )


def fine(left, right):
    left_high = left.astype(BF16)
    right_high = right.astype(BF16)
    left_low = (left - left_high.astype(F32)).astype(BF16)
    right_low = (right - right_high.astype(F32)).astype(BF16)
    wide = right.shape[1]
    both = dot(left_high, jnp.concatenate([right_high, right_low], axis=1))
    return both[:, :wide] + both[:, wide:] + dot(left_low, right_high)


def split_diagonal(matrix):
    row, column = iotas(WIDTH, WIDTH)
    high = matrix.astype(BF16)
    return high, jnp.where(row == column, matrix - high.astype(F32), 0.0)


def compose(left, right):
    left_t, left_o = left
    right_t, right_o = right
    left_high, left_rest = split_diagonal(left_t)
    right_high, right_rest = split_diagonal(right_t)
    left_column = jnp.sum(left_rest, axis=1, keepdims=True)
    right_row = jnp.sum(right_rest, axis=0, keepdims=True)
    offset = dot(left_high, right_o.astype(BF16)) + left_column * right_o + left_o
    product = dot(left_high, right_high) + left_column * right_t + left_high.astype(F32) * right_row
    return product, offset


def apply(left, state):
    left_t, left_o = left
    left_high, left_rest = split_diagonal(left_t)
    left_column = jnp.sum(left_rest, axis=1, keepdims=True)
    return dot(left_high, state.astype(BF16)) + left_column * state + left_o


def store_payload(ref, pair):
    row, _ = iotas(16, 2 * WIDTH)
    transition, offset = pair
    high, rest = split_diagonal(transition)
    ref[0:WIDTH, 0:WIDTH] = high
    ref[0:WIDTH, WIDTH : 2 * WIDTH] = offset.astype(BF16)
    line = jnp.sum(rest, axis=0, keepdims=True)
    line = jnp.concatenate([line, jnp.zeros_like(line)], axis=1)
    ref[WIDTH : WIDTH + 16, :] = jnp.where(row == 0, line, 0.0).astype(BF16)


def load_payload(ref):
    row, column = iotas(WIDTH, WIDTH)
    line = ref[WIDTH : WIDTH + 16, 0:WIDTH].astype(F32)
    line = jnp.sum(line, axis=0, keepdims=True)
    transition = ref[0:WIDTH, 0:WIDTH].astype(F32)
    transition = transition + jnp.where(row == column, line, 0.0)
    return transition, ref[0:WIDTH, WIDTH : 2 * WIDTH].astype(F32)


def joined(pair):
    return jnp.concatenate(pair, axis=1)


def parted(array):
    return array[:, :WIDTH], array[:, WIDTH:]


def to_unit(vectors):
    return vectors * lax.rsqrt(jnp.sum(vectors * vectors, axis=-1, keepdims=True) + 1e-06)


def lower_inverses(couplings):
    rows = couplings[0].shape[0]
    row, column = iotas(rows, rows)
    identity = (row == column).astype(F32)
    inside = (row >> 3) == (column >> 3)
    powers = [jnp.where(inside, c, 0.0) for c in couplings]
    results = [identity - p for p in powers]
    span = 2
    while span < 8:
        powers = [fine(p, p) for p in powers]
        results = [fine(r, identity + p) for r, p in zip(results, powers)]
        span *= 2
    shift = 3
    while (1 << shift) < rows:
        level = ((row >> (shift + 1)) == (column >> (shift + 1))) & ((row >> shift) > (column >> shift))
        crossing = [fine(r, jnp.where(level, c, 0.0)) for r, c in zip(results, couplings)]
        results = [r - fine(x, r) for r, x in zip(results, crossing)]
        shift += 1
    return results


def decays(gb_ref):
    rows = gb_ref.shape[1]
    groups = gb_ref.shape[0] // 2
    row, column = iotas(rows, rows)
    both = gb_ref[...]
    high = both.astype(BF16)
    rest = both - high.astype(F32)
    middle = rest.astype(BF16)
    low = (rest - middle.astype(F32)).astype(BF16)
    sums = dot(jnp.concatenate([high, middle, low], axis=0), (row <= column).astype(BF16))
    count = 2 * groups
    summed_row = sums[:count] + sums[count : 2 * count] + sums[2 * count :]
    columns = jnp.concatenate([summed_row[:groups], both[groups:]], axis=0).T
    causal = row >= column
    spreads = [columns[:, h : h + 1] - summed_row[h : h + 1, :] for h in range(groups)]
    return columns, [
        jnp.where(causal, jnp.exp(jnp.where(causal, spread, 0.0)), 0.0) for spread in spreads
    ]


def map_kernel(
    place, gb_ref, k_hbm, v_hbm, keys_ref, writes_ref, erasers_ref, own_ref, pay1_ref, pay2_ref, pay3_ref, k_ref, v_ref, pairs, sems
):
    part = place[1]
    rows = gb_ref.shape[1]
    groups = gb_ref.shape[0] // 2
    loads = [
        pltpu.make_async_copy(k_hbm, k_ref, sems.at[0]),
        pltpu.make_async_copy(v_hbm, v_ref, sems.at[1]),
    ]
    for load in loads:
        load.start()
    row, column = iotas(rows, rows)
    summed, decay = decays(gb_ref)
    betas = summed[:, groups:]
    loads[0].wait()
    keys, couplings = [], []
    for h in range(groups):
        span = slice(h * WIDTH, (h + 1) * WIDTH)
        key = to_unit(k_ref[:, span].astype(F32)).astype(BF16)
        keys_ref[:, span] = key
        both = dot(key, key, (1, 1))
        couplings.append(jnp.where(row > column, betas[:, h : h + 1] * decay[h] * both, 0.0))
        keys.append(key.astype(F32))
    inverses = lower_inverses(couplings)
    loads[1].wait()
    for h in range(groups):
        span = slice(h * WIDTH, (h + 1) * WIDTH)
        along = summed[:, h : h + 1]
        last = summed[rows - 1 : rows, h : h + 1]
        beta = betas[:, h : h + 1]
        value = v_ref[:, span].astype(F32)
        made = fine(
            inverses[h],
            jnp.concatenate([beta * value, (beta * jnp.exp(along)) * keys[h]], axis=1),
        ).astype(BF16)
        writes_ref[h], erasers_ref[h] = parted(made)
        ended = (jnp.exp(last - along) * keys[h]).astype(BF16)
        effect = dot(ended, made, (0, 0))
        identity = iotas(WIDTH, WIDTH)
        kept = jnp.where(identity[0] == identity[1], jnp.exp(last), 0.0)
        pairs[h, :, 0:WIDTH] = kept - effect[:, WIDTH:]
        pairs[h, :, WIDTH:] = effect[:, :WIDTH]
    own_ref[...] = pairs[part]
    for r, ref in ((1, pay1_ref), (2, pay2_ref), (3, pay3_ref)):
        store_payload(ref, parted(pairs[part ^ r]))


def query_kernel(gb_ref, q_ref, keys_ref, writes_ref, erasers_ref, local_ref, through_ref):
    groups = gb_ref.shape[0] // 2
    summed, decay = decays(gb_ref)
    for h in range(groups):
        span = slice(h * WIDTH, (h + 1) * WIDTH)
        query = to_unit(q_ref[:, span].astype(F32)).astype(BF16)
        mixing = (dot(query, keys_ref[:, span], (1, 1)) * decay[h]).astype(BF16)
        inner = dot(mixing, joined((writes_ref[h], erasers_ref[h])))
        local_ref[h] = inner[:, :WIDTH].astype(BF16)
        decayed = jnp.exp(summed[:, h : h + 1]) * query.astype(F32)
        through_ref[h] = (decayed - inner[:, WIDTH:]).astype(BF16)


def prefixes(blocks):
    two = compose(blocks[1], blocks[0])
    return two, compose(blocks[2], two), compose(compose(blocks[3], blocks[2]), two)


def group_kernel(place, own_ref, recv2_ref, recv3_ref, recv1_ref, before_ref, all_ref, pay_ref, pairs):
    part = place[1]
    pairs[part] = own_ref[...]
    for r, ref in ((1, recv1_ref), (2, recv2_ref), (3, recv3_ref)):
        pairs[part ^ r] = joined(load_payload(ref))
    two, three, total = prefixes([parted(pairs[n]) for n in range(4)])
    store_payload(pay_ref, total)
    all_ref[...] = joined(total)
    before_ref[0] = pairs[0]
    before_ref[1] = joined(two)
    before_ref[2] = joined(three)


def fetch_wide_kernel(token_ref, source_ref, fetched_ref, token_out, sem):
    load = pltpu.make_async_copy(source_ref, fetched_ref, sem)
    load.start()
    token_out[...] = token_ref[...]
    load.wait()


def fetch_kernel(
    place, before_row_ref, before_ref, weight_ref, stream_ref, weight_out, stream_out, maps_ref, sems
):
    width = stream_out.shape[1]
    begin = pl.multiple_of(place[2] * width, width)
    loads = [
        pltpu.make_async_copy(weight_ref, weight_out, sems.at[0]),
        pltpu.make_async_copy(stream_ref.at[:, pl.ds(begin, width)], stream_out, sems.at[1]),
    ]
    for load in loads:
        load.start()
    maps_ref[0] = before_row_ref[...]
    for n in range(3):
        maps_ref[n + 1] = joined(compose(parted(before_ref[n]), parted(before_row_ref[...])))
    for load in loads:
        load.wait()


def row_kernel(place, all_ref, recv2_ref, recv3_ref, recv1_ref, before_ref, pay_ref, pairs, starts):
    group = place[3]
    pairs[group] = all_ref[...]
    for d, ref in ((1, recv1_ref), (2, recv2_ref), (3, recv3_ref)):
        pairs[group ^ d] = joined(load_payload(ref))
    two, three, total = prefixes([parted(pairs[n]) for n in range(4)])
    store_payload(pay_ref, total)
    row, column = iotas(WIDTH, 2 * WIDTH)
    starts[0] = (row == column).astype(F32)
    starts[1] = pairs[0]
    starts[2] = joined(two)
    starts[3] = joined(three)
    before_ref[...] = starts[group]


def state_kernel(
    place, recv2_ref, recv3_ref, recv1_ref, maps_ref, mine_ref, out1_ref, out2_ref, out3_ref, rows, states
):
    part, line = place[1], place[4]
    rows[line] = jnp.zeros(rows.shape[1:], F32)
    for r, ref in ((1, recv1_ref), (2, recv2_ref), (3, recv3_ref)):
        rows[line ^ r] = joined(load_payload(ref))
    state = jnp.where(line > 0, rows[0][:, WIDTH:], 0.0)
    for n in (1, 2):
        state = jnp.where(line > n, apply(parted(rows[n]), state), state)
    for n in range(4):
        states[n] = apply(parted(maps_ref[n]), state).astype(BF16)
    mine_ref[...] = states[part]
    for r, ref in ((1, out1_ref), (2, out2_ref), (3, out3_ref)):
        ref[...] = states[part ^ r]


def out_kernel(
    place, local_ref, through_ref, mine_ref, recv2_ref, recv3_ref, recv1_ref, w_ref, term_ref, *refs
):
    part = place[1]
    me = place[2]
    sent_refs, states = refs[:-1], refs[-1]
    groups = local_ref.shape[0]
    states[part] = mine_ref[...]
    for r, ref in ((1, recv1_ref), (2, recv2_ref), (3, recv3_ref)):
        states[part ^ r] = ref[...]
    normed = []
    for h in range(groups):
        result = local_ref[h].astype(F32) + dot(through_ref[h], states[h])
        normed.append(
            (
                result * lax.rsqrt(jnp.mean(result * result, axis=-1, keepdims=True) + 1e-05)
            ).astype(BF16)
        )
    normed = jnp.concatenate(normed, axis=1)
    width = term_ref.shape[1]
    count = len(sent_refs) + 1
    for r in range(count):
        begin = pl.multiple_of((me ^ r) * width, width)
        term = dot(normed, w_ref[:, pl.ds(begin, width)])
        if r == 0:
            term_ref[...] = term
        else:
            sent_refs[r - 1][...] = term.astype(BF16)


def hidden_kernel(stream_ref, term_ref, *refs):
    total = term_ref[...]
    for ref in refs[:-1]:
        total = total + ref[...].astype(F32)
    refs[-1][...] = (stream_ref[...].astype(F32) + total).astype(BF16)


def own_kernel(place, hidden_ref, w_ref, part_ref):
    width = hidden_ref.shape[1]
    begin = pl.multiple_of(place[2] * width, width)
    part_ref[...] = dot(hidden_ref[...], w_ref[pl.ds(begin, width), :])


def project_kernel(place, w_ref, part_ref, hidden_ref, block2_ref, block1_ref, block3_ref, q_ref, kv_ref):
    me = place[2]
    blocks = [block2_ref, block1_ref, block3_ref]
    rows, width = hidden_ref.shape
    total = part_ref[...]
    for block, r in zip(blocks, (2, 1, 3)):
        begin = pl.multiple_of((me ^ r) * width, width)
        total = total + dot(block[...], w_ref[pl.ds(begin, width), :])
    squares = 0.0
    for ref in [hidden_ref] + blocks:
        value = ref[...].astype(F32)
        squares = squares + jnp.sum(value * value, axis=-1, keepdims=True)
    total = total * lax.rsqrt(squares / (4 * width) + 1e-05)
    groups = width // WIDTH
    for h in range(groups):
        base = h * 3 * WIDTH
        span = slice(h * WIDTH, (h + 1) * WIDTH)
        q_ref[:, span] = to_unit(total[:, base : base + WIDTH]).astype(BF16)
        kv_ref[:, span] = to_unit(total[:, base + WIDTH : base + 2 * WIDTH]).astype(BF16)
        kv_ref[:, (groups + h) * WIDTH : (groups + h + 1) * WIDTH] = total[
            :, base + 2 * WIDTH : base + 3 * WIDTH
        ].astype(BF16)


def window_part(query_place, key_chip, core, q_ref, own_ref, other_ref, sums):
    rows = q_ref.shape[0]
    groups = q_ref.shape[1] // WIDTH
    row, column = iotas(rows, 2 * rows)
    query_place = query_place * rows + row
    own_place = (2 * key_chip + core) * rows + column
    other_place = (2 * key_chip + 1 - core) * rows + column - rows
    key_place = jnp.where(column < rows, own_place, other_place)
    allowed = (key_place <= query_place) & (key_place > query_place - WINDOW) & (key_place >= 0)
    ones = jnp.ones((2 * rows, WIDTH), BF16)
    for h in range(groups):
        span = slice(h * WIDTH, (h + 1) * WIDTH)
        value_span = slice((groups + h) * WIDTH, (groups + h + 1) * WIDTH)
        keys = jnp.concatenate([own_ref[:, span], other_ref[:, span]], axis=0)
        values = jnp.concatenate([own_ref[:, value_span], other_ref[:, value_span]], axis=0)
        scores = SCORE_SCALE * dot(q_ref[:, span], keys, (1, 1))
        weights = jnp.where(allowed, jnp.exp(scores), 0.0).astype(BF16)
        part = dot(weights, jnp.concatenate([values, ones], axis=1))
        sums[h] = part if sums[h] is None else sums[h] + part


def sum_spans(groups):
    return [slice(2 * h * WIDTH, 2 * (h + 1) * WIDTH) for h in range(groups)]


def away_kernel(place, hidden_ref, q_ref, own_ref, other_ref, sums_ref, keep_ref):
    seq = place[0]
    groups = q_ref.shape[1] // WIDTH
    sums = [None] * groups
    window_part(seq + 4, (seq >> 1) - 1, seq & 1, q_ref, own_ref, other_ref, sums)
    for h, span in enumerate(sum_spans(groups)):
        sums_ref[:, span] = sums[h]
    keep_ref[...] = hidden_ref[...]


def back_kernel(place, q_ref, sums_ref, own_ref, other_ref, back_ref):
    seq = place[0]
    rows = q_ref.shape[0]
    groups = q_ref.shape[1] // WIDTH
    sums = [sums_ref[:, span] for span in sum_spans(groups)]
    window_part(seq + 4, (seq >> 1) - 2, seq & 1, q_ref, own_ref, other_ref, sums)
    row, column = iotas(rows, WIDTH)
    line, _ = iotas(16, WIDTH)
    for h in range(groups):
        span = slice(h * WIDTH, (h + 1) * WIDTH)
        back_ref[0:rows, span] = sums[h][:, :WIDTH].astype(BF16)
        total = jnp.sum(jnp.where(row == column, sums[h][:, WIDTH:], 0.0), axis=0, keepdims=True)
        high = total.astype(BF16).astype(F32)
        totals = jnp.where(line == 0, high, jnp.where(line == 1, total - high, 0.0))
        back_ref[rows : rows + 16, span] = totals.astype(BF16)


def home_kernel(place, q_ref, *refs):
    blocks, sums_ref = refs[:-1], refs[-1]
    seq = place[0]
    groups = q_ref.shape[1] // WIDTH
    sums = [None] * groups
    for n in range(len(blocks) // 2):
        window_part(
            seq, (seq >> 1) - n, seq & 1, q_ref, blocks[2 * n], blocks[2 * n + 1], sums
        )
    for h, span in enumerate(sum_spans(groups)):
        sums_ref[:, span] = sums[h]


def last_kernel(sums_ref, back_ref, out_ref):
    groups = out_ref.shape[1] // WIDTH
    rows = out_ref.shape[0]
    row, column = iotas(rows, WIDTH)
    for h in range(groups):
        span = slice(h * WIDTH, (h + 1) * WIDTH)
        line = jnp.sum(back_ref[rows : rows + 16, span].astype(F32), axis=0, keepdims=True)
        far = jnp.sum(jnp.where(row == column, line, 0.0), axis=1, keepdims=True)
        mixed = sums_ref[:, 2 * h * WIDTH : (2 * h + 1) * WIDTH] + back_ref[0:rows, span].astype(F32)
        total = sums_ref[:, (2 * h + 1) * WIDTH : (2 * h + 2) * WIDTH] + far
        out_ref[:, span] = (mixed / total).astype(BF16)


def call(kernel, outs, smem=0, scratch=(), spaces=None, limit=LIMIT):
    def run(*args):
        places = [SMEM] * smem + (spaces or [VMEM] * (len(args) - smem))
        return pl.pallas_call(
            kernel,
            out_shape=[jax.ShapeDtypeStruct(shape, kind) for shape, kind in outs],
            in_specs=[pl.BlockSpec(memory_space=place) for place in places],
            out_specs=[pl.BlockSpec(memory_space=VMEM)] * len(outs),
            scratch_shapes=list(scratch),
            compiler_params=pltpu.CompilerParams(vmem_limit_bytes=limit),
        )(*args)

    return run


def moved(array, axis, distance):
    size = lax.axis_size(axis)
    return lax.ppermute(
        array, axis, [(i, i + distance) for i in range(size) if 0 <= i + distance < size]
    )


def crossed(array, mask, axis="seq"):
    return lax.ppermute(array, axis, [(i, i ^ mask) for i in range(lax.axis_size(axis))])


def body(queries, keys, values, gate_log, beta, stream, w_out, w_qkv):
    rows, wide = queries.shape
    groups = gate_log.shape[1]
    seq = lax.axis_index("seq")
    head = lax.axis_index("head")
    heads = lax.axis_size("head")
    place = jnp.stack([seq, seq & 3, head, (seq >> 2) & 3, seq >> 4]).astype(jnp.int32)
    pair_shape = ((WIDTH, 2 * WIDTH), F32)
    pay_shape = ((WIDTH + 16, 2 * WIDTH), BF16)
    state_shape = ((WIDTH, WIDTH), BF16)
    row_shape = ((rows, wide), BF16)
    four_pairs = pltpu.VMEM((4, WIDTH, 2 * WIDTH), F32)
    four_states = pltpu.VMEM((4, WIDTH, WIDTH), BF16)

    gates = jnp.concatenate([gate_log.T, beta.T], axis=0)
    unit_keys, writes, erasers, own, pay1, pay2, pay3 = call(
        map_kernel,
        [row_shape] + [((groups, rows, WIDTH), BF16)] * 2 + [pair_shape] + [pay_shape] * 3,
        1,
        [pltpu.VMEM((rows, wide), BF16)] * 2 + [four_pairs, pltpu.SemaphoreType.DMA((2,))],
        [VMEM] + [pltpu.HBM] * 2,
        CHUNK_LIMIT,
    )(place, gates, keys, values)
    pay2, pay3, pay1 = crossed(pay2, 2), crossed(pay3, 3), crossed(pay1, 1)
    local, through = call(query_kernel, [((groups, rows, WIDTH), BF16)] * 2)(
        gates, queries, unit_keys, writes, erasers
    )
    own, local, through = lax.optimization_barrier((own, local, through))
    before, everything, pay = call(
        group_kernel, [((3, WIDTH, 2 * WIDTH), F32), pair_shape, pay_shape], 1, [four_pairs]
    )(place, own, pay2, pay3, pay1)
    row2, row3, row1 = [crossed(pay, 4 * d) for d in (2, 3, 1)]
    everything, w_qkv = lax.optimization_barrier((everything, w_qkv))
    w_qkv, everything = call(
        fetch_wide_kernel,
        [(w_qkv.shape, BF16), pair_shape],
        0,
        [pltpu.SemaphoreType.DMA],
        [VMEM, pltpu.HBM],
        FETCH_LIMIT,
    )(everything, w_qkv)
    before_row, pay = call(row_kernel, [pair_shape, pay_shape], 1, [four_pairs] * 2)(
        place, everything, row2, row3, row1
    )
    row2, row3, row1 = [crossed(pay, 16 * d) for d in (2, 3, 1)]
    before_row, w_out, stream = lax.optimization_barrier((before_row, w_out, stream))
    w_out, stream, maps = call(
        fetch_kernel,
        [(w_out.shape, BF16), row_shape, ((4, WIDTH, 2 * WIDTH), F32)],
        1,
        [pltpu.SemaphoreType.DMA((2,))],
        [VMEM, VMEM, pltpu.HBM, pltpu.HBM],
        FETCH_LIMIT,
    )(place, before_row, before, w_out, stream)
    mine, out1, out2, out3 = call(state_kernel, [state_shape] * 4, 1, [four_pairs, four_states])(
        place, row2, row3, row1, maps
    )
    terms = call(
        out_kernel,
        [((rows, wide), F32)] + [row_shape] * (heads - 1),
        1,
        [four_states],
    )(
        place,
        local,
        through,
        mine,
        crossed(out2, 2),
        crossed(out3, 3),
        crossed(out1, 1),
        w_out,
    )
    received = [crossed(terms[r], r, "head") for r in (2, 1, 3)]
    (hidden,) = call(hidden_kernel, [row_shape])(stream, terms[0], *received)
    other2, other1, other3 = [crossed(hidden, r, "head") for r in (2, 1, 3)]
    (part,) = call(own_kernel, [((rows, w_qkv.shape[1]), F32)], 1)(place, hidden, w_qkv)
    unit_queries, pack = call(project_kernel, [row_shape, ((rows, 2 * wide), BF16)], 1)(
        place, w_qkv, part, hidden, other2, other1, other3
    )
    first, visitors = lax.optimization_barrier(
        (moved(pack, "seq", 2), moved(unit_queries, "seq", -2))
    )
    second, visitors = lax.optimization_barrier(
        (moved(first, "seq", 2), moved(visitors, "seq", -2))
    )
    home = [
        pack, crossed(pack, 1), first, crossed(first, 1), second, crossed(second, 1)
    ]
    sums_shape = ((rows, 2 * wide), F32)
    away, kept = call(away_kernel, [sums_shape, row_shape], 1)(
        place, hidden, visitors, home[2], home[3]
    )
    (back,) = call(back_kernel, [((rows + 16, wide), BF16)], 1)(
        place, visitors, away, home[4], home[5]
    )
    returned = moved(back, "seq", 4)
    (sums,) = call(home_kernel, [((rows, 2 * wide), F32)], 1)(place, unit_queries, *home)
    (attended,) = call(last_kernel, [row_shape])(sums, returned)
    return (kept, attended)


def solution(mesh):
    in_specs = (
        P("seq", "head"),
        P("seq", "head"),
        P("seq", "head"),
        P("seq", "head"),
        P("seq", "head"),
        P("seq", None),
        P("head", None),
        P(None, "head"),
    )
    out_specs = (P("seq", "head"), P("seq", "head"))
    return jax.shard_map(body, mesh=mesh, in_specs=in_specs, out_specs=out_specs, check_vma=False)
```
